768 devices in a mesh: gx: 96 (over x, z, core), gy: 8 (over y).
Axes of the slice: x: 4, y: 8, z: 12, core: 2. Of those that a mesh axis runs over, the one named last changes fastest.
Arguments:
- depth: float32 [3072, 4096], P('gx', 'gy'), may hold values from 0.5 to 2
- discharge: float32 [2, 3072, 4096], P(None, 'gx', 'gy'), may hold values from -1.5 to 1.5
- roughness: float32 [3072, 4096], P('gx', 'gy'), may hold values from 0.03 to 0.15
- reach_state: float32 [768, 1024], P('gx'), may hold values from 0.5 to 2.5
- celerity: float32 [768, 8], P('gx'), may hold values from 0.05 to 0.75
- base_inflow: float32 [768, 8], P('gx'), may hold values from 0.5 to 2
- upstream: int32 [768, 2], P('gx'), may hold values from -1 to 759, as said below
- bank_cell: int32 [2304, 1024], P('gx', 'gy'), may hold values from -1 to 16383, as said below
- bank_site: int32 [2304, 1024], P('gx', 'gy'), may hold values from 0 to 1023
- bank_coeff: float32 [2304, 1024], P('gx', 'gy'), may hold values from 0.02 to 0.2
Outputs:
- plain_state: float32 [3, 3072, 4096], P(None, 'gx', 'gy')
- reach_final: float32 [768, 1024], P('gx')
The draws below stay inside these ranges and needn't reach their ends.
Inputs may be any that keep to these rules, and one draw needn't show every extreme that they name: `upstream`: of the basins of each gx index g >= 1, a half lists two basins of gx index g - 1 each and the others list -1 twice; the basins of gx index 0 list -1 twice; every basin other than those of the last gx index is listed exactly once. `bank_cell`: in every block of 128 slots the occupied ones come first; the blocks of basins outside the grid are empty.
All inputs are finite; a program needn't handle non-finite values.
Results may differ from the reference program's by a relative error of at most 0.0001.
Values sent between devices are 32-bit elements; how exact they have to be, the bound alone decides.
No kernel may reach another device: no remote copies, remote signals or barrier semaphores. Data moves between devices by JAX's collectives and lax.ppermute only.
A program may use at most 32 MiB of HBM per device.

```python
import math
import jax
import jax.numpy as jnp
from jax import lax

CX = 32
CY = 512
BAS_DEV = 8
FIELDS = 8
STATIONS = 128
SLOTS = 128
STEPS = 4
NX = 3072
NY = 4096
BASINS = 768
SITES = 1024
BANK_ROWS = 2304
BANK_COLS = 1024


def draw_upstream(key, part):
    owners = BASINS // BAS_DEV
    source_key, receive_key = jax.random.split(key)
    orders = jax.vmap(lambda single: jax.random.permutation(single, BAS_DEV))(jax.random.split(source_key, owners)).astype(jnp.int32)
    ranks = jax.vmap(lambda single: jax.random.permutation(single, BAS_DEV))(jax.random.split(receive_key, owners)).astype(jnp.int32)
    basin = jnp.arange(BASINS, dtype=jnp.int32)
    owner = basin // BAS_DEV
    within = basin % BAS_DEV
    rank = ranks[owner, within]
    choose = jnp.arange(2, dtype=jnp.int32)
    source_slot = orders[jnp.maximum(owner - 1, 0)[:, None], jnp.minimum(2 * rank[:, None] + choose[None, :], BAS_DEV - 1)]
    valid = (owner >= 1)[:, None] & (rank < BAS_DEV // 2)[:, None]
    return jnp.where(valid, (owner[:, None] - 1) * BAS_DEV + source_slot, -1).astype(jnp.int32)


def draw_bank_cell(key, part):
    count_key, cell_key = jax.random.split(key)
    tiles_across = BANK_COLS // SLOTS
    counts = jax.random.randint(count_key, (BANK_ROWS, tiles_across), SLOTS // 4, 2 * SLOTS)
    counts = jnp.minimum(counts, SLOTS)
    block_rows = jnp.arange(BANK_ROWS, dtype=jnp.int32)
    tile_row = block_rows // (3 * BAS_DEV)
    position = block_rows % (3 * BAS_DEV) // BAS_DEV
    last_row = BANK_ROWS // (3 * BAS_DEV) - 1
    outside = (tile_row == 0) & (position == 0) | (tile_row == last_row) & (position == 2)
    counts = jnp.where(outside[:, None], 0, counts)
    columns = jnp.arange(BANK_COLS, dtype=jnp.int32)
    occupied = (columns % SLOTS)[None, :] < counts[:, columns // SLOTS]
    cells = jax.random.randint(cell_key, (BANK_ROWS, BANK_COLS), 0, CX * CY)
    return jnp.where(occupied, cells, -1).astype(jnp.int32)


def touch_ends(array, stream_key, smallest, largest):
    dims = array.shape
    index_at = [jax.random.randint(jax.random.fold_in(stream_key, axis), (), 0, dims[axis]) for axis in range(len(dims))]
    array = array.at[tuple(index_at)].set(smallest)
    longest = dims.index(max(dims))
    index_at[longest] = (index_at[longest] + 1) % dims[longest]
    return array.at[tuple(index_at)].set(largest)


def level_of(rng, dims, shards, smallest, high):
    gain = 1.0
    for dim, blocks in shards:
        steps = jax.random.uniform(jax.random.fold_in(jax.random.fold_in(rng, 6), dim), (blocks,), jnp.float32, smallest / len(shards), high / len(shards))
        gain = gain * jnp.repeat(jnp.exp(steps), dims[dim] // blocks).reshape((-1,) + (1,) * (len(dims) - 1 - dim))
    return gain


def noise(key, shape, scale, bound, cuts=(), kind=jnp.bfloat16):
    result = jax.random.normal(key, shape, jnp.float32) * scale
    if len(cuts) > 0:
        result = level_of(key, shape, cuts, -0.22, 0.18) * result
    return jnp.clip(result, min=-bound, max=bound).astype(kind)


def setup_inputs(seed: int = 0) -> dict:
    keys = jax.random.split(jax.random.key(seed), 11)
    depth = jnp.clip(0.5 + 1.5 * jax.random.uniform(keys[0], (NX, NY), jnp.float32) ** level_of(keys[0], (NX, NY), ((0, 96), (1, 8)), -0.2, 0.2), 0.5, 2.0)
    discharge = noise(keys[1], (2, NX, NY), 0.3, 1.5, ((1, 96), (2, 8)), jnp.float32)
    roughness = jnp.clip(jnp.exp(math.log(0.15) - 1.609438 * jax.random.uniform(keys[2], (NX, NY), jnp.float32) ** level_of(keys[2], (NX, NY), ((0, 96), (1, 8)), -0.2, 0.2)), 0.03, 0.15)
    reach_state = jnp.clip(0.5 + 2.0 * jax.random.uniform(keys[3], (BASINS, SITES), jnp.float32) ** level_of(keys[3], (BASINS, SITES), ((0, 96),), -0.2, 0.2), 0.5, 2.5)
    celerity = jnp.clip(jnp.exp(math.log(0.75) - 2.7080502 * jax.random.uniform(keys[4], (BASINS, FIELDS), jnp.float32) ** level_of(keys[4], (BASINS, FIELDS), ((0, 96),), -0.2, 0.2)), 0.05, 0.75)
    base_inflow = jnp.clip(0.5 + 1.5 * jax.random.uniform(keys[5], (BASINS, FIELDS), jnp.float32) ** level_of(keys[5], (BASINS, FIELDS), ((0, 96),), -0.2, 0.2), 0.5, 2.0)
    upstream = draw_upstream(jax.random.fold_in(keys[10], 71), 0)
    bank_cell = draw_bank_cell(jax.random.fold_in(keys[10], 71), 0)
    bank_site = touch_ends(jax.random.randint(keys[8], (BANK_ROWS, BANK_COLS), 0, SITES), jax.random.fold_in(keys[8], 1), 0, SITES - 1).astype(jnp.int32)
    bank_coeff = jnp.clip(jnp.exp(math.log(0.2) - 2.3025851 * jax.random.uniform(keys[9], (BANK_ROWS, BANK_COLS), jnp.float32) ** level_of(keys[9], (BANK_ROWS, BANK_COLS), ((0, 96), (1, 8)), -0.2, 0.2)), 0.02, 0.2)
    return {"depth": depth, "discharge": discharge, "roughness": roughness, "reach_state": reach_state, "celerity": celerity, "base_inflow": base_inflow, "upstream": upstream, "bank_cell": bank_cell, "bank_site": bank_site, "bank_coeff": bank_coeff}


GRAV = 9.81
DT = 0.5
DX = 10.0
NU = 0.1
RATIO = 0.25

def fluxes(state_cells):
    height = state_cells[0]
    velocity_x = state_cells[1] / height
    velocity_y = state_cells[2] / height
    pressure = 0.5 * GRAV * height * height
    flux_x = jnp.stack([state_cells[1], state_cells[1] * velocity_x + pressure, state_cells[2] * velocity_x])
    flux_y = jnp.stack([state_cells[2], state_cells[1] * velocity_y, state_cells[2] * velocity_y + pressure])
    return (flux_x, flux_y)

def flood_update(padded, roughness, source):
    flux_x, flux_y = fluxes(padded)
    centre = padded[:, 1:-1, 1:-1]
    average = 0.25 * (padded[:, 2:, 1:-1] + padded[:, :-2, 1:-1] + padded[:, 1:-1, 2:] + padded[:, 1:-1, :-2])
    factor = DT / (2.0 * DX)
    updated = average - factor * (flux_x[:, 2:, 1:-1] - flux_x[:, :-2, 1:-1]) - factor * (flux_y[:, 1:-1, 2:] - flux_y[:, 1:-1, :-2])
    height = centre[0]
    velocity_x = centre[1] / height
    velocity_y = centre[2] / height
    flow_speed = jnp.sqrt(velocity_x * velocity_x + velocity_y * velocity_y)
    drag_rate = GRAV * roughness * roughness * flow_speed / jnp.cbrt(height)
    return updated + DT * jnp.stack([source, -drag_rate * velocity_x, -drag_rate * velocity_y])

def river_update(reach, celerity, base_inflow, upstream, lateral):
    current = reach.reshape(BASINS, FIELDS, STATIONS)
    outlets = current[:, :, -1]
    linked = upstream >= 0
    picked = outlets[jnp.maximum(upstream, 0)]
    inflow = base_inflow + lax.optimization_barrier(jnp.sum(jnp.where(linked[:, :, None], picked, 0.0), axis=1))
    behind = jnp.concatenate([inflow[:, :, None], current[:, :, :-1]], axis=2)
    sides = jnp.concatenate([current[:, :1], current, current[:, -1:]], axis=1)
    mixing = sides[:, 2:] - 2.0 * current + sides[:, :-2]
    updated = current - celerity[:, :, None] * (current - behind) + NU * mixing - DT * RATIO * lateral.reshape(BASINS, FIELDS, STATIONS)
    return updated.reshape(BASINS, SITES)

def reference(depth, discharge, roughness, reach_state, celerity, base_inflow, upstream, bank_cell, bank_site, bank_coeff):
    plain = jnp.concatenate([depth[None], discharge], axis=0)
    reach = reach_state
    block_rows = jnp.arange(BANK_ROWS).astype(jnp.int32)
    tile_row = block_rows // (3 * BAS_DEV)
    position = block_rows % (3 * BAS_DEV)
    basin_id = (tile_row - 1 + position // BAS_DEV) * BAS_DEV + position % BAS_DEV
    basin_id = jnp.broadcast_to(jnp.clip(basin_id, 0, BASINS - 1)[:, None], bank_cell.shape)
    occupied = bank_cell >= 0
    cell_local = jnp.maximum(bank_cell, 0)
    tile_col = jnp.arange(BANK_COLS).astype(jnp.int32) // SLOTS
    cell_row = tile_row[:, None] * CX + cell_local // CY
    cell_col = tile_col[None, :] * CY + cell_local % CY
    for step_index in range(STEPS):
        river_segment = reach[basin_id, bank_site]
        cell_depth = plain[0][cell_row, cell_col]
        rates = jnp.where(occupied, bank_coeff * (river_segment - cell_depth), 0.0)
        source = jnp.zeros((NX, NY), jnp.float32).at[cell_row, cell_col].add(rates)
        lateral = jnp.zeros((BASINS, SITES), jnp.float32).at[basin_id, bank_site].add(rates)
        padded = jnp.pad(plain, ((0, 0), (1, 1), (1, 1)), mode='edge')
        plain_next = flood_update(padded, roughness, source)
        reach = river_update(reach, celerity, base_inflow, upstream, lateral)
        plain = plain_next
    return (plain, reach)
```

```python
import functools

import jax
import jax.numpy as jnp
from jax import lax
from jax.experimental import pallas as pl
from jax.experimental.pallas import tpu as pltpu
from jax.sharding import PartitionSpec as P

STEPS = 4


GRAV = 9.81
DT = 0.5
DX = 10.0
NU = 0.1
RATIO = 0.25
FACTOR = DT / (2.0 * DX)

LANES = 128
ROWS = 32
QUADS = 4
COLS = QUADS * LANES
FIELDS = 8
BASINS = 8
SLOT_ROWS = 3 * BASINS
FIRST_ROWS = 24
STEP_ROWS = 16
INTERPRET = False


def iota(shape, dim):
    return lax.broadcasted_iota(jnp.int32, shape, dim)


def lane_gather(rows, index):
    return jnp.take_along_axis(rows, index, axis=1, mode="promise_in_bounds")


def lane_to_column(row, count, offset):
    wide = jnp.broadcast_to(row, (count, LANES))
    hit = iota((count, LANES), 1) == iota((count, LANES), 0) + offset
    return jnp.sum(jnp.where(hit, wide, 0.0), axis=1, keepdims=True)


def column_to_lane(column, offset):
    count = column.shape[0]
    wide = jnp.broadcast_to(column, (count, LANES))
    hit = iota((count, LANES), 1) == iota((count, LANES), 0) + offset
    return jnp.sum(jnp.where(hit, wide, 0.0), axis=0, keepdims=True)


def own_row(block, y):
    return jnp.sum(jnp.where(iota(block.shape, 0) == y, block, 0.0), axis=0, keepdims=True)


def flux_terms(cells):
    h, p, q = cells
    inverse = 1.0 / h
    u = p * inverse
    v = q * inverse
    pressure = 0.5 * GRAV * h * h
    return (p, p * u + pressure, q * u), (q, p * v, q * v + pressure), u, v


def flood_update(cells, top, low, left, right, rough, source):
    flux_x, flux_y, u, v = flux_terms(cells)
    top_x = flux_terms(top)[0]
    low_x = flux_terms(low)[0]
    left_y = flux_terms(left)[1]
    right_y = flux_terms(right)[1]
    row = iota((ROWS, COLS), 0)
    col = iota((ROWS, COLS), 1)
    out = []
    for k in range(3):
        quarter = 0.25 * cells[k]
        from_top = jnp.where(
            row == 0, 0.25 * top[k] + FACTOR * top_x[k], pltpu.roll(quarter + FACTOR * flux_x[k], 1, 0)
        )
        from_low = jnp.where(
            row == ROWS - 1,
            0.25 * low[k] - FACTOR * low_x[k],
            pltpu.roll(quarter - FACTOR * flux_x[k], ROWS - 1, 0),
        )
        from_left = jnp.where(
            col == 0, 0.25 * left[k] + FACTOR * left_y[k], pltpu.roll(quarter + FACTOR * flux_y[k], 1, 1)
        )
        from_right = jnp.where(
            col == COLS - 1,
            0.25 * right[k] - FACTOR * right_y[k],
            pltpu.roll(quarter - FACTOR * flux_y[k], COLS - 1, 1),
        )
        out.append((from_top + from_low) + (from_left + from_right))
    h = cells[0]
    size = jnp.abs(h)
    root = jnp.exp(jnp.log(size) * (-1.0 / 3.0))
    root = root * (4.0 - size * (root * root * root)) * (1.0 / 3.0)
    root = jnp.where(h < 0.0, -root, root)
    drag = (GRAV * DT) * rough * rough * jnp.sqrt(u * u + v * v) * root
    return [out[0] + DT * source, out[1] - drag * u, out[2] - drag * v]


def halves(values):
    high = values.astype(jnp.bfloat16).astype(jnp.float32)
    return high, values - high


def spread(rates, major, minor, count):
    total = None
    rows = rates.shape[0]
    group = 4
    high, low = halves(rates)
    for start in range(0, rows, group):
        left, right = [], []
        for r in range(start, start + group):
            at = iota((count, LANES), 0) == major[r : r + 1]
            left.append(
                jnp.concatenate(
                    [
                        jnp.where(at, high[r : r + 1], 0.0),
                        jnp.where(at, low[r : r + 1], 0.0),
                    ],
                    axis=0,
                ).astype(jnp.bfloat16)
            )
            right.append(
                jnp.where(iota((LANES, LANES), 0) == minor[r : r + 1], 1.0, 0.0).astype(jnp.bfloat16)
            )
        part = lax.dot_general(
            jnp.concatenate(left, axis=1),
            jnp.concatenate(right, axis=1),
            (((1,), (1,)), ((), ())),
            preferred_element_type=jnp.float32,
        )
        total = part if total is None else total + part
    return total[:count] + total[count:]


def cell_parts(cell):
    col = cell & (COLS - 1)
    return (col >> 7) * ROWS + (cell >> 9), col & (LANES - 1)


def depth_at_slots(h_ref, index, cell):
    major, minor = cell_parts(cell)
    index_rows = [minor[8 * v : 8 * v + 8] for v in range(3)]
    key_rows = [major[8 * v : 8 * v + 8] for v in range(3)]
    found = [jnp.zeros((8, LANES), jnp.float32) for _ in range(3)]
    for quad in range(QUADS):
        for row in range(ROWS):
            values = h_ref[index + (slice(row, row + 1), slice(quad * LANES, (quad + 1) * LANES))]
            values = jnp.broadcast_to(values, (8, LANES))
            for v in range(3):
                found[v] = jnp.where(
                    key_rows[v] == quad * ROWS + row, lane_gather(values, index_rows[v]), found[v]
                )
    return jnp.concatenate(found, axis=0)


def level_at_sites(reach_rows, site):
    found = []
    for v in range(3):
        sites = site[8 * v : 8 * v + 8]
        field = sites >> 7
        station = sites & (LANES - 1)
        level = jnp.zeros((8, LANES), jnp.float32)
        for f in range(FIELDS):
            level = jnp.where(field == f, lane_gather(reach_rows(f, v), station), level)
        found.append(level)
    return jnp.concatenate(found, axis=0)


def put_edges(send_ref, across_ref, cells, even, mine, other, y, col_row, edge_row):
    lane_left = column_to_lane(cells[0][:, 0:1], 0)
    lane_right = column_to_lane(cells[0][:, COLS - 1 : COLS], 0)
    for k in (1, 2):
        lane_left = lane_left + column_to_lane(cells[k][:, 0:1], k * ROWS)
        lane_right = lane_right + column_to_lane(cells[k][:, COLS - 1 : COLS], k * ROWS)
    send_ref[mine, jnp.maximum(y - 1, 0), col_row : col_row + 1, :] = lane_left
    send_ref[mine, jnp.minimum(y + 1, BASINS - 1), col_row : col_row + 1, :] = lane_right
    for k in range(3):
        first = cells[k][0:1]
        last = cells[k][ROWS - 1 : ROWS]
        inner = jnp.where(even, last, first)
        outer = jnp.where(even, first, last)
        for quad in range(QUADS):
            at = k * QUADS + quad
            lanes = slice(quad * LANES, (quad + 1) * LANES)
            send_ref[other, y, edge_row + at : edge_row + at + 1, :] = inner[:, lanes]
            across_ref[at : at + 1, :] = outer[:, lanes]


def get_edges(got_ref, over_ref, cells, scal, mine, other, y, col_row, edge_row, over_edge):
    even = scal[0] == 0
    is_first, is_last = scal[2] == 1, scal[3] == 1
    before = got_ref[mine, jnp.maximum(y - 1, 0), col_row : col_row + 1, :]
    after = got_ref[mine, jnp.minimum(y + 1, BASINS - 1), col_row : col_row + 1, :]
    top, low, left, right = [], [], [], []
    for k in range(3):
        inner = jnp.concatenate(
            [
                got_ref[other, y, edge_row + k * QUADS + quad : edge_row + k * QUADS + quad + 1, :]
                for quad in range(QUADS)
            ],
            axis=1,
        )
        outer = jnp.concatenate(
            [
                over_ref[over_edge + k * QUADS + quad : over_edge + k * QUADS + quad + 1, :]
                for quad in range(QUADS)
            ],
            axis=1,
        )
        top.append(jnp.where(is_first, cells[k][0:1], jnp.where(even, outer, inner)))
        low.append(jnp.where(is_last, cells[k][ROWS - 1 : ROWS], jnp.where(even, inner, outer)))
        left.append(jnp.where(y == 0, cells[k][:, 0:1], lane_to_column(before, ROWS, k * ROWS)))
        right.append(
            jnp.where(
                y == BASINS - 1, cells[k][:, COLS - 1 : COLS], lane_to_column(after, ROWS, k * ROWS)
            )
        )
    return top, low, left, right


def river_update(current, outlets, own, lateral):
    rate = own[0:8]
    base = own[8:16, 0:1]
    weight = own[16:24]
    inflow_row = jnp.sum(weight * outlets, axis=0, keepdims=True)
    inflow = base + lane_to_column(inflow_row, FIELDS, 0)
    lane = iota((FIELDS, LANES), 1)
    sub = iota((FIELDS, LANES), 0)
    behind = jnp.where(lane == 0, inflow, pltpu.roll(current, 1, 1))
    above = jnp.where(sub == FIELDS - 1, current, pltpu.roll(current, FIELDS - 1, 0))
    below = jnp.where(sub == 0, current, pltpu.roll(current, 1, 0))
    mixing = above - 2.0 * current + below
    return current - rate * (current - behind) + NU * mixing - (DT * RATIO) * lateral


def first_kernel(
    scal, depth, discharge, cell_in, site_in, coeff_in, reach, send_ref, across_ref, cell_ref, site_ref, coeff_ref, slots_ref
):
    even = scal[0] == 0
    mine, other, y = scal[0], 1 - scal[0], scal[1]
    send_ref[...] = jnp.zeros_like(send_ref)
    across_ref[...] = jnp.zeros_like(across_ref)

    def arranged(ref):
        low, own, high = ref[0:8], ref[8:16], ref[16:24]
        return jnp.concatenate([own, jnp.where(even, high, low), jnp.where(even, low, high)], axis=0)

    cell = arranged(cell_in)
    site = arranged(site_in)
    coeff = jnp.where(cell >= 0, arranged(coeff_in), 0.0)
    cell = jnp.maximum(cell, 0)
    cell_ref[...] = cell
    site_ref[...] = site
    coeff_ref[...] = coeff
    slots = depth_at_slots(depth, (), cell)
    slots_ref[...] = slots
    site_value = site.astype(jnp.float32)
    level_rows = [own_row(reach[:, f * LANES : (f + 1) * LANES], y) for f in range(FIELDS)]
    for b in range(BASINS):
        for at, value in enumerate((slots, site_value, coeff)):
            send_ref[mine, b, at : at + 1, :] = value[b : b + 1]
            send_ref[other, b, at : at + 1, :] = value[8 + b : 9 + b]
            send_ref[mine, b, 3 + at : 4 + at, :] = value[16 + b : 17 + b]
        for f in range(FIELDS):
            send_ref[other, b, 15 + f : 16 + f, :] = level_rows[f]
    cells = [depth[...], discharge[0], discharge[1]]
    put_edges(send_ref, across_ref, cells, even, mine, other, y, 6, 3)


def step_kernel(first, last, *refs):
    refs = list(refs)

    def take(n):
        taken = refs[:n]
        del refs[:n]
        return taken

    (scal,) = take(1)
    if first:
        depth, discharge, reach = take(3)
    else:
        state, levels, owner_levels, owner_site, owner_coeff = take(5)
    got, over, rough, own, cell_ref, coeff_ref, slots_ref = take(7)
    if first:
        (site_ref,) = take(1)
    (state_out,) = take(1)
    if last:
        (all_levels,) = take(1)
    else:
        levels_out, owner_levels_out, slots_out, send_ref, across_ref = take(5)
        if first:
            owner_site_out, owner_coeff_out = take(2)
    even = scal[0] == 0
    mine, other, y = scal[0], 1 - scal[0], scal[1]
    cell = cell_ref[...]

    def gathered(row, across_row):
        return jnp.concatenate(
            [got[mine, :, row, :], got[other, :, row, :], over[pl.ds(across_row, 8, stride=8), :]],
            axis=0,
        )

    if first:
        cells = [depth[...], discharge[0], discharge[1]]
        current = jnp.concatenate(
            [own_row(reach[:, f * LANES : (f + 1) * LANES], y) for f in range(FIELDS)], axis=0
        )
        over_edge = 64

        def tile_rows(f, v):
            if v == 0:
                return reach[:, f * LANES : (f + 1) * LANES]
            if v == 1:
                return got[other, :, 15 + f, :]
            return over[80 + 8 * f : 88 + 8 * f, :]

        segment = level_at_sites(tile_rows, site_ref[...])
        site_owner = gathered(1, 4).astype(jnp.int32)
        coeff_owner = gathered(2, 5)
        slots_owner = gathered(0, 3)
        outlets = jnp.zeros((BASINS, LANES), jnp.float32)
        for f in range(FIELDS):
            source_rows = jnp.where(even, tile_rows(f, 2), tile_rows(f, 1))
            outlets = jnp.where(
                iota((BASINS, LANES), 1) == f, source_rows[:, LANES - 1 : LANES], outlets
            )
        segment_owner = level_at_sites(
            lambda f, v: jnp.broadcast_to(current[f : f + 1], (8, LANES)), site_owner
        )
        edge_rows = (6, 3)
    else:
        cells = [state[0], state[1], state[2]]
        current = levels[...]
        over_edge = 64
        segment = gathered(1, 4)
        slots_owner = gathered(0, 3)
        site_owner = owner_site[...]
        coeff_owner = owner_coeff[...]
        segment_owner = owner_levels[...]
        outlets = jnp.where(even, over[pl.ds(2, 8, stride=8), :], got[other, :, 2, :])
        edge_rows = (5, 3)

    rates_owner = coeff_owner * (segment_owner - slots_owner)
    lateral = spread(rates_owner, site_owner >> 7, site_owner & (LANES - 1), FIELDS)
    levels_next = river_update(current, outlets, own[...], lateral)

    major, minor = cell_parts(cell)
    rates = coeff_ref[...] * (segment - slots_ref[...])
    blocks = spread(rates, major, minor, QUADS * ROWS)
    source = jnp.concatenate([blocks[q * ROWS : (q + 1) * ROWS] for q in range(QUADS)], axis=1)
    top, low, left, right = get_edges(
        got, over, cells, scal, mine, other, y, edge_rows[0], edge_rows[1], over_edge
    )
    new = flood_update(cells, top, low, left, right, rough[...], source)
    for k in range(3):
        state_out[k] = new[k]

    if last:
        for b in range(BASINS):
            all_levels[b] = levels_next
        return

    if first:
        owner_site_out[...] = site_owner
        owner_coeff_out[...] = coeff_owner
    send_ref[...] = jnp.zeros_like(send_ref)
    across_ref[...] = jnp.zeros_like(across_ref)
    levels_out[...] = levels_next
    owned = level_at_sites(
        lambda f, v: jnp.broadcast_to(levels_next[f : f + 1], (8, LANES)), site_owner
    )
    owner_levels_out[...] = owned
    slots = depth_at_slots(state_out, (0,), cell)
    slots_out[...] = slots
    outlet_row = column_to_lane(levels_next[:, LANES - 1 : LANES], 0)
    for b in range(BASINS):
        for at, value in enumerate((slots, owned)):
            send_ref[mine, b, at : at + 1, :] = value[b : b + 1]
            send_ref[other, b, at : at + 1, :] = value[8 + b : 9 + b]
            send_ref[mine, b, 3 + at : 4 + at, :] = value[16 + b : 17 + b]
        send_ref[mine, b, 2:3, :] = outlet_row
        send_ref[other, b, 2:3, :] = outlet_row
    put_edges(send_ref, across_ref, new, even, mine, other, y, 5, 3)


def call(kernel, outs, args):
    specs = [pl.BlockSpec(memory_space=pltpu.SMEM)]
    specs += [pl.BlockSpec(memory_space=pltpu.VMEM) for _ in args[1:]]
    return pl.pallas_call(
        kernel,
        out_shape=outs,
        in_specs=specs,
        out_specs=[pl.BlockSpec(memory_space=pltpu.VMEM) for _ in outs],
        compiler_params=None if INTERPRET else pltpu.CompilerParams(vmem_limit_bytes=16 << 20),
        interpret=INTERPRET,
    )(*args)


def f32(*shape):
    return jax.ShapeDtypeStruct(shape, jnp.float32)


def i32(*shape):
    return jax.ShapeDtypeStruct(shape, jnp.int32)


def per_device(
    depth,
    discharge,
    roughness,
    reach_state,
    celerity,
    base_inflow,
    upstream,
    bank_cell,
    bank_site,
    bank_coeff,
):
    count_x = lax.axis_size("gx")
    count_y = lax.axis_size("gy")
    gx = lax.axis_index("gx")
    gy = lax.axis_index("gy")
    core = gx % 2
    pairs = [list(range(c * 2 * count_y, (c + 1) * 2 * count_y)) for c in range(count_x // 2)]
    border = [(i, i + 1) for i in range(1, count_x - 1, 2)]
    border = border + [(b, a) for a, b in border]
    scal = jnp.stack(
        [core, gy, (gx == 0).astype(jnp.int32), (gx == count_x - 1).astype(jnp.int32)]
    ).astype(jnp.int32)

    def mine_of(array):
        return lax.dynamic_slice_in_dim(array, gy, 1, axis=0)

    ids = (gx - 1) * BASINS + jnp.arange(BASINS, dtype=jnp.int32)
    weight = jnp.sum((mine_of(upstream) == ids[:, None]).astype(jnp.float32), axis=1, keepdims=True)
    own = jnp.concatenate(
        [
            jnp.broadcast_to(mine_of(celerity).reshape(FIELDS, 1), (FIELDS, LANES)),
            jnp.broadcast_to(mine_of(base_inflow).reshape(FIELDS, 1), (FIELDS, LANES)),
            jnp.broadcast_to(weight, (BASINS, LANES)),
        ],
        axis=0,
    )

    def exchange(send, across, extra):
        rows = send.shape[2]
        got = lax.all_to_all(
            send.reshape(2 * BASINS, rows, LANES), ("gx", "gy"), 0, 0, axis_index_groups=pairs
        )
        part = lax.dynamic_slice(got, (core * BASINS, 0, 0), (BASINS, 8, LANES))
        packed = jnp.concatenate([part.reshape(BASINS * 8, LANES), across] + extra, axis=0)
        over = lax.ppermute(packed, "gx", border)
        return got.reshape(2, BASINS, rows, LANES), over

    send, across, cell, site, coeff, slots = call(
        first_kernel,
        [
            f32(2, BASINS, FIRST_ROWS, LANES),
            f32(16, LANES),
            i32(SLOT_ROWS, LANES),
            i32(SLOT_ROWS, LANES),
            f32(SLOT_ROWS, LANES),
            f32(SLOT_ROWS, LANES),
        ],
        [scal, depth, discharge, bank_cell, bank_site, bank_coeff, reach_state],
    )
    fields_major = [reach_state[:, f * LANES : (f + 1) * LANES] for f in range(FIELDS)]
    got, over = exchange(send, across, fields_major)
    for step in range(STEPS):
        first, last = step == 0, step == STEPS - 1
        outs = [f32(3, ROWS, COLS)]
        if last:
            outs += [f32(BASINS, FIELDS, LANES)]
        else:
            outs += [
                f32(FIELDS, LANES),
                f32(SLOT_ROWS, LANES),
                f32(SLOT_ROWS, LANES),
                f32(2, BASINS, STEP_ROWS, LANES),
                f32(16, LANES),
            ]
        if first:
            outs += [i32(SLOT_ROWS, LANES), f32(SLOT_ROWS, LANES)]
            args = [scal, depth, discharge, reach_state]
        else:
            args = [scal, state, levels, owner_levels, owner_site, owner_coeff]
        args += [got, over, roughness, own, cell, coeff, slots]
        if first:
            args += [site]
        result = call(functools.partial(step_kernel, first, last), outs, args)
        state = result[0]
        if last:
            break
        levels, owner_levels, slots, send, across = result[1:6]
        if first:
            owner_site, owner_coeff = result[6:8]
        got, over = exchange(send, across, [])
    final = lax.all_to_all(result[1], "gy", 0, 0)
    return state, final.reshape(BASINS, FIELDS * LANES)


def solution(mesh):
    return jax.shard_map(
        per_device,
        mesh=mesh,
        in_specs=(
            P("gx", "gy"),
            P(None, "gx", "gy"),
            P("gx", "gy"),
            P("gx", None),
            P("gx", None),
            P("gx", None),
            P("gx", None),
            P("gx", "gy"),
            P("gx", "gy"),
            P("gx", "gy"),
        ),
        out_specs=(P(None, "gx", "gy"), P("gx", None)),
        check_vma=False,
    )
```

```python
import functools

import jax
import jax.numpy as jnp
from jax import lax
from jax.experimental import pallas as pl
from jax.experimental.pallas import tpu as pltpu
from jax.sharding import PartitionSpec as P

STEPS = 4


GRAV = 9.81
DT = 0.5
DX = 10.0
NU = 0.1
RATIO = 0.25
FACTOR = DT / (2.0 * DX)

LANES = 128
ROWS = 32
QUADS = 4
COLS = QUADS * LANES
FIELDS = 8
BASINS = 8
SLOT_ROWS = 3 * BASINS
BLOCK = 8
EDGE = 16
WHOLE = EDGE + FIELDS * BASINS
INTERPRET = False


def iota(shape, dim):
    return lax.broadcasted_iota(jnp.int32, shape, dim)


def lane_gather(rows, index):
    return jnp.take_along_axis(rows, index, axis=1, mode="promise_in_bounds")


def lane_to_column(row, count, offset):
    wide = jnp.broadcast_to(row, (count, LANES))
    hit = iota((count, LANES), 1) == iota((count, LANES), 0) + offset
    return jnp.sum(jnp.where(hit, wide, 0.0), axis=1, keepdims=True)


def column_to_lane(column, offset):
    count = column.shape[0]
    wide = jnp.broadcast_to(column, (count, LANES))
    hit = iota((count, LANES), 1) == iota((count, LANES), 0) + offset
    return jnp.sum(jnp.where(hit, wide, 0.0), axis=0, keepdims=True)


def own_row(block, y):
    return jnp.sum(jnp.where(iota(block.shape, 0) == y, block, 0.0), axis=0, keepdims=True)


def flux_terms(cells):
    h, p, q = cells
    inverse = 1.0 / h
    u = p * inverse
    v = q * inverse
    pressure = 0.5 * GRAV * h * h
    return (p, p * u + pressure, q * u), (q, p * v, q * v + pressure), u, v


def flood_update(cells, top, low, left, right, rough, source):
    flux_x, flux_y, u, v = flux_terms(cells)
    top_x = flux_terms(top)[0]
    low_x = flux_terms(low)[0]
    left_y = flux_terms(left)[1]
    right_y = flux_terms(right)[1]
    row = iota((ROWS, COLS), 0)
    col = iota((ROWS, COLS), 1)
    out = []
    for k in range(3):
        quarter = 0.25 * cells[k]
        from_top = jnp.where(
            row == 0, 0.25 * top[k] + FACTOR * top_x[k], pltpu.roll(quarter + FACTOR * flux_x[k], 1, 0)
        )
        from_low = jnp.where(
            row == ROWS - 1,
            0.25 * low[k] - FACTOR * low_x[k],
            pltpu.roll(quarter - FACTOR * flux_x[k], ROWS - 1, 0),
        )
        from_left = jnp.where(
            col == 0, 0.25 * left[k] + FACTOR * left_y[k], pltpu.roll(quarter + FACTOR * flux_y[k], 1, 1)
        )
        from_right = jnp.where(
            col == COLS - 1,
            0.25 * right[k] - FACTOR * right_y[k],
            pltpu.roll(quarter - FACTOR * flux_y[k], COLS - 1, 1),
        )
        out.append((from_top + from_low) + (from_left + from_right))
    h = cells[0]
    size = jnp.abs(h)
    root = jnp.exp(jnp.log(size) * (-1.0 / 3.0))
    root = root * (4.0 - size * (root * root * root)) * (1.0 / 3.0)
    root = jnp.where(h < 0.0, -root, root)
    drag = (GRAV * DT) * rough * rough * jnp.sqrt(u * u + v * v) * root
    return [out[0] + DT * source, out[1] - drag * u, out[2] - drag * v]


def halves(values):
    high = values.astype(jnp.bfloat16).astype(jnp.float32)
    return high, values - high


def spread(rates, major, minor, count):
    total = None
    rows = rates.shape[0]
    group = 4
    high, low = halves(rates)
    for start in range(0, rows, group):
        left, right = [], []
        for r in range(start, start + group):
            at = iota((count, LANES), 0) == major[r : r + 1]
            left.append(
                jnp.concatenate(
                    [
                        jnp.where(at, high[r : r + 1], 0.0),
                        jnp.where(at, low[r : r + 1], 0.0),
                    ],
                    axis=0,
                ).astype(jnp.bfloat16)
            )
            right.append(
                jnp.where(iota((LANES, LANES), 0) == minor[r : r + 1], 1.0, 0.0).astype(jnp.bfloat16)
            )
        part = lax.dot_general(
            jnp.concatenate(left, axis=1),
            jnp.concatenate(right, axis=1),
            (((1,), (1,)), ((), ())),
            preferred_element_type=jnp.float32,
        )
        total = part if total is None else total + part
    return total[:count] + total[count:]


def cell_parts(cell):
    col = cell & (COLS - 1)
    return (col >> 7) * ROWS + (cell >> 9), col & (LANES - 1)


def depth_at_slots(h_ref, index, cell):
    major, minor = cell_parts(cell)
    index_rows = [minor[8 * v : 8 * v + 8] for v in range(3)]
    key_rows = [major[8 * v : 8 * v + 8] for v in range(3)]
    found = [jnp.zeros((8, LANES), jnp.float32) for _ in range(3)]
    for quad in range(QUADS):
        for row in range(ROWS):
            values = h_ref[index + (slice(row, row + 1), slice(quad * LANES, (quad + 1) * LANES))]
            values = jnp.broadcast_to(values, (8, LANES))
            for v in range(3):
                found[v] = jnp.where(
                    key_rows[v] == quad * ROWS + row, lane_gather(values, index_rows[v]), found[v]
                )
    return jnp.concatenate(found, axis=0)


def level_at_sites(reach_rows, site):
    found = []
    for v in range(3):
        sites = site[8 * v : 8 * v + 8]
        field = sites >> 7
        station = sites & (LANES - 1)
        level = jnp.zeros((8, LANES), jnp.float32)
        for f in range(FIELDS):
            level = jnp.where(field == f, lane_gather(reach_rows(f, v), station), level)
        found.append(level)
    return jnp.concatenate(found, axis=0)


def put_edges(send_ref, beside_ref, across_ref, cells, even, mine, y, col_row):
    lane_left = column_to_lane(cells[0][:, 0:1], 0)
    lane_right = column_to_lane(cells[0][:, COLS - 1 : COLS], 0)
    for k in (1, 2):
        lane_left = lane_left + column_to_lane(cells[k][:, 0:1], k * ROWS)
        lane_right = lane_right + column_to_lane(cells[k][:, COLS - 1 : COLS], k * ROWS)
    send_ref[mine, jnp.maximum(y - 1, 0), col_row : col_row + 1, :] = lane_left
    send_ref[mine, jnp.minimum(y + 1, BASINS - 1), col_row : col_row + 1, :] = lane_right
    for k in range(3):
        first = cells[k][0:1]
        last = cells[k][ROWS - 1 : ROWS]
        inner = jnp.where(even, last, first)
        outer = jnp.where(even, first, last)
        for quad in range(QUADS):
            at = k * QUADS + quad
            lanes = slice(quad * LANES, (quad + 1) * LANES)
            beside_ref[at : at + 1, :] = inner[:, lanes]
            across_ref[at : at + 1, :] = outer[:, lanes]


def get_edges(got_ref, near_ref, over_ref, cells, scal, mine, y, col_row):
    even = scal[0] == 0
    is_first, is_last = scal[2] == 1, scal[3] == 1
    before = got_ref[mine, jnp.maximum(y - 1, 0), col_row : col_row + 1, :]
    after = got_ref[mine, jnp.minimum(y + 1, BASINS - 1), col_row : col_row + 1, :]
    over_edge = BASINS * BLOCK
    top, low, left, right = [], [], [], []
    for k in range(3):
        inner = jnp.concatenate(
            [
                near_ref[k * QUADS + quad : k * QUADS + quad + 1, :]
                for quad in range(QUADS)
            ],
            axis=1,
        )
        outer = jnp.concatenate(
            [
                over_ref[over_edge + k * QUADS + quad : over_edge + k * QUADS + quad + 1, :]
                for quad in range(QUADS)
            ],
            axis=1,
        )
        top.append(jnp.where(is_first, cells[k][0:1], jnp.where(even, outer, inner)))
        low.append(jnp.where(is_last, cells[k][ROWS - 1 : ROWS], jnp.where(even, inner, outer)))
        left.append(jnp.where(y == 0, cells[k][:, 0:1], lane_to_column(before, ROWS, k * ROWS)))
        right.append(
            jnp.where(
                y == BASINS - 1, cells[k][:, COLS - 1 : COLS], lane_to_column(after, ROWS, k * ROWS)
            )
        )
    return top, low, left, right


def river_update(current, outlets, own, lateral):
    rate = own[0:8]
    base = own[8:16, 0:1]
    weight = own[16:24]
    inflow_row = jnp.sum(weight * outlets, axis=0, keepdims=True)
    inflow = base + lane_to_column(inflow_row, FIELDS, 0)
    lane = iota((FIELDS, LANES), 1)
    sub = iota((FIELDS, LANES), 0)
    behind = jnp.where(lane == 0, inflow, pltpu.roll(current, 1, 1))
    above = jnp.where(sub == FIELDS - 1, current, pltpu.roll(current, FIELDS - 1, 0))
    below = jnp.where(sub == 0, current, pltpu.roll(current, 1, 0))
    mixing = above - 2.0 * current + below
    return current - rate * (current - behind) + NU * mixing - (DT * RATIO) * lateral


def first_kernel(
    scal,
    depth,
    discharge,
    cell_in,
    site_in,
    coeff_in,
    reach,
    send_ref,
    beside_ref,
    across_ref,
    cell_ref,
    site_ref,
    coeff_ref,
    slots_ref,
):
    even = scal[0] == 0
    mine, other, y = scal[0], 1 - scal[0], scal[1]
    send_ref[...] = jnp.zeros_like(send_ref)

    def arranged(ref):
        low, own, high = ref[0:8], ref[8:16], ref[16:24]
        return jnp.concatenate([own, jnp.where(even, high, low), jnp.where(even, low, high)], axis=0)

    cell = arranged(cell_in)
    site = arranged(site_in)
    coeff = jnp.where(cell >= 0, arranged(coeff_in), 0.0)
    cell = jnp.maximum(cell, 0)
    cell_ref[...] = cell
    site_ref[...] = site
    coeff_ref[...] = coeff
    slots = depth_at_slots(depth, (), cell)
    slots_ref[...] = slots
    site_value = site.astype(jnp.float32)
    for b in range(BASINS):
        for at, value in enumerate((slots, site_value, coeff)):
            send_ref[mine, b, at : at + 1, :] = value[b : b + 1]
            send_ref[other, b, at : at + 1, :] = value[8 + b : 9 + b]
            send_ref[mine, b, 3 + at : 4 + at, :] = value[16 + b : 17 + b]
    for ref in (beside_ref, across_ref):
        ref[0:EDGE] = jnp.zeros((EDGE, LANES), jnp.float32)
        for f in range(FIELDS):
            ref[EDGE + 8 * f : EDGE + 8 * f + 8] = reach[:, f * LANES : (f + 1) * LANES]
    cells = [depth[...], discharge[0], discharge[1]]
    put_edges(send_ref, beside_ref, across_ref, cells, even, mine, y, 6)


OVER = BASINS * BLOCK


def gathered(got, over, scal, row, across_row):
    mine, other = scal[0], 1 - scal[0]
    return jnp.concatenate(
        [got[mine, :, row, :], got[other, :, row, :], over[pl.ds(across_row, 8, stride=BLOCK), :]],
        axis=0,
    )


def advance_levels(scal, current, outlets, own, site_owner, coeff_owner, segment_owner, slots_owner):
    rates = coeff_owner * (segment_owner - slots_owner)
    lateral = spread(rates, site_owner >> 7, site_owner & (LANES - 1), FIELDS)
    return river_update(current, outlets, own, lateral)


def advance_cells(scal, cells, got, near, over, rough, cell, coeff, segment, slots, col_row):
    mine, y = scal[0], scal[1]
    major, minor = cell_parts(cell)
    rates = coeff * (segment - slots)
    blocks = spread(rates, major, minor, QUADS * ROWS)
    source = jnp.concatenate([blocks[q * ROWS : (q + 1) * ROWS] for q in range(QUADS)], axis=1)
    top, low, left, right = get_edges(got, near, over, cells, scal, mine, y, col_row)
    return flood_update(cells, top, low, left, right, rough, source)


def levels_kernel(scal, levels, owner_levels, owner_site, owner_coeff, got, over, own, all_levels):
    even = scal[0] == 0
    outlets = jnp.where(even, over[pl.ds(2, 8, stride=BLOCK), :], got[1 - scal[0], :, 2, :])
    new = advance_levels(
        scal,
        levels[...],
        outlets,
        own[...],
        owner_site[...],
        owner_coeff[...],
        owner_levels[...],
        gathered(got, over, scal, 0, 3),
    )
    for b in range(BASINS):
        all_levels[b] = new


def cells_kernel(scal, state, got, near, over, rough, cell_ref, coeff_ref, slots_ref, state_out):
    new = advance_cells(
        scal,
        [state[0], state[1], state[2]],
        got,
        near,
        over,
        rough[...],
        cell_ref[...],
        coeff_ref[...],
        gathered(got, over, scal, 1, 4),
        slots_ref[...],
        5,
    )
    for k in range(3):
        state_out[k] = new[k]


def step_kernel(first, *refs):
    refs = list(refs)

    def take(n):
        taken = refs[:n]
        del refs[:n]
        return taken

    (scal,) = take(1)
    if first:
        depth, discharge, reach, site_ref = take(4)
    else:
        state, levels, owner_levels, owner_site, owner_coeff = take(5)
    got, near, over, rough, own, cell_ref, coeff_ref, slots_ref = take(8)
    state_out, levels_out, owner_levels_out, slots_out, send_ref, beside_ref, across_ref = take(7)
    if first:
        owner_site_out, owner_coeff_out = take(2)
    even = scal[0] == 0
    mine, other, y = scal[0], 1 - scal[0], scal[1]
    cell = cell_ref[...]

    slots_owner = gathered(got, over, scal, 0, 3)
    if first:
        cells = [depth[...], discharge[0], discharge[1]]
        current = jnp.concatenate(
            [own_row(reach[:, f * LANES : (f + 1) * LANES], y) for f in range(FIELDS)], axis=0
        )

        def tile_rows(f, v):
            if v == 0:
                return reach[:, f * LANES : (f + 1) * LANES]
            if v == 1:
                return near[EDGE + 8 * f : EDGE + 8 * f + 8, :]
            return over[OVER + EDGE + 8 * f : OVER + EDGE + 8 * f + 8, :]

        segment = level_at_sites(tile_rows, site_ref[...])
        site_owner = gathered(got, over, scal, 1, 4).astype(jnp.int32)
        coeff_owner = gathered(got, over, scal, 2, 5)
        outlets = jnp.zeros((BASINS, LANES), jnp.float32)
        for f in range(FIELDS):
            source_rows = jnp.where(even, tile_rows(f, 2), tile_rows(f, 1))
            outlets = jnp.where(
                iota((BASINS, LANES), 1) == f, source_rows[:, LANES - 1 : LANES], outlets
            )
        segment_owner = level_at_sites(
            lambda f, v: jnp.broadcast_to(current[f : f + 1], (8, LANES)), site_owner
        )
        owner_site_out[...] = site_owner
        owner_coeff_out[...] = coeff_owner
    else:
        cells = [state[0], state[1], state[2]]
        current = levels[...]
        segment = gathered(got, over, scal, 1, 4)
        site_owner = owner_site[...]
        coeff_owner = owner_coeff[...]
        segment_owner = owner_levels[...]
        outlets = jnp.where(even, over[pl.ds(2, 8, stride=BLOCK), :], got[other, :, 2, :])

    levels_next = advance_levels(
        scal, current, outlets, own[...], site_owner, coeff_owner, segment_owner, slots_owner
    )
    new = advance_cells(
        scal,
        cells,
        got,
        near,
        over,
        rough[...],
        cell,
        coeff_ref[...],
        segment,
        slots_ref[...],
        6 if first else 5,
    )
    for k in range(3):
        state_out[k] = new[k]
    levels_out[...] = levels_next
    owned = level_at_sites(
        lambda f, v: jnp.broadcast_to(levels_next[f : f + 1], (8, LANES)), site_owner
    )
    owner_levels_out[...] = owned
    slots = depth_at_slots(state_out, (0,), cell)
    slots_out[...] = slots
    send_ref[...] = jnp.zeros_like(send_ref)
    beside_ref[...] = jnp.zeros_like(beside_ref)
    across_ref[...] = jnp.zeros_like(across_ref)
    outlet_row = column_to_lane(levels_next[:, LANES - 1 : LANES], 0)
    for b in range(BASINS):
        for at, value in enumerate((slots, owned)):
            send_ref[mine, b, at : at + 1, :] = value[b : b + 1]
            send_ref[other, b, at : at + 1, :] = value[8 + b : 9 + b]
            send_ref[mine, b, 3 + at : 4 + at, :] = value[16 + b : 17 + b]
        send_ref[mine, b, 2:3, :] = outlet_row
        send_ref[other, b, 2:3, :] = outlet_row
    put_edges(send_ref, beside_ref, across_ref, new, even, mine, y, 5)


def call(kernel, outs, args, limit=16 << 20):
    specs = [pl.BlockSpec(memory_space=pltpu.SMEM)]
    specs += [pl.BlockSpec(memory_space=pltpu.VMEM) for _ in args[1:]]
    return pl.pallas_call(
        kernel,
        out_shape=outs,
        in_specs=specs,
        out_specs=[pl.BlockSpec(memory_space=pltpu.VMEM) for _ in outs],
        compiler_params=None if INTERPRET else pltpu.CompilerParams(vmem_limit_bytes=limit),
        interpret=INTERPRET,
    )(*args)


def f32(*shape):
    return jax.ShapeDtypeStruct(shape, jnp.float32)


def i32(*shape):
    return jax.ShapeDtypeStruct(shape, jnp.int32)


def per_device(
    depth,
    discharge,
    roughness,
    reach_state,
    celerity,
    base_inflow,
    upstream,
    bank_cell,
    bank_site,
    bank_coeff,
):
    count_x = lax.axis_size("gx")
    count_y = lax.axis_size("gy")
    gx = lax.axis_index("gx")
    gy = lax.axis_index("gy")
    core = gx % 2
    pairs = [list(range(c * 2 * count_y, (c + 1) * 2 * count_y)) for c in range(count_x // 2)]
    border = [(i, i + 1) for i in range(1, count_x - 1, 2)]
    border = border + [(b, a) for a, b in border]
    chip = [(i, i ^ 1) for i in range(count_x)]
    scal = jnp.stack(
        [core, gy, (gx == 0).astype(jnp.int32), (gx == count_x - 1).astype(jnp.int32)]
    ).astype(jnp.int32)

    def mine_of(array):
        return lax.dynamic_slice_in_dim(array, gy, 1, axis=0)

    ids = (gx - 1) * BASINS + jnp.arange(BASINS, dtype=jnp.int32)
    weight = jnp.sum((mine_of(upstream) == ids[:, None]).astype(jnp.float32), axis=1, keepdims=True)
    own = jnp.concatenate(
        [
            jnp.broadcast_to(mine_of(celerity).reshape(FIELDS, 1), (FIELDS, LANES)),
            jnp.broadcast_to(mine_of(base_inflow).reshape(FIELDS, 1), (FIELDS, LANES)),
            jnp.broadcast_to(weight, (BASINS, LANES)),
        ],
        axis=0,
    )

    def exchange(send, beside, across):
        got = lax.all_to_all(
            send.reshape(2 * BASINS, BLOCK, LANES), ("gx", "gy"), 0, 0, axis_index_groups=pairs
        )
        near = lax.ppermute(beside, "gx", chip)
        got, near = lax.optimization_barrier((got, near))
        part = lax.dynamic_slice(got, (core * BASINS, 0, 0), (BASINS, BLOCK, LANES))
        over = lax.ppermute(
            jnp.concatenate([part.reshape(BASINS * BLOCK, LANES), across], axis=0), "gx", border
        )
        return got.reshape(2, BASINS, BLOCK, LANES), near, over

    table = (SLOT_ROWS, LANES)
    block = f32(2, BASINS, BLOCK, LANES)
    send, beside, across, cell, site, coeff, slots = call(
        first_kernel,
        [block, f32(WHOLE, LANES), f32(WHOLE, LANES), i32(*table), i32(*table), f32(*table), f32(*table)],
        [scal, depth, discharge, bank_cell, bank_site, bank_coeff, reach_state],
        limit=60 << 20,
    )
    got, near, over = exchange(send, beside, across)
    for step in range(STEPS - 1):
        first = step == 0
        outs = [
            f32(3, ROWS, COLS),
            f32(FIELDS, LANES),
            f32(*table),
            f32(*table),
            block,
            f32(EDGE, LANES),
            f32(EDGE, LANES),
        ]
        if first:
            outs += [i32(*table), f32(*table)]
            args = [scal, depth, discharge, reach_state, site]
        else:
            args = [scal, state, levels, owner_levels, owner_site, owner_coeff]
        args += [got, near, over, roughness, own, cell, coeff, slots]
        result = call(functools.partial(step_kernel, first), outs, args)
        state, levels, owner_levels, slots, send, beside, across = result[:7]
        if first:
            owner_site, owner_coeff = result[7:9]
        got, near, over = exchange(send, beside, across)
    copies = call(
        levels_kernel,
        [f32(BASINS, FIELDS, LANES)],
        [scal, levels, owner_levels, owner_site, owner_coeff, got, over, own],
    )[0]
    final = lax.all_to_all(copies, "gy", 0, 0)
    state = call(
        cells_kernel,
        [f32(3, ROWS, COLS)],
        [scal, state, got, near, over, roughness, cell, coeff, slots],
    )[0]
    return state, final.reshape(BASINS, FIELDS * LANES)


def solution(mesh):
    return jax.shard_map(
        per_device,
        mesh=mesh,
        in_specs=(
            P("gx", "gy"),
            P(None, "gx", "gy"),
            P("gx", "gy"),
            P("gx", None),
            P("gx", None),
            P("gx", None),
            P("gx", None),
            P("gx", "gy"),
            P("gx", "gy"),
            P("gx", "gy"),
        ),
        out_specs=(P(None, "gx", "gy"), P("gx", None)),
        check_vma=False,
    )
```

```python
import functools

import jax
import jax.numpy as jnp
from jax import lax
from jax.experimental import pallas as pl
from jax.experimental.pallas import tpu as pltpu
from jax.sharding import PartitionSpec as P

STEPS = 4


GRAV = 9.81
DT = 0.5
DX = 10.0
NU = 0.1
RATIO = 0.25
FACTOR = DT / (2.0 * DX)

LANES = 128
ROWS = 32
QUADS = 4
COLS = QUADS * LANES
FIELDS = 8
BASINS = 8
SLOT_ROWS = 3 * BASINS
BLOCK = 8
EDGE = 16
WHOLE = EDGE + FIELDS * BASINS
INTERPRET = False


def iota(shape, dim):
    return lax.broadcasted_iota(jnp.int32, shape, dim)


def lane_gather(rows, index):
    return jnp.take_along_axis(rows, index, axis=1, mode="promise_in_bounds")


def lane_to_column(row, count, offset):
    wide = jnp.broadcast_to(row, (count, LANES))
    hit = iota((count, LANES), 1) == iota((count, LANES), 0) + offset
    return jnp.sum(jnp.where(hit, wide, 0.0), axis=1, keepdims=True)


def column_to_lane(column, offset):
    count = column.shape[0]
    wide = jnp.broadcast_to(column, (count, LANES))
    hit = iota((count, LANES), 1) == iota((count, LANES), 0) + offset
    return jnp.sum(jnp.where(hit, wide, 0.0), axis=0, keepdims=True)


def own_row(block, y):
    return jnp.sum(jnp.where(iota(block.shape, 0) == y, block, 0.0), axis=0, keepdims=True)


def flux_terms(cells):
    h, p, q = cells
    inverse = 1.0 / h
    u = p * inverse
    v = q * inverse
    pressure = 0.5 * GRAV * h * h
    return (p, p * u + pressure, q * u), (q, p * v, q * v + pressure), u, v


def flood_update(cells, top, low, left, right, rough, source):
    flux_x, flux_y, u, v = flux_terms(cells)
    top_x = flux_terms(top)[0]
    low_x = flux_terms(low)[0]
    left_y = flux_terms(left)[1]
    right_y = flux_terms(right)[1]
    row = iota((ROWS, COLS), 0)
    col = iota((ROWS, COLS), 1)
    out = []
    for k in range(3):
        quarter = 0.25 * cells[k]
        from_top = jnp.where(
            row == 0, 0.25 * top[k] + FACTOR * top_x[k], pltpu.roll(quarter + FACTOR * flux_x[k], 1, 0)
        )
        from_low = jnp.where(
            row == ROWS - 1,
            0.25 * low[k] - FACTOR * low_x[k],
            pltpu.roll(quarter - FACTOR * flux_x[k], ROWS - 1, 0),
        )
        from_left = jnp.where(
            col == 0, 0.25 * left[k] + FACTOR * left_y[k], pltpu.roll(quarter + FACTOR * flux_y[k], 1, 1)
        )
        from_right = jnp.where(
            col == COLS - 1,
            0.25 * right[k] - FACTOR * right_y[k],
            pltpu.roll(quarter - FACTOR * flux_y[k], COLS - 1, 1),
        )
        out.append((from_top + from_low) + (from_left + from_right))
    h = cells[0]
    size = jnp.abs(h)
    root = jnp.exp(jnp.log(size) * (-1.0 / 3.0))
    root = root * (4.0 - size * (root * root * root)) * (1.0 / 3.0)
    root = jnp.where(h < 0.0, -root, root)
    drag = (GRAV * DT) * rough * rough * jnp.sqrt(u * u + v * v) * root
    return [out[0] + DT * source, out[1] - drag * u, out[2] - drag * v]


def halves(values):
    high = values.astype(jnp.bfloat16).astype(jnp.float32)
    return high, values - high


def spread(rates, major, minor, count):
    total = None
    rows = rates.shape[0]
    group = 4
    high, low = halves(rates)
    for start in range(0, rows, group):
        left, right = [], []
        for r in range(start, start + group):
            at = iota((count, LANES), 0) == major[r : r + 1]
            left.append(
                jnp.concatenate(
                    [
                        jnp.where(at, high[r : r + 1], 0.0),
                        jnp.where(at, low[r : r + 1], 0.0),
                    ],
                    axis=0,
                ).astype(jnp.bfloat16)
            )
            right.append(
                jnp.where(iota((LANES, LANES), 0) == minor[r : r + 1], 1.0, 0.0).astype(jnp.bfloat16)
            )
        part = lax.dot_general(
            jnp.concatenate(left, axis=1),
            jnp.concatenate(right, axis=1),
            (((1,), (1,)), ((), ())),
            preferred_element_type=jnp.float32,
        )
        total = part if total is None else total + part
    return total[:count] + total[count:]


def cell_parts(cell):
    col = cell & (COLS - 1)
    return (col >> 7) * ROWS + (cell >> 9), col & (LANES - 1)


def depth_at_slots(h_ref, index, cell):
    major, minor = cell_parts(cell)
    found = []
    for v in range(3):
        key = major[8 * v : 8 * v + 8]
        lane = minor[8 * v : 8 * v + 8]
        depth = jnp.zeros((8, LANES), jnp.float32)
        for quad in range(QUADS):
            for row in range(ROWS):
                values = h_ref[index + (slice(row, row + 1), slice(quad * LANES, (quad + 1) * LANES))]
                values = jnp.broadcast_to(values, (8, LANES))
                depth = jnp.where(key == quad * ROWS + row, lane_gather(values, lane), depth)
        found.append(depth)
    return jnp.concatenate(found, axis=0)


def level_at_sites(reach_rows, site):
    found = []
    for v in range(3):
        sites = site[8 * v : 8 * v + 8]
        field = sites >> 7
        station = sites & (LANES - 1)
        level = jnp.zeros((8, LANES), jnp.float32)
        for f in range(FIELDS):
            level = jnp.where(field == f, lane_gather(reach_rows(f, v), station), level)
        found.append(level)
    return jnp.concatenate(found, axis=0)


def put_edges(send_ref, beside_ref, across_ref, cells, even, mine, y, col_row):
    lane_left = column_to_lane(cells[0][:, 0:1], 0)
    lane_right = column_to_lane(cells[0][:, COLS - 1 : COLS], 0)
    for k in (1, 2):
        lane_left = lane_left + column_to_lane(cells[k][:, 0:1], k * ROWS)
        lane_right = lane_right + column_to_lane(cells[k][:, COLS - 1 : COLS], k * ROWS)
    send_ref[mine, jnp.maximum(y - 1, 0), col_row : col_row + 1, :] = lane_left
    send_ref[mine, jnp.minimum(y + 1, BASINS - 1), col_row : col_row + 1, :] = lane_right
    for k in range(3):
        first = cells[k][0:1]
        last = cells[k][ROWS - 1 : ROWS]
        inner = jnp.where(even, last, first)
        outer = jnp.where(even, first, last)
        for quad in range(QUADS):
            at = k * QUADS + quad
            lanes = slice(quad * LANES, (quad + 1) * LANES)
            beside_ref[at : at + 1, :] = inner[:, lanes]
            across_ref[at : at + 1, :] = outer[:, lanes]


def get_edges(got_ref, near_ref, over_ref, cells, scal, mine, y, col_row):
    even = scal[0] == 0
    is_first, is_last = scal[2] == 1, scal[3] == 1
    before = got_ref[mine, jnp.maximum(y - 1, 0), col_row : col_row + 1, :]
    after = got_ref[mine, jnp.minimum(y + 1, BASINS - 1), col_row : col_row + 1, :]
    over_edge = BASINS * BLOCK
    top, low, left, right = [], [], [], []
    for k in range(3):
        inner = jnp.concatenate(
            [
                near_ref[k * QUADS + quad : k * QUADS + quad + 1, :]
                for quad in range(QUADS)
            ],
            axis=1,
        )
        outer = jnp.concatenate(
            [
                over_ref[over_edge + k * QUADS + quad : over_edge + k * QUADS + quad + 1, :]
                for quad in range(QUADS)
            ],
            axis=1,
        )
        top.append(jnp.where(is_first, cells[k][0:1], jnp.where(even, outer, inner)))
        low.append(jnp.where(is_last, cells[k][ROWS - 1 : ROWS], jnp.where(even, inner, outer)))
        left.append(jnp.where(y == 0, cells[k][:, 0:1], lane_to_column(before, ROWS, k * ROWS)))
        right.append(
            jnp.where(
                y == BASINS - 1, cells[k][:, COLS - 1 : COLS], lane_to_column(after, ROWS, k * ROWS)
            )
        )
    return top, low, left, right


def river_update(current, outlets, own, lateral):
    rate = own[0:8]
    base = own[8:16, 0:1]
    weight = own[16:24]
    inflow_row = jnp.sum(weight * outlets, axis=0, keepdims=True)
    inflow = base + lane_to_column(inflow_row, FIELDS, 0)
    lane = iota((FIELDS, LANES), 1)
    sub = iota((FIELDS, LANES), 0)
    behind = jnp.where(lane == 0, inflow, pltpu.roll(current, 1, 1))
    above = jnp.where(sub == FIELDS - 1, current, pltpu.roll(current, FIELDS - 1, 0))
    below = jnp.where(sub == 0, current, pltpu.roll(current, 1, 0))
    mixing = above - 2.0 * current + below
    return current - rate * (current - behind) + NU * mixing - (DT * RATIO) * lateral


def owned_terms(celerity, base_inflow, upstream, y):
    square = iota((FIELDS, FIELDS), 0) == iota((FIELDS, FIELDS), 1)

    def by_field(ref):
        row = jnp.broadcast_to(own_row(ref[...], y), (FIELDS, FIELDS))
        return jnp.sum(jnp.where(square, row, 0.0), axis=1, keepdims=True)

    feeders = own_row(upstream[...].astype(jnp.float32), y)
    ids = ((lax.axis_index("gx") - 1) * BASINS + iota((BASINS, feeders.shape[1]), 0)).astype(jnp.float32)
    hits = jnp.where(jnp.broadcast_to(feeders, ids.shape) == ids, 1.0, 0.0)
    weight = jnp.sum(hits, axis=1, keepdims=True)
    return jnp.concatenate(
        [jnp.broadcast_to(column, (8, LANES)) for column in (by_field(celerity), by_field(base_inflow), weight)],
        axis=0,
    )


def first_kernel(
    depth,
    discharge,
    cell_in,
    site_in,
    coeff_in,
    reach,
    send_ref,
    beside_ref,
    across_ref,
    cell_ref,
    site_ref,
    coeff_ref,
    slots_ref,
):
    scal = place()
    even = scal[0] == 0
    mine, other, y = scal[0], 1 - scal[0], scal[1]
    send_ref[...] = jnp.zeros_like(send_ref)

    def arranged(ref):
        low, own, high = ref[0:8], ref[8:16], ref[16:24]
        return jnp.concatenate([own, jnp.where(even, high, low), jnp.where(even, low, high)], axis=0)

    cell = arranged(cell_in)
    site = arranged(site_in)
    coeff = jnp.where(cell >= 0, arranged(coeff_in), 0.0)
    cell = jnp.maximum(cell, 0)
    cell_ref[...] = cell
    site_ref[...] = site
    coeff_ref[...] = coeff
    slots = depth_at_slots(depth, (), cell)
    slots_ref[...] = slots
    site_value = site.astype(jnp.float32)
    for b in range(BASINS):
        for at, value in enumerate((slots, site_value, coeff)):
            send_ref[mine, b, at : at + 1, :] = value[b : b + 1]
            send_ref[other, b, at : at + 1, :] = value[8 + b : 9 + b]
            send_ref[mine, b, 3 + at : 4 + at, :] = value[16 + b : 17 + b]
    for ref in (beside_ref, across_ref):
        ref[0:EDGE] = jnp.zeros((EDGE, LANES), jnp.float32)
        for f in range(FIELDS):
            ref[EDGE + 8 * f : EDGE + 8 * f + 8] = reach[:, f * LANES : (f + 1) * LANES]
    cells = [depth[...], discharge[0], discharge[1]]
    put_edges(send_ref, beside_ref, across_ref, cells, even, mine, y, 6)


OVER = BASINS * BLOCK


def place():
    gx = lax.axis_index("gx")
    y = lax.axis_index("gy")
    last = lax.axis_size("gx") - 1
    return gx & 1, y, (gx == 0).astype(jnp.int32), (gx == last).astype(jnp.int32)


def gathered(got, over, scal, row, across_row):
    mine, other = scal[0], 1 - scal[0]
    return jnp.concatenate(
        [got[mine, :, row, :], got[other, :, row, :], over[pl.ds(across_row, 8, stride=BLOCK), :]],
        axis=0,
    )


def advance_levels(scal, current, outlets, own, site_owner, coeff_owner, segment_owner, slots_owner):
    rates = coeff_owner * (segment_owner - slots_owner)
    lateral = spread(rates, site_owner >> 7, site_owner & (LANES - 1), FIELDS)
    return river_update(current, outlets, own, lateral)


def advance_cells(scal, cells, got, near, over, rough, cell, coeff, segment, slots, col_row):
    mine, y = scal[0], scal[1]
    major, minor = cell_parts(cell)
    rates = coeff * (segment - slots)
    blocks = spread(rates, major, minor, QUADS * ROWS)
    source = jnp.concatenate([blocks[q * ROWS : (q + 1) * ROWS] for q in range(QUADS)], axis=1)
    top, low, left, right = get_edges(got, near, over, cells, scal, mine, y, col_row)
    return flood_update(cells, top, low, left, right, rough, source)


def levels_kernel(levels, owner_levels, owner_site, owner_coeff, got, over, own, all_levels):
    scal = place()
    even = scal[0] == 0
    outlets = jnp.where(even, over[pl.ds(2, 8, stride=BLOCK), :], got[1 - scal[0], :, 2, :])
    new = advance_levels(
        scal,
        levels[...],
        outlets,
        own[...],
        owner_site[...],
        owner_coeff[...],
        owner_levels[...],
        gathered(got, over, scal, 0, 3),
    )
    for b in range(BASINS):
        all_levels[b] = new


def cells_kernel(state, got, near, over, rough, cell_ref, coeff_ref, slots_ref, state_out):
    scal = place()
    new = advance_cells(
        scal,
        [state[0], state[1], state[2]],
        got,
        near,
        over,
        rough[...],
        cell_ref[...],
        coeff_ref[...],
        gathered(got, over, scal, 1, 4),
        slots_ref[...],
        5,
    )
    for k in range(3):
        state_out[k] = new[k]


def step_kernel(first, *refs):
    refs = list(refs)

    def take(n):
        taken = refs[:n]
        del refs[:n]
        return taken

    scal = place()
    if first:
        depth, discharge, reach, site_ref, celerity, base_inflow, upstream = take(7)
    else:
        state, levels, owner_levels, owner_site, owner_coeff = take(5)
    if not first:
        own = take(1)[0][...]
    got, near, over, rough, cell_ref, coeff_ref, slots_ref = take(7)
    state_out, levels_out, owner_levels_out, slots_out, send_ref, beside_ref, across_ref = take(7)
    if first:
        owner_site_out, owner_coeff_out, own_out = take(3)
    even = scal[0] == 0
    mine, other, y = scal[0], 1 - scal[0], scal[1]
    cell = cell_ref[...]

    slots_owner = gathered(got, over, scal, 0, 3)
    if first:
        cells = [depth[...], discharge[0], discharge[1]]
        current = jnp.concatenate(
            [own_row(reach[:, f * LANES : (f + 1) * LANES], y) for f in range(FIELDS)], axis=0
        )

        def tile_rows(f, v):
            if v == 0:
                return reach[:, f * LANES : (f + 1) * LANES]
            if v == 1:
                return near[EDGE + 8 * f : EDGE + 8 * f + 8, :]
            return over[OVER + EDGE + 8 * f : OVER + EDGE + 8 * f + 8, :]

        segment = level_at_sites(tile_rows, site_ref[...])
        site_owner = gathered(got, over, scal, 1, 4).astype(jnp.int32)
        coeff_owner = gathered(got, over, scal, 2, 5)
        outlets = jnp.zeros((BASINS, LANES), jnp.float32)
        for f in range(FIELDS):
            source_rows = jnp.where(even, tile_rows(f, 2), tile_rows(f, 1))
            outlets = jnp.where(
                iota((BASINS, LANES), 1) == f, source_rows[:, LANES - 1 : LANES], outlets
            )
        segment_owner = level_at_sites(
            lambda f, v: jnp.broadcast_to(current[f : f + 1], (8, LANES)), site_owner
        )
        owner_site_out[...] = site_owner
        owner_coeff_out[...] = coeff_owner
        own = owned_terms(celerity, base_inflow, upstream, y)
        own_out[...] = own
    else:
        cells = [state[0], state[1], state[2]]
        current = levels[...]
        segment = gathered(got, over, scal, 1, 4)
        site_owner = owner_site[...]
        coeff_owner = owner_coeff[...]
        segment_owner = owner_levels[...]
        outlets = jnp.where(even, over[pl.ds(2, 8, stride=BLOCK), :], got[other, :, 2, :])

    levels_next = advance_levels(
        scal, current, outlets, own, site_owner, coeff_owner, segment_owner, slots_owner
    )
    new = advance_cells(
        scal,
        cells,
        got,
        near,
        over,
        rough[...],
        cell,
        coeff_ref[...],
        segment,
        slots_ref[...],
        6 if first else 5,
    )
    for k in range(3):
        state_out[k] = new[k]
    levels_out[...] = levels_next
    owned = level_at_sites(
        lambda f, v: jnp.broadcast_to(levels_next[f : f + 1], (8, LANES)), site_owner
    )
    owner_levels_out[...] = owned
    slots = depth_at_slots(state_out, (0,), cell)
    slots_out[...] = slots
    send_ref[...] = jnp.zeros_like(send_ref)
    beside_ref[...] = jnp.zeros_like(beside_ref)
    across_ref[...] = jnp.zeros_like(across_ref)
    outlet_row = column_to_lane(levels_next[:, LANES - 1 : LANES], 0)
    for b in range(BASINS):
        for at, value in enumerate((slots, owned)):
            send_ref[mine, b, at : at + 1, :] = value[b : b + 1]
            send_ref[other, b, at : at + 1, :] = value[8 + b : 9 + b]
            send_ref[mine, b, 3 + at : 4 + at, :] = value[16 + b : 17 + b]
        send_ref[mine, b, 2:3, :] = outlet_row
        send_ref[other, b, 2:3, :] = outlet_row
    put_edges(send_ref, beside_ref, across_ref, new, even, mine, y, 5)


def call(kernel, outs, args, limit=16 << 20):
    specs = [pl.BlockSpec(memory_space=pltpu.VMEM) for _ in args]
    return pl.pallas_call(
        kernel,
        out_shape=outs,
        in_specs=specs,
        out_specs=[pl.BlockSpec(memory_space=pltpu.VMEM) for _ in outs],
        compiler_params=None if INTERPRET else pltpu.CompilerParams(vmem_limit_bytes=limit),
        interpret=INTERPRET,
    )(*args)


def f32(*shape):
    return jax.ShapeDtypeStruct(shape, jnp.float32)


def i32(*shape):
    return jax.ShapeDtypeStruct(shape, jnp.int32)


def per_device(
    depth,
    discharge,
    roughness,
    reach_state,
    celerity,
    base_inflow,
    upstream,
    bank_cell,
    bank_site,
    bank_coeff,
):
    count_x = lax.axis_size("gx")
    count_y = lax.axis_size("gy")
    gx = lax.axis_index("gx")
    core = gx & 1
    pairs = [list(range(c * 2 * count_y, (c + 1) * 2 * count_y)) for c in range(count_x // 2)]
    border = [(i, i + 1) for i in range(1, count_x - 1, 2)]
    border = border + [(b, a) for a, b in border]
    chip = [(i, i ^ 1) for i in range(count_x)]
    def exchange(send, beside, across):
        got = lax.all_to_all(
            send.reshape(2 * BASINS, BLOCK, LANES), ("gx", "gy"), 0, 0, axis_index_groups=pairs
        )
        part = lax.dynamic_slice(got, (core * BASINS, 0, 0), (BASINS, BLOCK, LANES))
        packed = jnp.concatenate([part.reshape(BASINS * BLOCK, LANES), across], axis=0)
        packed, beside = lax.optimization_barrier((packed, beside))
        over = lax.ppermute(packed, "gx", border)
        near = lax.ppermute(beside, "gx", chip)
        near, over = lax.optimization_barrier((near, over))
        return got.reshape(2, BASINS, BLOCK, LANES), near, over

    table = (SLOT_ROWS, LANES)
    block = f32(2, BASINS, BLOCK, LANES)
    send, beside, across, cell, site, coeff, slots = call(
        first_kernel,
        [block, f32(WHOLE, LANES), f32(WHOLE, LANES), i32(*table), i32(*table), f32(*table), f32(*table)],
        [depth, discharge, bank_cell, bank_site, bank_coeff, reach_state],
        limit=60 << 20,
    )
    got, near, over = exchange(send, beside, across)
    for step in range(STEPS - 1):
        first = step == 0
        outs = [
            f32(3, ROWS, COLS),
            f32(FIELDS, LANES),
            f32(*table),
            f32(*table),
            block,
            f32(EDGE, LANES),
            f32(EDGE, LANES),
        ]
        if first:
            outs += [i32(*table), f32(*table), f32(*table)]
            args = [depth, discharge, reach_state, site, celerity, base_inflow, upstream]
        else:
            args = [state, levels, owner_levels, owner_site, owner_coeff, own]
        args += [got, near, over, roughness, cell, coeff, slots]
        result = call(functools.partial(step_kernel, first), outs, args)
        state, levels, owner_levels, slots, send, beside, across = result[:7]
        if first:
            owner_site, owner_coeff, own = result[7:10]
        got, near, over = exchange(send, beside, across)
    copies = call(
        levels_kernel,
        [f32(BASINS, FIELDS, LANES)],
        [levels, owner_levels, owner_site, owner_coeff, got, over, own],
    )[0]
    final = lax.all_to_all(copies, "gy", 0, 0)
    state = call(
        cells_kernel,
        [f32(3, ROWS, COLS)],
        [state, got, near, over, roughness, cell, coeff, slots],
    )[0]
    return state, final.reshape(BASINS, FIELDS * LANES)


def solution(mesh):
    return jax.shard_map(
        per_device,
        mesh=mesh,
        in_specs=(
            P("gx", "gy"),
            P(None, "gx", "gy"),
            P("gx", "gy"),
            P("gx", None),
            P("gx", None),
            P("gx", None),
            P("gx", None),
            P("gx", "gy"),
            P("gx", "gy"),
            P("gx", "gy"),
        ),
        out_specs=(P(None, "gx", "gy"), P("gx", None)),
        check_vma=False,
    )
```

```python
import functools

import jax
import jax.numpy as jnp
from jax import lax
from jax.experimental import pallas as pl
from jax.experimental.pallas import tpu as pltpu
from jax.sharding import PartitionSpec as P

STEPS = 4


GRAV = 9.81
DT = 0.5
DX = 10.0
NU = 0.1
RATIO = 0.25
FACTOR = DT / (2.0 * DX)

LANES = 128
ROWS = 32
QUADS = 4
COLS = QUADS * LANES
FIELDS = 8
BASINS = 8
SLOT_ROWS = 3 * BASINS
BLOCK = 8
FIRST_ROWS = 24
STEP_ROWS = 16
EDGE_ROW = 3
LEVEL_ROW = 15
EDGE = 16
WHOLE = EDGE + FIELDS * BASINS
INTERPRET = False


def iota(shape, dim):
    return lax.broadcasted_iota(jnp.int32, shape, dim)


def lane_gather(rows, index):
    return jnp.take_along_axis(rows, index, axis=1, mode="promise_in_bounds")


def lane_to_column(row, count, offset):
    wide = jnp.broadcast_to(row, (count, LANES))
    hit = iota((count, LANES), 1) == iota((count, LANES), 0) + offset
    return jnp.sum(jnp.where(hit, wide, 0.0), axis=1, keepdims=True)


def column_to_lane(column, offset):
    count = column.shape[0]
    wide = jnp.broadcast_to(column, (count, LANES))
    hit = iota((count, LANES), 1) == iota((count, LANES), 0) + offset
    return jnp.sum(jnp.where(hit, wide, 0.0), axis=0, keepdims=True)


def own_row(block, y):
    return jnp.sum(jnp.where(iota(block.shape, 0) == y, block, 0.0), axis=0, keepdims=True)


def flux_terms(cells):
    h, p, q = cells
    inverse = 1.0 / h
    u = p * inverse
    v = q * inverse
    pressure = 0.5 * GRAV * h * h
    return (p, p * u + pressure, q * u), (q, p * v, q * v + pressure), u, v


def flood_update(cells, top, low, left, right, rough, source):
    flux_x, flux_y, u, v = flux_terms(cells)
    top_x = flux_terms(top)[0]
    low_x = flux_terms(low)[0]
    left_y = flux_terms(left)[1]
    right_y = flux_terms(right)[1]
    row = iota((ROWS, COLS), 0)
    col = iota((ROWS, COLS), 1)
    out = []
    for k in range(3):
        quarter = 0.25 * cells[k]
        from_top = jnp.where(
            row == 0, 0.25 * top[k] + FACTOR * top_x[k], pltpu.roll(quarter + FACTOR * flux_x[k], 1, 0)
        )
        from_low = jnp.where(
            row == ROWS - 1,
            0.25 * low[k] - FACTOR * low_x[k],
            pltpu.roll(quarter - FACTOR * flux_x[k], ROWS - 1, 0),
        )
        from_left = jnp.where(
            col == 0, 0.25 * left[k] + FACTOR * left_y[k], pltpu.roll(quarter + FACTOR * flux_y[k], 1, 1)
        )
        from_right = jnp.where(
            col == COLS - 1,
            0.25 * right[k] - FACTOR * right_y[k],
            pltpu.roll(quarter - FACTOR * flux_y[k], COLS - 1, 1),
        )
        out.append((from_top + from_low) + (from_left + from_right))
    h = cells[0]
    size = jnp.abs(h)
    root = jnp.exp(jnp.log(size) * (-1.0 / 3.0))
    root = root * (4.0 - size * (root * root * root)) * (1.0 / 3.0)
    root = jnp.where(h < 0.0, -root, root)
    drag = (GRAV * DT) * rough * rough * jnp.sqrt(u * u + v * v) * root
    return [out[0] + DT * source, out[1] - drag * u, out[2] - drag * v]


def halves(values):
    high = values.astype(jnp.bfloat16).astype(jnp.float32)
    return high, values - high


def spread(rates, major, minor, count):
    total = None
    rows = rates.shape[0]
    group = 4
    high, low = halves(rates)
    for start in range(0, rows, group):
        left, right = [], []
        for r in range(start, start + group):
            at = iota((count, LANES), 0) == major[r : r + 1]
            left.append(
                jnp.concatenate(
                    [
                        jnp.where(at, high[r : r + 1], 0.0),
                        jnp.where(at, low[r : r + 1], 0.0),
                    ],
                    axis=0,
                ).astype(jnp.bfloat16)
            )
            right.append(
                jnp.where(iota((LANES, LANES), 0) == minor[r : r + 1], 1.0, 0.0).astype(jnp.bfloat16)
            )
        part = lax.dot_general(
            jnp.concatenate(left, axis=1),
            jnp.concatenate(right, axis=1),
            (((1,), (1,)), ((), ())),
            preferred_element_type=jnp.float32,
        )
        total = part if total is None else total + part
    return total[:count] + total[count:]


def cell_parts(cell):
    col = cell & (COLS - 1)
    return (col >> 7) * ROWS + (cell >> 9), col & (LANES - 1)


def depth_at_slots(h_ref, index, cell):
    major, minor = cell_parts(cell)
    found = []
    for v in range(3):
        key = major[8 * v : 8 * v + 8]
        lane = minor[8 * v : 8 * v + 8]
        depth = jnp.zeros((8, LANES), jnp.float32)
        for quad in range(QUADS):
            for row in range(ROWS):
                values = h_ref[index + (slice(row, row + 1), slice(quad * LANES, (quad + 1) * LANES))]
                values = jnp.broadcast_to(values, (8, LANES))
                depth = jnp.where(key == quad * ROWS + row, lane_gather(values, lane), depth)
        found.append(depth)
    return jnp.concatenate(found, axis=0)


def level_at_sites(reach_rows, site):
    found = []
    for v in range(3):
        sites = site[8 * v : 8 * v + 8]
        field = sites >> 7
        station = sites & (LANES - 1)
        level = jnp.zeros((8, LANES), jnp.float32)
        for f in range(FIELDS):
            level = jnp.where(field == f, lane_gather(reach_rows(f, v), station), level)
        found.append(level)
    return jnp.concatenate(found, axis=0)


def put_edges(send_ref, across_ref, cells, even, mine, y, col_row):
    lane_left = column_to_lane(cells[0][:, 0:1], 0)
    lane_right = column_to_lane(cells[0][:, COLS - 1 : COLS], 0)
    for k in (1, 2):
        lane_left = lane_left + column_to_lane(cells[k][:, 0:1], k * ROWS)
        lane_right = lane_right + column_to_lane(cells[k][:, COLS - 1 : COLS], k * ROWS)
    send_ref[mine, jnp.maximum(y - 1, 0), col_row : col_row + 1, :] = lane_left
    send_ref[mine, jnp.minimum(y + 1, BASINS - 1), col_row : col_row + 1, :] = lane_right
    for k in range(3):
        first = cells[k][0:1]
        last = cells[k][ROWS - 1 : ROWS]
        inner = jnp.where(even, last, first)
        outer = jnp.where(even, first, last)
        for quad in range(QUADS):
            at = k * QUADS + quad
            lanes = slice(quad * LANES, (quad + 1) * LANES)
            send_ref[1 - mine, y, EDGE_ROW + at : EDGE_ROW + at + 1, :] = inner[:, lanes]
            across_ref[at : at + 1, :] = outer[:, lanes]


def get_edges(got_ref, over_ref, cells, scal, mine, y, col_row):
    even = scal[0] == 0
    is_first, is_last = scal[2] == 1, scal[3] == 1
    before = got_ref[mine, jnp.maximum(y - 1, 0), col_row : col_row + 1, :]
    after = got_ref[mine, jnp.minimum(y + 1, BASINS - 1), col_row : col_row + 1, :]
    over_edge = BASINS * BLOCK
    top, low, left, right = [], [], [], []
    for k in range(3):
        inner = jnp.concatenate(
            [
                got_ref[1 - mine, y, EDGE_ROW + k * QUADS + quad : EDGE_ROW + k * QUADS + quad + 1, :]
                for quad in range(QUADS)
            ],
            axis=1,
        )
        outer = jnp.concatenate(
            [
                over_ref[over_edge + k * QUADS + quad : over_edge + k * QUADS + quad + 1, :]
                for quad in range(QUADS)
            ],
            axis=1,
        )
        top.append(jnp.where(is_first, cells[k][0:1], jnp.where(even, outer, inner)))
        low.append(jnp.where(is_last, cells[k][ROWS - 1 : ROWS], jnp.where(even, inner, outer)))
        left.append(jnp.where(y == 0, cells[k][:, 0:1], lane_to_column(before, ROWS, k * ROWS)))
        right.append(
            jnp.where(
                y == BASINS - 1, cells[k][:, COLS - 1 : COLS], lane_to_column(after, ROWS, k * ROWS)
            )
        )
    return top, low, left, right


def river_update(current, outlets, own, lateral):
    rate = own[0:8]
    base = own[8:16, 0:1]
    weight = own[16:24]
    inflow_row = jnp.sum(weight * outlets, axis=0, keepdims=True)
    inflow = base + lane_to_column(inflow_row, FIELDS, 0)
    lane = iota((FIELDS, LANES), 1)
    sub = iota((FIELDS, LANES), 0)
    behind = jnp.where(lane == 0, inflow, pltpu.roll(current, 1, 1))
    above = jnp.where(sub == FIELDS - 1, current, pltpu.roll(current, FIELDS - 1, 0))
    below = jnp.where(sub == 0, current, pltpu.roll(current, 1, 0))
    mixing = above - 2.0 * current + below
    return current - rate * (current - behind) + NU * mixing - (DT * RATIO) * lateral


def owned_terms(celerity, base_inflow, upstream, y):
    square = iota((FIELDS, FIELDS), 0) == iota((FIELDS, FIELDS), 1)

    def by_field(ref):
        row = jnp.broadcast_to(own_row(ref[...], y), (FIELDS, FIELDS))
        return jnp.sum(jnp.where(square, row, 0.0), axis=1, keepdims=True)

    feeders = own_row(upstream[...].astype(jnp.float32), y)
    ids = ((lax.axis_index("gx") - 1) * BASINS + iota((BASINS, feeders.shape[1]), 0)).astype(jnp.float32)
    hits = jnp.where(jnp.broadcast_to(feeders, ids.shape) == ids, 1.0, 0.0)
    weight = jnp.sum(hits, axis=1, keepdims=True)
    return jnp.concatenate(
        [jnp.broadcast_to(column, (8, LANES)) for column in (by_field(celerity), by_field(base_inflow), weight)],
        axis=0,
    )


def first_kernel(
    depth,
    discharge,
    cell_in,
    site_in,
    coeff_in,
    reach,
    send_ref,
    across_ref,
    cell_ref,
    site_ref,
    coeff_ref,
    slots_ref,
):
    scal = place()
    even = scal[0] == 0
    mine, other, y = scal[0], 1 - scal[0], scal[1]
    send_ref[...] = jnp.zeros_like(send_ref)

    def arranged(ref):
        low, own, high = ref[0:8], ref[8:16], ref[16:24]
        return jnp.concatenate([own, jnp.where(even, high, low), jnp.where(even, low, high)], axis=0)

    cell = arranged(cell_in)
    site = arranged(site_in)
    coeff = jnp.where(cell >= 0, arranged(coeff_in), 0.0)
    cell = jnp.maximum(cell, 0)
    cell_ref[...] = cell
    site_ref[...] = site
    coeff_ref[...] = coeff
    slots = depth_at_slots(depth, (), cell)
    slots_ref[...] = slots
    site_value = site.astype(jnp.float32)
    for b in range(BASINS):
        for at, value in enumerate((slots, site_value, coeff)):
            send_ref[mine, b, at : at + 1, :] = value[b : b + 1]
            send_ref[other, b, at : at + 1, :] = value[8 + b : 9 + b]
            send_ref[mine, b, 3 + at : 4 + at, :] = value[16 + b : 17 + b]
    across_ref[0:EDGE] = jnp.zeros((EDGE, LANES), jnp.float32)
    for f in range(FIELDS):
        rows = reach[:, f * LANES : (f + 1) * LANES]
        across_ref[EDGE + 8 * f : EDGE + 8 * f + 8] = rows
        row = own_row(rows, y)
        for b in range(BASINS):
            send_ref[other, b, LEVEL_ROW + f : LEVEL_ROW + f + 1, :] = row
    cells = [depth[...], discharge[0], discharge[1]]
    put_edges(send_ref, across_ref, cells, even, mine, y, 6)


OVER = BASINS * BLOCK


def place():
    gx = lax.axis_index("gx")
    y = lax.axis_index("gy")
    last = lax.axis_size("gx") - 1
    return gx & 1, y, (gx == 0).astype(jnp.int32), (gx == last).astype(jnp.int32)


def gathered(got, over, scal, row, across_row):
    mine, other = scal[0], 1 - scal[0]
    return jnp.concatenate(
        [got[mine, :, row, :], got[other, :, row, :], over[pl.ds(across_row, 8, stride=BLOCK), :]],
        axis=0,
    )


def advance_levels(scal, current, outlets, own, site_owner, coeff_owner, segment_owner, slots_owner):
    rates = coeff_owner * (segment_owner - slots_owner)
    lateral = spread(rates, site_owner >> 7, site_owner & (LANES - 1), FIELDS)
    return river_update(current, outlets, own, lateral)


def advance_cells(scal, cells, got, over, rough, cell, coeff, segment, slots, col_row):
    mine, y = scal[0], scal[1]
    major, minor = cell_parts(cell)
    rates = coeff * (segment - slots)
    blocks = spread(rates, major, minor, QUADS * ROWS)
    source = jnp.concatenate([blocks[q * ROWS : (q + 1) * ROWS] for q in range(QUADS)], axis=1)
    top, low, left, right = get_edges(got, over, cells, scal, mine, y, col_row)
    return flood_update(cells, top, low, left, right, rough, source)


def levels_kernel(levels, owner_levels, owner_site, owner_coeff, got, over, own, all_levels):
    scal = place()
    even = scal[0] == 0
    outlets = jnp.where(even, over[pl.ds(2, 8, stride=BLOCK), :], got[1 - scal[0], :, 2, :])
    new = advance_levels(
        scal,
        levels[...],
        outlets,
        own[...],
        owner_site[...],
        owner_coeff[...],
        owner_levels[...],
        gathered(got, over, scal, 0, 3),
    )
    for b in range(BASINS):
        all_levels[b] = new


def cells_kernel(state, got, over, rough, cell_ref, coeff_ref, slots_ref, state_out):
    scal = place()
    new = advance_cells(
        scal,
        [state[0], state[1], state[2]],
        got,
        over,
        rough[...],
        cell_ref[...],
        coeff_ref[...],
        gathered(got, over, scal, 1, 4),
        slots_ref[...],
        5,
    )
    for k in range(3):
        state_out[k] = new[k]


def step_kernel(first, *refs):
    refs = list(refs)

    def take(n):
        taken = refs[:n]
        del refs[:n]
        return taken

    scal = place()
    if first:
        depth, discharge, reach, site_ref, celerity, base_inflow, upstream = take(7)
    else:
        state, levels, owner_levels, owner_site, owner_coeff = take(5)
    if not first:
        own = take(1)[0][...]
    got, over, rough, cell_ref, coeff_ref, slots_ref = take(6)
    state_out, levels_out, owner_levels_out, slots_out, send_ref, across_ref = take(6)
    if first:
        owner_site_out, owner_coeff_out, own_out = take(3)
    even = scal[0] == 0
    mine, other, y = scal[0], 1 - scal[0], scal[1]
    cell = cell_ref[...]

    slots_owner = gathered(got, over, scal, 0, 3)
    if first:
        cells = [depth[...], discharge[0], discharge[1]]
        current = jnp.concatenate(
            [own_row(reach[:, f * LANES : (f + 1) * LANES], y) for f in range(FIELDS)], axis=0
        )

        def tile_rows(f, v):
            if v == 0:
                return reach[:, f * LANES : (f + 1) * LANES]
            if v == 1:
                return got[other, :, LEVEL_ROW + f, :]
            return over[OVER + EDGE + 8 * f : OVER + EDGE + 8 * f + 8, :]

        segment = level_at_sites(tile_rows, site_ref[...])
        site_owner = gathered(got, over, scal, 1, 4).astype(jnp.int32)
        coeff_owner = gathered(got, over, scal, 2, 5)
        outlets = jnp.zeros((BASINS, LANES), jnp.float32)
        for f in range(FIELDS):
            source_rows = jnp.where(even, tile_rows(f, 2), tile_rows(f, 1))
            outlets = jnp.where(
                iota((BASINS, LANES), 1) == f, source_rows[:, LANES - 1 : LANES], outlets
            )
        segment_owner = level_at_sites(
            lambda f, v: jnp.broadcast_to(current[f : f + 1], (8, LANES)), site_owner
        )
        owner_site_out[...] = site_owner
        owner_coeff_out[...] = coeff_owner
        own = owned_terms(celerity, base_inflow, upstream, y)
        own_out[...] = own
    else:
        cells = [state[0], state[1], state[2]]
        current = levels[...]
        segment = gathered(got, over, scal, 1, 4)
        site_owner = owner_site[...]
        coeff_owner = owner_coeff[...]
        segment_owner = owner_levels[...]
        outlets = jnp.where(even, over[pl.ds(2, 8, stride=BLOCK), :], got[other, :, 2, :])

    levels_next = advance_levels(
        scal, current, outlets, own, site_owner, coeff_owner, segment_owner, slots_owner
    )
    new = advance_cells(
        scal,
        cells,
        got,
        over,
        rough[...],
        cell,
        coeff_ref[...],
        segment,
        slots_ref[...],
        6 if first else 5,
    )
    for k in range(3):
        state_out[k] = new[k]
    levels_out[...] = levels_next
    owned = level_at_sites(
        lambda f, v: jnp.broadcast_to(levels_next[f : f + 1], (8, LANES)), site_owner
    )
    owner_levels_out[...] = owned
    slots = depth_at_slots(state_out, (0,), cell)
    slots_out[...] = slots
    send_ref[...] = jnp.zeros_like(send_ref)
    across_ref[...] = jnp.zeros_like(across_ref)
    outlet_row = column_to_lane(levels_next[:, LANES - 1 : LANES], 0)
    for b in range(BASINS):
        for at, value in enumerate((slots, owned)):
            send_ref[mine, b, at : at + 1, :] = value[b : b + 1]
            send_ref[other, b, at : at + 1, :] = value[8 + b : 9 + b]
            send_ref[mine, b, 3 + at : 4 + at, :] = value[16 + b : 17 + b]
        send_ref[mine, b, 2:3, :] = outlet_row
        send_ref[other, b, 2:3, :] = outlet_row
    put_edges(send_ref, across_ref, new, even, mine, y, 5)


def call(kernel, outs, args, limit=16 << 20):
    specs = [pl.BlockSpec(memory_space=pltpu.VMEM) for _ in args]
    return pl.pallas_call(
        kernel,
        out_shape=outs,
        in_specs=specs,
        out_specs=[pl.BlockSpec(memory_space=pltpu.VMEM) for _ in outs],
        compiler_params=None if INTERPRET else pltpu.CompilerParams(vmem_limit_bytes=limit),
        interpret=INTERPRET,
    )(*args)


def f32(*shape):
    return jax.ShapeDtypeStruct(shape, jnp.float32)


def i32(*shape):
    return jax.ShapeDtypeStruct(shape, jnp.int32)


def per_device(
    depth,
    discharge,
    roughness,
    reach_state,
    celerity,
    base_inflow,
    upstream,
    bank_cell,
    bank_site,
    bank_coeff,
):
    count_x = lax.axis_size("gx")
    count_y = lax.axis_size("gy")
    gx = lax.axis_index("gx")
    core = gx & 1
    pairs = [list(range(c * 2 * count_y, (c + 1) * 2 * count_y)) for c in range(count_x // 2)]
    border = [(i, i + 1) for i in range(1, count_x - 1, 2)]
    border = border + [(b, a) for a, b in border]
    def exchange(send, across):
        rows = send.shape[2]
        got = lax.all_to_all(
            send.reshape(2 * BASINS, rows, LANES), ("gx", "gy"), 0, 0, axis_index_groups=pairs
        )
        part = lax.dynamic_slice(got, (core * BASINS, 0, 0), (BASINS, BLOCK, LANES))
        packed = jnp.concatenate([part.reshape(BASINS * BLOCK, LANES), across], axis=0)
        over = lax.ppermute(packed, "gx", border)
        return got.reshape(2, BASINS, rows, LANES), over

    table = (SLOT_ROWS, LANES)
    send, across, cell, site, coeff, slots = call(
        first_kernel,
        [
            f32(2, BASINS, FIRST_ROWS, LANES),
            f32(WHOLE, LANES),
            i32(*table),
            i32(*table),
            f32(*table),
            f32(*table),
        ],
        [depth, discharge, bank_cell, bank_site, bank_coeff, reach_state],
        limit=60 << 20,
    )
    got, over = exchange(send, across)
    for step in range(STEPS - 1):
        first = step == 0
        outs = [
            f32(3, ROWS, COLS),
            f32(FIELDS, LANES),
            f32(*table),
            f32(*table),
            f32(2, BASINS, STEP_ROWS, LANES),
            f32(EDGE, LANES),
        ]
        if first:
            outs += [i32(*table), f32(*table), f32(*table)]
            args = [depth, discharge, reach_state, site, celerity, base_inflow, upstream]
        else:
            args = [state, levels, owner_levels, owner_site, owner_coeff, own]
        args += [got, over, roughness, cell, coeff, slots]
        result = call(functools.partial(step_kernel, first), outs, args)
        state, levels, owner_levels, slots, send, across = result[:6]
        if first:
            owner_site, owner_coeff, own = result[6:9]
        got, over = exchange(send, across)
    copies = call(
        levels_kernel,
        [f32(BASINS, FIELDS, LANES)],
        [levels, owner_levels, owner_site, owner_coeff, got, over, own],
    )[0]
    final = lax.all_to_all(copies, "gy", 0, 0)
    state = call(
        cells_kernel,
        [f32(3, ROWS, COLS)],
        [state, got, over, roughness, cell, coeff, slots],
    )[0]
    return state, final.reshape(BASINS, FIELDS * LANES)


def solution(mesh):
    return jax.shard_map(
        per_device,
        mesh=mesh,
        in_specs=(
            P("gx", "gy"),
            P(None, "gx", "gy"),
            P("gx", "gy"),
            P("gx", None),
            P("gx", None),
            P("gx", None),
            P("gx", None),
            P("gx", "gy"),
            P("gx", "gy"),
            P("gx", "gy"),
        ),
        out_specs=(P(None, "gx", "gy"), P("gx", None)),
        check_vma=False,
    )
```

```python
import functools

import jax
import jax.numpy as jnp
from jax import lax
from jax.experimental import pallas as pl
from jax.experimental.pallas import tpu as pltpu
from jax.sharding import PartitionSpec as P

STEPS = 4


GRAV = 9.81
DT = 0.5
DX = 10.0
NU = 0.1
RATIO = 0.25
FACTOR = DT / (2.0 * DX)

LANES = 128
ROWS = 32
QUADS = 4
COLS = QUADS * LANES
FIELDS = 8
BASINS = 8
SLOT_ROWS = 3 * BASINS
INTERPRET = False

FIRST_EDGE = 24
FIRST_LEVELS = 40
FIRST_SWAP = FIRST_LEVELS + FIELDS * BASINS
OUTLET = 16
EDGE = 24
SWAP = 40


def iota(shape, dim):
    return lax.broadcasted_iota(jnp.int32, shape, dim)


def lane_gather(rows, index):
    return jnp.take_along_axis(rows, index, axis=1, mode="promise_in_bounds")


def lane_to_column(row, count, offset):
    wide = jnp.broadcast_to(row, (count, LANES))
    hit = iota((count, LANES), 1) == iota((count, LANES), 0) + offset
    return jnp.sum(jnp.where(hit, wide, 0.0), axis=1, keepdims=True)


def column_to_lane(column, offset):
    count = column.shape[0]
    wide = jnp.broadcast_to(column, (count, LANES))
    hit = iota((count, LANES), 1) == iota((count, LANES), 0) + offset
    return jnp.sum(jnp.where(hit, wide, 0.0), axis=0, keepdims=True)


def own_row(block, y):
    return jnp.sum(jnp.where(iota(block.shape, 0) == y, block, 0.0), axis=0, keepdims=True)


def flux_terms(cells):
    h, p, q = cells
    inverse = 1.0 / h
    u = p * inverse
    v = q * inverse
    pressure = 0.5 * GRAV * h * h
    return (p, p * u + pressure, q * u), (q, p * v, q * v + pressure), u, v


def flood_update(cells, top, low, left, right, rough, source):
    flux_x, flux_y, u, v = flux_terms(cells)
    top_x = flux_terms(top)[0]
    low_x = flux_terms(low)[0]
    left_y = flux_terms(left)[1]
    right_y = flux_terms(right)[1]
    row = iota((ROWS, COLS), 0)
    col = iota((ROWS, COLS), 1)
    out = []
    for k in range(3):
        quarter = 0.25 * cells[k]
        from_top = jnp.where(
            row == 0, 0.25 * top[k] + FACTOR * top_x[k], pltpu.roll(quarter + FACTOR * flux_x[k], 1, 0)
        )
        from_low = jnp.where(
            row == ROWS - 1,
            0.25 * low[k] - FACTOR * low_x[k],
            pltpu.roll(quarter - FACTOR * flux_x[k], ROWS - 1, 0),
        )
        from_left = jnp.where(
            col == 0, 0.25 * left[k] + FACTOR * left_y[k], pltpu.roll(quarter + FACTOR * flux_y[k], 1, 1)
        )
        from_right = jnp.where(
            col == COLS - 1,
            0.25 * right[k] - FACTOR * right_y[k],
            pltpu.roll(quarter - FACTOR * flux_y[k], COLS - 1, 1),
        )
        out.append((from_top + from_low) + (from_left + from_right))
    h = cells[0]
    size = jnp.abs(h)
    root = jnp.exp(jnp.log(size) * (-1.0 / 3.0))
    root = root * (4.0 - size * (root * root * root)) * (1.0 / 3.0)
    root = jnp.where(h < 0.0, -root, root)
    drag = (GRAV * DT) * rough * rough * jnp.sqrt(u * u + v * v) * root
    return [out[0] + DT * source, out[1] - drag * u, out[2] - drag * v]


def halves(values):
    high = values.astype(jnp.bfloat16).astype(jnp.float32)
    return high, values - high


def spread(rates, major, minor, count):
    total = None
    rows = rates.shape[0]
    group = 4
    high, low = halves(rates)
    for start in range(0, rows, group):
        left, right = [], []
        for r in range(start, start + group):
            at = iota((count, LANES), 0) == major[r : r + 1]
            left.append(
                jnp.concatenate(
                    [
                        jnp.where(at, high[r : r + 1], 0.0),
                        jnp.where(at, low[r : r + 1], 0.0),
                    ],
                    axis=0,
                ).astype(jnp.bfloat16)
            )
            right.append(
                jnp.where(iota((LANES, LANES), 0) == minor[r : r + 1], 1.0, 0.0).astype(jnp.bfloat16)
            )
        part = lax.dot_general(
            jnp.concatenate(left, axis=1),
            jnp.concatenate(right, axis=1),
            (((1,), (1,)), ((), ())),
            preferred_element_type=jnp.float32,
        )
        total = part if total is None else total + part
    return total[:count] + total[count:]


def cell_parts(cell):
    col = cell & (COLS - 1)
    return (col >> 7) * ROWS + (cell >> 9), col & (LANES - 1)


def depth_at_slots(h_ref, index, cell):
    major, minor = cell_parts(cell)
    found = []
    for v in range(3):
        key = major[8 * v : 8 * v + 8]
        lane = minor[8 * v : 8 * v + 8]
        depth = jnp.zeros((8, LANES), jnp.float32)
        for quad in range(QUADS):
            for row in range(ROWS):
                values = h_ref[index + (slice(row, row + 1), slice(quad * LANES, (quad + 1) * LANES))]
                values = jnp.broadcast_to(values, (8, LANES))
                depth = jnp.where(key == quad * ROWS + row, lane_gather(values, lane), depth)
        found.append(depth)
    return jnp.concatenate(found, axis=0)


def level_at_sites(reach_rows, site):
    found = []
    for v in range(3):
        sites = site[8 * v : 8 * v + 8]
        field = sites >> 7
        station = sites & (LANES - 1)
        level = jnp.zeros((8, LANES), jnp.float32)
        for f in range(FIELDS):
            level = jnp.where(field == f, lane_gather(reach_rows(f, v), station), level)
        found.append(level)
    return jnp.concatenate(found, axis=0)


def edge_columns(cells):
    left = column_to_lane(cells[0][:, 0:1], 0)
    right = column_to_lane(cells[0][:, COLS - 1 : COLS], 0)
    for k in (1, 2):
        left = left + column_to_lane(cells[k][:, 0:1], k * ROWS)
        right = right + column_to_lane(cells[k][:, COLS - 1 : COLS], k * ROWS)
    return left, right


def put_edges(beside_ref, across_ref, cells, even, start):
    for k in range(3):
        first = cells[k][0:1]
        last = cells[k][ROWS - 1 : ROWS]
        inner = jnp.where(even, last, first)
        outer = jnp.where(even, first, last)
        for quad in range(QUADS):
            at = start + k * QUADS + quad
            lanes = slice(quad * LANES, (quad + 1) * LANES)
            beside_ref[at : at + 1, :] = inner[:, lanes]
            across_ref[at : at + 1, :] = outer[:, lanes]


def get_edges(got_ref, near_ref, over_ref, cells, spot, start, col_row):
    even, y, is_first, is_last = spot
    before = got_ref[jnp.maximum(y - 1, 0), col_row : col_row + 1, :]
    after = got_ref[jnp.minimum(y + 1, BASINS - 1), col_row : col_row + 1, :]

    def edge(ref, k):
        rows = [ref[start + k * QUADS + q : start + k * QUADS + q + 1, :] for q in range(QUADS)]
        return jnp.concatenate(rows, axis=1)

    top, low, left, right = [], [], [], []
    for k in range(3):
        inner = edge(near_ref, k)
        outer = edge(over_ref, k)
        top.append(jnp.where(is_first, cells[k][0:1], jnp.where(even, outer, inner)))
        low.append(jnp.where(is_last, cells[k][ROWS - 1 : ROWS], jnp.where(even, inner, outer)))
        left.append(jnp.where(y == 0, cells[k][:, 0:1], lane_to_column(before, ROWS, k * ROWS)))
        right.append(
            jnp.where(
                y == BASINS - 1, cells[k][:, COLS - 1 : COLS], lane_to_column(after, ROWS, k * ROWS)
            )
        )
    return top, low, left, right


def inflow_of(own, outlets):
    row = jnp.sum(own[16:24] * outlets, axis=0, keepdims=True)
    return own[8:16, 0:1] + lane_to_column(row, FIELDS, 0)


def river_update(current, inflow, rate, lateral):
    lane = iota((FIELDS, LANES), 1)
    sub = iota((FIELDS, LANES), 0)
    behind = jnp.where(lane == 0, inflow, pltpu.roll(current, 1, 1))
    above = jnp.where(sub == FIELDS - 1, current, pltpu.roll(current, FIELDS - 1, 0))
    below = jnp.where(sub == 0, current, pltpu.roll(current, 1, 0))
    mixing = above - 2.0 * current + below
    return current - rate * (current - behind) + NU * mixing - (DT * RATIO) * lateral


def owned_terms(celerity, base_inflow, upstream, y):
    square = iota((FIELDS, FIELDS), 0) == iota((FIELDS, FIELDS), 1)

    def by_field(ref):
        row = jnp.broadcast_to(own_row(ref[...], y), (FIELDS, FIELDS))
        return jnp.sum(jnp.where(square, row, 0.0), axis=1, keepdims=True)

    feeders = own_row(upstream[...].astype(jnp.float32), y)
    ids = ((lax.axis_index("gx") - 1) * BASINS + iota((BASINS, feeders.shape[1]), 0)).astype(jnp.float32)
    hits = jnp.where(jnp.broadcast_to(feeders, ids.shape) == ids, 1.0, 0.0)
    weight = jnp.sum(hits, axis=1, keepdims=True)
    return jnp.concatenate(
        [jnp.broadcast_to(column, (8, LANES)) for column in (by_field(celerity), by_field(base_inflow), weight)],
        axis=0,
    )


def place():
    gx = lax.axis_index("gx")
    return (gx & 1) == 0, lax.axis_index("gy"), gx == 0, gx == lax.axis_size("gx") - 1


def first_kernel(
    depth,
    discharge,
    cell_in,
    site_in,
    coeff_in,
    reach,
    beside_ref,
    across_ref,
    mine_ref,
    cell_ref,
    site_ref,
    coeff_ref,
    slots_ref,
):
    even = place()[0]

    def arranged(ref):
        low, own, high = ref[0:8], ref[8:16], ref[16:24]
        return jnp.concatenate([own, jnp.where(even, high, low), jnp.where(even, low, high)], axis=0)

    cell = arranged(cell_in)
    site = arranged(site_in)
    coeff = jnp.where(cell >= 0, arranged(coeff_in), 0.0)
    cell = jnp.maximum(cell, 0)
    cell_ref[...] = cell
    site_ref[...] = site
    coeff_ref[...] = coeff
    slots = depth_at_slots(depth, (), cell)
    slots_ref[...] = slots
    for at, value in enumerate((slots, site.astype(jnp.float32), coeff)):
        for v, ref in enumerate((mine_ref, beside_ref, across_ref)):
            ref[8 * at : 8 * at + 8] = value[8 * v : 8 * v + 8]
    cells = [depth[...], discharge[0], discharge[1]]
    mine_ref[24:32] = jnp.zeros((8, LANES), jnp.float32)
    left, right = edge_columns(cells)
    mine_ref[24:25] = left
    mine_ref[25:26] = right
    for ref in (beside_ref, across_ref):
        ref[FIRST_EDGE:FIRST_LEVELS] = jnp.zeros((FIRST_LEVELS - FIRST_EDGE, LANES), jnp.float32)
        for f in range(FIELDS):
            at = FIRST_LEVELS + 8 * f
            ref[at : at + 8] = reach[:, f * LANES : (f + 1) * LANES]
    put_edges(beside_ref, across_ref, cells, even, FIRST_EDGE)


def column_for(mine, b, start):
    y = lax.axis_index("gy")
    left = mine[start : start + 1]
    right = mine[start + 1 : start + 2]
    return jnp.where(b == y - 1, left, jnp.where(b == y + 1, right, 0.0))


def first_pack(mine, near, over, send):
    refs = (mine, near, over)
    for b in range(BASINS):
        for v, ref in enumerate(refs):
            send[b, v : v + 1] = ref[b : b + 1]
            send[b, 3 + v : 4 + v] = ref[16 + b : 17 + b]
            send[b, 8 + 8 * v : 16 + 8 * v] = ref[8:16]
        send[b, 6:7] = column_for(mine, b, 24)
        send[b, 7:8] = jnp.zeros((1, LANES), jnp.float32)


def pack(mine, near, over, send):
    even = place()[0]
    outlet = jnp.where(even, over[OUTLET : OUTLET + 1], near[OUTLET : OUTLET + 1])
    refs = (mine, near, over)
    for b in range(BASINS):
        for v, ref in enumerate(refs):
            send[b, v : v + 1] = ref[b : b + 1]
            send[b, 3 + v : 4 + v] = ref[8 + b : 9 + b]
        send[b, 6:7] = column_for(mine, b, 16)
        send[b, 7:8] = outlet


def last_pack(mine, near, over, send):
    even = place()[0]
    outlet = jnp.where(even, over[OUTLET : OUTLET + 1], near[OUTLET : OUTLET + 1])
    refs = (mine, near, over)
    for b in range(BASINS):
        for v, ref in enumerate(refs):
            send[b, 3 + v : 4 + v] = ref[8 + b : 9 + b]
            send[b, 8 + 8 * v : 16 + 8 * v] = ref[0:8]
            send[b, v : v + 1] = jnp.zeros((1, LANES), jnp.float32)
        send[b, 6:7] = column_for(mine, b, 16)
        send[b, 7:8] = outlet
        send[b, 32:40] = mine[24:32]


def gathered(got, row):
    return jnp.concatenate([got[:, row + v, :] for v in range(3)], axis=0)


def advance_levels(current, outlets, own, site_owner, coeff_owner, segment_owner, slots_owner):
    rates = coeff_owner * (segment_owner - slots_owner)
    lateral = spread(rates, site_owner >> 7, site_owner & (LANES - 1), FIELDS)
    return river_update(current, inflow_of(own, outlets), own[0:8], lateral)


def advance_cells(cells, edges, rough, cell, coeff, segment, slots):
    major, minor = cell_parts(cell)
    rates = coeff * (segment - slots)
    blocks = spread(rates, major, minor, QUADS * ROWS)
    source = jnp.concatenate([blocks[q * ROWS : (q + 1) * ROWS] for q in range(QUADS)], axis=1)
    return flood_update(cells, *edges, rough, source)


def last_kernel(
    state, got, near, over, rough, cell_ref, coeff_ref, slots_ref, got_first, celerity, base_inflow, upstream, state_out, reach_out
):
    cells = [state[0], state[1], state[2]]
    edges = get_edges(got, near, over, cells, place(), EDGE, 6)
    new = advance_cells(
        cells, edges, rough[...], cell_ref[...], coeff_ref[...], gathered(got, 3), slots_ref[...]
    )
    for k in range(3):
        state_out[k] = new[k]
    outlets = got[:, 7, :]
    lane = iota((FIELDS, LANES), 1)
    for b in range(BASINS):
        own = owned_terms(celerity, base_inflow, upstream, b)
        site = jnp.concatenate([got_first[:, 8 + 8 * v + b, :] for v in range(3)], axis=0)
        site = site.astype(jnp.int32)
        held = jnp.concatenate([got[:, 8 + 8 * v + b, :] for v in range(3)], axis=0)
        drawn = spread(held, site >> 7, site & (LANES - 1), FIELDS)
        entering = jnp.where(lane == 0, own[0:8] * inflow_of(own, outlets), 0.0)
        level = got[b, 32:40, :] + entering + (DT * RATIO) * drawn
        for f in range(FIELDS):
            reach_out[b : b + 1, f * LANES : (f + 1) * LANES] = level[f : f + 1]


def step_kernel(first, tail, *refs):
    refs = list(refs)

    def take(n):
        taken = refs[:n]
        del refs[:n]
        return taken

    if first:
        depth, discharge, reach, site_ref, celerity, base_inflow, upstream = take(7)
    else:
        state, levels, owner_levels, owner_site, owner_coeff, own_ref = take(6)
    got, near, over, rough, cell_ref, coeff_ref, slots_ref = take(7)
    state_out, levels_out, owner_levels_out, slots_out, beside_ref, across_ref, mine_ref = take(7)
    if first:
        owner_site_out, owner_coeff_out, own_out = take(3)
    spot = place()
    even, y = spot[0], spot[1]
    cell = cell_ref[...]

    slots_owner = gathered(got, 0)
    if first:
        cells = [depth[...], discharge[0], discharge[1]]
        current = jnp.concatenate(
            [own_row(reach[:, f * LANES : (f + 1) * LANES], y) for f in range(FIELDS)], axis=0
        )

        def tile_rows(f, v):
            if v == 0:
                return reach[:, f * LANES : (f + 1) * LANES]
            return (near if v == 1 else over)[FIRST_LEVELS + 8 * f : FIRST_LEVELS + 8 * f + 8, :]

        segment = level_at_sites(tile_rows, site_ref[...])
        site_owner = jnp.concatenate([got[:, 8 + 8 * v + y, :] for v in range(3)], axis=0)
        site_owner = site_owner.astype(jnp.int32)
        coeff_owner = gathered(got, 3)
        outlets = jnp.zeros((BASINS, LANES), jnp.float32)
        for f in range(FIELDS):
            source_rows = jnp.where(even, tile_rows(f, 2), tile_rows(f, 1))
            outlets = jnp.where(
                iota((BASINS, LANES), 1) == f, source_rows[:, LANES - 1 : LANES], outlets
            )
        segment_owner = level_at_sites(
            lambda f, v: jnp.broadcast_to(current[f : f + 1], (8, LANES)), site_owner
        )
        own = owned_terms(celerity, base_inflow, upstream, y)
        owner_site_out[...] = site_owner
        owner_coeff_out[...] = coeff_owner
        own_out[...] = own
    else:
        cells = [state[0], state[1], state[2]]
        current = levels[...]
        segment = gathered(got, 3)
        site_owner = owner_site[...]
        coeff_owner = owner_coeff[...]
        segment_owner = owner_levels[...]
        outlets = got[:, 7, :]
        own = own_ref[...]

    levels_next = advance_levels(
        current, outlets, own, site_owner, coeff_owner, segment_owner, slots_owner
    )
    edges = get_edges(got, near, over, cells, spot, FIRST_EDGE if first else EDGE, 6)
    new = advance_cells(cells, edges, rough[...], cell, coeff_ref[...], segment, slots_ref[...])
    for k in range(3):
        state_out[k] = new[k]
    levels_out[...] = levels_next
    owned = level_at_sites(
        lambda f, v: jnp.broadcast_to(levels_next[f : f + 1], (8, LANES)), site_owner
    )
    owner_levels_out[...] = owned
    slots = depth_at_slots(state_out, (0,), cell)
    slots_out[...] = slots
    if tail:
        slots = slots * coeff_ref[...]
    blank = jnp.zeros((8, LANES), jnp.float32)
    outlet_row = column_to_lane(levels_next[:, LANES - 1 : LANES], 0)
    for v, ref in enumerate((mine_ref, beside_ref, across_ref)):
        ref[0:8] = slots[8 * v : 8 * v + 8]
        ref[8:16] = owned[8 * v : 8 * v + 8]
        ref[16:24] = blank
        if v > 0:
            ref[OUTLET : OUTLET + 1] = outlet_row
            ref[EDGE : EDGE + 8] = blank
            ref[EDGE + 8 : EDGE + 16] = blank
    left, right = edge_columns(new)
    mine_ref[16:17] = left
    mine_ref[17:18] = right
    put_edges(beside_ref, across_ref, new, even, EDGE)
    if tail:
        total = spread(coeff_owner, site_owner >> 7, site_owner & (LANES - 1), FIELDS)
        none = jnp.zeros((FIELDS, 1), jnp.float32)
        mine_ref[24:32] = river_update(levels_next, none, own[0:8], total * levels_next)
    else:
        mine_ref[24:32] = blank


def call(kernel, outs, args, limit=16 << 20):
    return pl.pallas_call(
        kernel,
        out_shape=outs,
        in_specs=[pl.BlockSpec(memory_space=pltpu.VMEM) for _ in args],
        out_specs=[pl.BlockSpec(memory_space=pltpu.VMEM) for _ in outs],
        compiler_params=None if INTERPRET else pltpu.CompilerParams(vmem_limit_bytes=limit),
        interpret=INTERPRET,
    )(*args)


def f32(*shape):
    return jax.ShapeDtypeStruct(shape, jnp.float32)


def i32(*shape):
    return jax.ShapeDtypeStruct(shape, jnp.int32)


def per_device(
    depth,
    discharge,
    roughness,
    reach_state,
    celerity,
    base_inflow,
    upstream,
    bank_cell,
    bank_site,
    bank_coeff,
):
    count_x = lax.axis_size("gx")
    chip = [(i, i ^ 1) for i in range(count_x)]
    border = [(i, i + 1) for i in range(1, count_x - 1, 2)]
    border = border + [(b, a) for a, b in border]

    def exchange(kernel, rows, beside, across, mine):
        across, beside = lax.optimization_barrier((across, beside))
        near = lax.ppermute(beside, "gx", chip)
        over = lax.ppermute(across, "gx", border)
        over, near = lax.optimization_barrier((over, near))
        send = call(kernel, [f32(BASINS, rows, LANES)], [mine, near, over])[0]
        return lax.all_to_all(send, "gy", 0, 0), near, over

    table = (SLOT_ROWS, LANES)
    beside, across, mine, cell, site, coeff, slots = call(
        first_kernel,
        [
            f32(FIRST_SWAP, LANES),
            f32(FIRST_SWAP, LANES),
            f32(32, LANES),
            i32(*table),
            i32(*table),
            f32(*table),
            f32(*table),
        ],
        [depth, discharge, bank_cell, bank_site, bank_coeff, reach_state],
        limit=60 << 20,
    )
    got, near, over = exchange(first_pack, 32, beside, across, mine)
    got_first = got
    for step in range(STEPS - 1):
        first, tail = step == 0, step == STEPS - 2
        outs = [
            f32(3, ROWS, COLS),
            f32(FIELDS, LANES),
            f32(*table),
            f32(*table),
            f32(SWAP, LANES),
            f32(SWAP, LANES),
            f32(32, LANES),
        ]
        if first:
            outs += [i32(*table), f32(*table), f32(*table)]
            args = [depth, discharge, reach_state, site, celerity, base_inflow, upstream]
        else:
            args = [state, levels, owner_levels, owner_site, owner_coeff, own]
        args += [got, near, over, roughness, cell, coeff, slots]
        result = call(functools.partial(step_kernel, first, tail), outs, args)
        state, levels, owner_levels, slots, beside, across, mine = result[:7]
        if first:
            owner_site, owner_coeff, own = result[7:10]
        got, near, over = exchange(last_pack if tail else pack, 40 if tail else 8, beside, across, mine)
    state, reach = call(
        last_kernel,
        [f32(3, ROWS, COLS), f32(BASINS, FIELDS * LANES)],
        [state, got, near, over, roughness, cell, coeff, slots, got_first, celerity, base_inflow, upstream],
    )
    return state, reach


def solution(mesh):
    return jax.shard_map(
        per_device,
        mesh=mesh,
        in_specs=(
            P("gx", "gy"),
            P(None, "gx", "gy"),
            P("gx", "gy"),
            P("gx", None),
            P("gx", None),
            P("gx", None),
            P("gx", None),
            P("gx", "gy"),
            P("gx", "gy"),
            P("gx", "gy"),
        ),
        out_specs=(P(None, "gx", "gy"), P("gx", None)),
        check_vma=False,
    )
```

```python
import functools

import jax
import jax.numpy as jnp
from jax import lax
from jax.experimental import pallas as pl
from jax.experimental.pallas import tpu as pltpu
from jax.sharding import PartitionSpec as P

STEPS = 4


GRAV = 9.81
DT = 0.5
DX = 10.0
NU = 0.1
RATIO = 0.25
FACTOR = DT / (2.0 * DX)

LANES = 128
ROWS = 32
QUADS = 4
COLS = QUADS * LANES
FIELDS = 8
BASINS = 8
SLOT_ROWS = 3 * BASINS
INTERPRET = False

FIRST_EDGE = 24
FIRST_LEVELS = 40
FIRST_SWAP = FIRST_LEVELS + FIELDS * BASINS
OUTLET = 16
EDGE = 24
SWAP = 40


def iota(shape, dim):
    return lax.broadcasted_iota(jnp.int32, shape, dim)


def lane_gather(rows, index):
    return jnp.take_along_axis(rows, index, axis=1, mode="promise_in_bounds")


def lane_to_column(row, count, offset):
    wide = jnp.broadcast_to(row, (count, LANES))
    hit = iota((count, LANES), 1) == iota((count, LANES), 0) + offset
    return jnp.sum(jnp.where(hit, wide, 0.0), axis=1, keepdims=True)


def column_to_lane(column, offset):
    count = column.shape[0]
    wide = jnp.broadcast_to(column, (count, LANES))
    hit = iota((count, LANES), 1) == iota((count, LANES), 0) + offset
    return jnp.sum(jnp.where(hit, wide, 0.0), axis=0, keepdims=True)


def own_row(block, y):
    return jnp.sum(jnp.where(iota(block.shape, 0) == y, block, 0.0), axis=0, keepdims=True)


def flux_terms(cells):
    h, p, q = cells
    inverse = 1.0 / h
    u = p * inverse
    v = q * inverse
    pressure = 0.5 * GRAV * h * h
    return (p, p * u + pressure, q * u), (q, p * v, q * v + pressure), u, v


def flood_base(cells, rough):
    flux_x, flux_y, u, v = flux_terms(cells)
    row = iota((ROWS, COLS), 0)
    col = iota((ROWS, COLS), 1)
    out = []
    for k in range(3):
        quarter = 0.25 * cells[k]
        from_top = jnp.where(row == 0, 0.0, pltpu.roll(quarter + FACTOR * flux_x[k], 1, 0))
        from_low = jnp.where(row == ROWS - 1, 0.0, pltpu.roll(quarter - FACTOR * flux_x[k], ROWS - 1, 0))
        from_left = jnp.where(col == 0, 0.0, pltpu.roll(quarter + FACTOR * flux_y[k], 1, 1))
        from_right = jnp.where(col == COLS - 1, 0.0, pltpu.roll(quarter - FACTOR * flux_y[k], COLS - 1, 1))
        out.append((from_top + from_low) + (from_left + from_right))
    h = cells[0]
    size = jnp.abs(h)
    root = jnp.exp(jnp.log(size) * (-1.0 / 3.0))
    root = root * (4.0 - size * (root * root * root)) * (1.0 / 3.0)
    root = jnp.where(h < 0.0, -root, root)
    drag = (GRAV * DT) * rough * rough * jnp.sqrt(u * u + v * v) * root
    return [out[0], out[1] - drag * u, out[2] - drag * v]


def flood_finish(base, edges, source):
    top, low, left, right = edges
    top_x = flux_terms(top)[0]
    low_x = flux_terms(low)[0]
    left_y = flux_terms(left)[1]
    right_y = flux_terms(right)[1]
    first_row = iota((8, COLS), 0) == 0
    last_row = iota((8, COLS), 0) == 7
    first_col = iota((ROWS, LANES), 1) == 0
    last_col = iota((ROWS, LANES), 1) == LANES - 1
    out = []
    for k in range(3):
        cells = base[k]
        upper = cells[0:8] + jnp.where(first_row, 0.25 * top[k] + FACTOR * top_x[k], 0.0)
        lower = cells[ROWS - 8 : ROWS] + jnp.where(last_row, 0.25 * low[k] - FACTOR * low_x[k], 0.0)
        cells = jnp.concatenate([upper, cells[8 : ROWS - 8], lower], axis=0)
        west = cells[:, :LANES] + jnp.where(first_col, 0.25 * left[k] + FACTOR * left_y[k], 0.0)
        east = cells[:, COLS - LANES :] + jnp.where(last_col, 0.25 * right[k] - FACTOR * right_y[k], 0.0)
        out.append(jnp.concatenate([west, cells[:, LANES : COLS - LANES], east], axis=1))
    out[0] = out[0] + DT * source
    return out


def halves(values):
    high = values.astype(jnp.bfloat16).astype(jnp.float32)
    return high, values - high


def spread(rates, major, minor, count):
    total = None
    rows = rates.shape[0]
    group = 4
    high, low = halves(rates)
    for start in range(0, rows, group):
        left, right = [], []
        for r in range(start, start + group):
            at = iota((count, LANES), 0) == major[r : r + 1]
            left.append(
                jnp.concatenate(
                    [
                        jnp.where(at, high[r : r + 1], 0.0),
                        jnp.where(at, low[r : r + 1], 0.0),
                    ],
                    axis=0,
                ).astype(jnp.bfloat16)
            )
            right.append(
                jnp.where(iota((LANES, LANES), 0) == minor[r : r + 1], 1.0, 0.0).astype(jnp.bfloat16)
            )
        part = lax.dot_general(
            jnp.concatenate(left, axis=1),
            jnp.concatenate(right, axis=1),
            (((1,), (1,)), ((), ())),
            preferred_element_type=jnp.float32,
        )
        total = part if total is None else total + part
    return total[:count] + total[count:]


def cell_parts(cell):
    col = cell & (COLS - 1)
    return (col >> 7) * ROWS + (cell >> 9), col & (LANES - 1)


def depth_at_slots(h_ref, index, cell):
    major, minor = cell_parts(cell)
    found = []
    for v in range(3):
        key = major[8 * v : 8 * v + 8]
        lane = minor[8 * v : 8 * v + 8]
        depth = jnp.zeros((8, LANES), jnp.float32)
        for quad in range(QUADS):
            for row in range(ROWS):
                values = h_ref[index + (slice(row, row + 1), slice(quad * LANES, (quad + 1) * LANES))]
                values = jnp.broadcast_to(values, (8, LANES))
                depth = jnp.where(key == quad * ROWS + row, lane_gather(values, lane), depth)
        found.append(depth)
    return jnp.concatenate(found, axis=0)


def level_at_sites(reach_rows, site):
    found = []
    for v in range(3):
        sites = site[8 * v : 8 * v + 8]
        field = sites >> 7
        station = sites & (LANES - 1)
        level = jnp.zeros((8, LANES), jnp.float32)
        for f in range(FIELDS):
            level = jnp.where(field == f, lane_gather(reach_rows(f, v), station), level)
        found.append(level)
    return jnp.concatenate(found, axis=0)


def edge_columns(cells):
    left = column_to_lane(cells[0][:, 0:1], 0)
    right = column_to_lane(cells[0][:, COLS - 1 : COLS], 0)
    for k in (1, 2):
        left = left + column_to_lane(cells[k][:, 0:1], k * ROWS)
        right = right + column_to_lane(cells[k][:, COLS - 1 : COLS], k * ROWS)
    return left, right


def put_edges(beside_ref, across_ref, cells, even, start):
    for k in range(3):
        first = cells[k][0:1]
        last = cells[k][ROWS - 1 : ROWS]
        inner = jnp.where(even, last, first)
        outer = jnp.where(even, first, last)
        for quad in range(QUADS):
            at = start + k * QUADS + quad
            lanes = slice(quad * LANES, (quad + 1) * LANES)
            beside_ref[at : at + 1, :] = inner[:, lanes]
            across_ref[at : at + 1, :] = outer[:, lanes]


def get_edges(got_ref, near_ref, over_ref, cells, spot, start, col_row):
    even, y, is_first, is_last = spot
    before = got_ref[jnp.maximum(y - 1, 0), col_row : col_row + 1, :]
    after = got_ref[jnp.minimum(y + 1, BASINS - 1), col_row : col_row + 1, :]

    def edge(ref, k):
        rows = [ref[start + k * QUADS + q : start + k * QUADS + q + 1, :] for q in range(QUADS)]
        return jnp.concatenate(rows, axis=1)

    top, low, left, right = [], [], [], []
    for k in range(3):
        inner = edge(near_ref, k)
        outer = edge(over_ref, k)
        top.append(jnp.where(is_first, cells[k][0:1], jnp.where(even, outer, inner)))
        low.append(jnp.where(is_last, cells[k][ROWS - 1 : ROWS], jnp.where(even, inner, outer)))
        left.append(jnp.where(y == 0, cells[k][:, 0:1], lane_to_column(before, ROWS, k * ROWS)))
        right.append(
            jnp.where(
                y == BASINS - 1, cells[k][:, COLS - 1 : COLS], lane_to_column(after, ROWS, k * ROWS)
            )
        )
    return top, low, left, right


def inflow_of(own, outlets):
    row = jnp.sum(own[16:24] * outlets, axis=0, keepdims=True)
    return own[8:16, 0:1] + lane_to_column(row, FIELDS, 0)


def river_update(current, inflow, rate, lateral):
    lane = iota((FIELDS, LANES), 1)
    sub = iota((FIELDS, LANES), 0)
    behind = jnp.where(lane == 0, inflow, pltpu.roll(current, 1, 1))
    above = jnp.where(sub == FIELDS - 1, current, pltpu.roll(current, FIELDS - 1, 0))
    below = jnp.where(sub == 0, current, pltpu.roll(current, 1, 0))
    mixing = above - 2.0 * current + below
    return current - rate * (current - behind) + NU * mixing - (DT * RATIO) * lateral


def owned_terms(celerity, base_inflow, upstream, y):
    square = iota((FIELDS, FIELDS), 0) == iota((FIELDS, FIELDS), 1)

    def by_field(ref):
        row = jnp.broadcast_to(own_row(ref[...], y), (FIELDS, FIELDS))
        return jnp.sum(jnp.where(square, row, 0.0), axis=1, keepdims=True)

    feeders = own_row(upstream[...].astype(jnp.float32), y)
    ids = ((lax.axis_index("gx") - 1) * BASINS + iota((BASINS, feeders.shape[1]), 0)).astype(jnp.float32)
    hits = jnp.where(jnp.broadcast_to(feeders, ids.shape) == ids, 1.0, 0.0)
    weight = jnp.sum(hits, axis=1, keepdims=True)
    return jnp.concatenate(
        [jnp.broadcast_to(column, (8, LANES)) for column in (by_field(celerity), by_field(base_inflow), weight)],
        axis=0,
    )


def place():
    gx = lax.axis_index("gx")
    return (gx & 1) == 0, lax.axis_index("gy"), gx == 0, gx == lax.axis_size("gx") - 1


def first_kernel(*refs):
    count = len(refs) - 1
    sources, held, arrived = refs[:6], refs[count - 6 : count], refs[count]
    copies = [
        pltpu.make_async_copy(source, target, arrived.at[i])
        for i, (source, target) in enumerate(zip(sources, held))
    ]
    for copy in copies:
        copy.start()
    for copy in copies:
        copy.wait()
    first_body(*held, *refs[6 : count - 6])


def first_body(
    depth,
    discharge,
    cell_in,
    site_in,
    coeff_in,
    reach,
    beside_ref,
    across_ref,
    mine_ref,
    cell_ref,
    site_ref,
    coeff_ref,
    slots_ref,
):
    even = place()[0]

    def arranged(ref):
        low, own, high = ref[0:8], ref[8:16], ref[16:24]
        return jnp.concatenate([own, jnp.where(even, high, low), jnp.where(even, low, high)], axis=0)

    cell = arranged(cell_in)
    site = arranged(site_in)
    coeff = jnp.where(cell >= 0, arranged(coeff_in), 0.0)
    cell = jnp.maximum(cell, 0)
    cell_ref[...] = cell
    site_ref[...] = site
    coeff_ref[...] = coeff
    slots = depth_at_slots(depth, (), cell)
    slots_ref[...] = slots
    for at, value in enumerate((slots, site.astype(jnp.float32), coeff)):
        for v, ref in enumerate((mine_ref, beside_ref, across_ref)):
            ref[8 * at : 8 * at + 8] = value[8 * v : 8 * v + 8]
    cells = [depth[...], discharge[0], discharge[1]]
    mine_ref[24:32] = jnp.zeros((8, LANES), jnp.float32)
    left, right = edge_columns(cells)
    mine_ref[24:25] = left
    mine_ref[25:26] = right
    for ref in (beside_ref, across_ref):
        ref[FIRST_EDGE:FIRST_LEVELS] = jnp.zeros((FIRST_LEVELS - FIRST_EDGE, LANES), jnp.float32)
        for f in range(FIELDS):
            at = FIRST_LEVELS + 8 * f
            ref[at : at + 8] = reach[:, f * LANES : (f + 1) * LANES]
    put_edges(beside_ref, across_ref, cells, even, FIRST_EDGE)


def column_for(mine, b, start):
    y = lax.axis_index("gy")
    left = mine[start : start + 1]
    right = mine[start + 1 : start + 2]
    return jnp.where(b == y - 1, left, jnp.where(b == y + 1, right, 0.0))


def first_pack(mine, near, over, send):
    refs = (mine, near, over)
    for b in range(BASINS):
        for v, ref in enumerate(refs):
            send[b, v : v + 1] = ref[b : b + 1]
            send[b, 3 + v : 4 + v] = ref[16 + b : 17 + b]
            send[b, 8 + 8 * v : 16 + 8 * v] = ref[8:16]
        send[b, 6:7] = column_for(mine, b, 24)
        send[b, 7:8] = jnp.zeros((1, LANES), jnp.float32)


def pack(mine, near, over, send):
    even = place()[0]
    outlet = jnp.where(even, over[OUTLET : OUTLET + 1], near[OUTLET : OUTLET + 1])
    refs = (mine, near, over)
    for b in range(BASINS):
        for v, ref in enumerate(refs):
            send[b, v : v + 1] = ref[b : b + 1]
            send[b, 3 + v : 4 + v] = ref[8 + b : 9 + b]
        send[b, 6:7] = column_for(mine, b, 16)
        send[b, 7:8] = outlet


def last_pack(mine, near, over, send):
    even = place()[0]
    outlet = jnp.where(even, over[OUTLET : OUTLET + 1], near[OUTLET : OUTLET + 1])
    refs = (mine, near, over)
    for b in range(BASINS):
        for v, ref in enumerate(refs):
            send[b, 3 + v : 4 + v] = ref[8 + b : 9 + b]
            send[b, 8 + 8 * v : 16 + 8 * v] = ref[0:8]
            send[b, v : v + 1] = jnp.zeros((1, LANES), jnp.float32)
        send[b, 6:7] = column_for(mine, b, 16)
        send[b, 7:8] = outlet
        send[b, 32:40] = mine[24:32]


def gathered(got, row):
    return jnp.concatenate([got[:, row + v, :] for v in range(3)], axis=0)


def advance_levels(current, outlets, own, site_owner, coeff_owner, segment_owner, slots_owner):
    rates = coeff_owner * (segment_owner - slots_owner)
    lateral = spread(rates, site_owner >> 7, site_owner & (LANES - 1), FIELDS)
    return river_update(current, inflow_of(own, outlets), own[0:8], lateral)


def advance_cells(base, edges, cell, coeff, segment, slots):
    major, minor = cell_parts(cell)
    rates = coeff * (segment - slots)
    blocks = spread(rates, major, minor, QUADS * ROWS)
    source = jnp.concatenate([blocks[q * ROWS : (q + 1) * ROWS] for q in range(QUADS)], axis=1)
    return flood_finish([base[0], base[1], base[2]], edges, source)


def first_flow(depth, discharge, rough, base):
    new = flood_base([depth[...], discharge[0], discharge[1]], rough[...])
    for k in range(3):
        base[k] = new[k]


def flow(state, rough, base):
    new = flood_base([state[0], state[1], state[2]], rough[...])
    for k in range(3):
        base[k] = new[k]


def flow_and_total(state, rough, owner_coeff, owner_site, base, total):
    flow(state, rough, base)
    site = owner_site[...]
    total[...] = spread(owner_coeff[...], site >> 7, site & (LANES - 1), FIELDS)


def last_kernel(
    state, got, near, over, base, cell_ref, coeff_ref, slots_ref, got_first, celerity, base_inflow, upstream, state_out, reach_out
):
    cells = [state[0], state[1], state[2]]
    edges = get_edges(got, near, over, cells, place(), EDGE, 6)
    new = advance_cells(
        base, edges, cell_ref[...], coeff_ref[...], gathered(got, 3), slots_ref[...]
    )
    for k in range(3):
        state_out[k] = new[k]
    outlets = got[:, 7, :]
    lane = iota((FIELDS, LANES), 1)
    for b in range(BASINS):
        own = owned_terms(celerity, base_inflow, upstream, b)
        site = jnp.concatenate([got_first[:, 8 + 8 * v + b, :] for v in range(3)], axis=0)
        site = site.astype(jnp.int32)
        held = jnp.concatenate([got[:, 8 + 8 * v + b, :] for v in range(3)], axis=0)
        drawn = spread(held, site >> 7, site & (LANES - 1), FIELDS)
        entering = jnp.where(lane == 0, own[0:8] * inflow_of(own, outlets), 0.0)
        level = got[b, 32:40, :] + entering + (DT * RATIO) * drawn
        for f in range(FIELDS):
            reach_out[b : b + 1, f * LANES : (f + 1) * LANES] = level[f : f + 1]


def step_kernel(first, tail, *refs):
    refs = list(refs)

    def take(n):
        taken = refs[:n]
        del refs[:n]
        return taken

    if first:
        depth, discharge, reach, site_ref, celerity, base_inflow, upstream = take(7)
    else:
        state, levels, owner_levels, owner_site, owner_coeff, own_ref = take(6)
    got, near, over, base, cell_ref, coeff_ref, slots_ref = take(7)
    if tail:
        (total,) = take(1)
    state_out, levels_out, owner_levels_out, slots_out, beside_ref, across_ref, mine_ref = take(7)
    if first:
        owner_site_out, owner_coeff_out, own_out = take(3)
    spot = place()
    even, y = spot[0], spot[1]
    cell = cell_ref[...]

    slots_owner = gathered(got, 0)
    if first:
        cells = [depth[...], discharge[0], discharge[1]]
        current = jnp.concatenate(
            [own_row(reach[:, f * LANES : (f + 1) * LANES], y) for f in range(FIELDS)], axis=0
        )

        def tile_rows(f, v):
            if v == 0:
                return reach[:, f * LANES : (f + 1) * LANES]
            return (near if v == 1 else over)[FIRST_LEVELS + 8 * f : FIRST_LEVELS + 8 * f + 8, :]

        segment = level_at_sites(tile_rows, site_ref[...])
        site_owner = jnp.concatenate([got[:, 8 + 8 * v + y, :] for v in range(3)], axis=0)
        site_owner = site_owner.astype(jnp.int32)
        coeff_owner = gathered(got, 3)
        outlets = jnp.zeros((BASINS, LANES), jnp.float32)
        for f in range(FIELDS):
            source_rows = jnp.where(even, tile_rows(f, 2), tile_rows(f, 1))
            outlets = jnp.where(
                iota((BASINS, LANES), 1) == f, source_rows[:, LANES - 1 : LANES], outlets
            )
        segment_owner = level_at_sites(
            lambda f, v: jnp.broadcast_to(current[f : f + 1], (8, LANES)), site_owner
        )
        own = owned_terms(celerity, base_inflow, upstream, y)
        owner_site_out[...] = site_owner
        owner_coeff_out[...] = coeff_owner
        own_out[...] = own
    else:
        cells = [state[0], state[1], state[2]]
        current = levels[...]
        segment = gathered(got, 3)
        site_owner = owner_site[...]
        coeff_owner = owner_coeff[...]
        segment_owner = owner_levels[...]
        outlets = got[:, 7, :]
        own = own_ref[...]

    levels_next = advance_levels(
        current, outlets, own, site_owner, coeff_owner, segment_owner, slots_owner
    )
    edges = get_edges(got, near, over, cells, spot, FIRST_EDGE if first else EDGE, 6)
    new = advance_cells(base, edges, cell, coeff_ref[...], segment, slots_ref[...])
    for k in range(3):
        state_out[k] = new[k]
    levels_out[...] = levels_next
    owned = level_at_sites(
        lambda f, v: jnp.broadcast_to(levels_next[f : f + 1], (8, LANES)), site_owner
    )
    owner_levels_out[...] = owned
    slots = depth_at_slots(state_out, (0,), cell)
    slots_out[...] = slots
    if tail:
        slots = slots * coeff_ref[...]
    blank = jnp.zeros((8, LANES), jnp.float32)
    outlet_row = column_to_lane(levels_next[:, LANES - 1 : LANES], 0)
    for v, ref in enumerate((mine_ref, beside_ref, across_ref)):
        ref[0:8] = slots[8 * v : 8 * v + 8]
        ref[8:16] = owned[8 * v : 8 * v + 8]
        ref[16:24] = blank
        if v > 0:
            ref[OUTLET : OUTLET + 1] = outlet_row
            ref[EDGE : EDGE + 8] = blank
            ref[EDGE + 8 : EDGE + 16] = blank
    left, right = edge_columns(new)
    mine_ref[16:17] = left
    mine_ref[17:18] = right
    put_edges(beside_ref, across_ref, new, even, EDGE)
    if tail:
        none = jnp.zeros((FIELDS, 1), jnp.float32)
        mine_ref[24:32] = river_update(levels_next, none, own[0:8], total[...] * levels_next)
    else:
        mine_ref[24:32] = blank


def call(kernel, outs, args, limit=16 << 20):
    return pl.pallas_call(
        kernel,
        out_shape=outs,
        in_specs=[pl.BlockSpec(memory_space=pltpu.VMEM) for _ in args],
        out_specs=[pl.BlockSpec(memory_space=pltpu.VMEM) for _ in outs],
        compiler_params=None if INTERPRET else pltpu.CompilerParams(vmem_limit_bytes=limit),
        interpret=INTERPRET,
    )(*args)


def f32(*shape):
    return jax.ShapeDtypeStruct(shape, jnp.float32)


def i32(*shape):
    return jax.ShapeDtypeStruct(shape, jnp.int32)


def per_device(
    depth,
    discharge,
    roughness,
    reach_state,
    celerity,
    base_inflow,
    upstream,
    bank_cell,
    bank_site,
    bank_coeff,
):
    count_x = lax.axis_size("gx")
    chip = [(i, i ^ 1) for i in range(count_x)]
    border = [(i, i + 1) for i in range(1, count_x - 1, 2)]
    border = border + [(b, a) for a, b in border]

    def exchange(kernel, rows, beside, across, mine, base=None):
        across, beside = lax.optimization_barrier((across, beside))
        near = lax.ppermute(beside, "gx", chip)
        over = lax.ppermute(across, "gx", border)
        over, near = lax.optimization_barrier((over, near))
        send = call(kernel, [f32(BASINS, rows, LANES)], [mine, near, over])[0]
        if base is not None:
            send, base = lax.optimization_barrier((send, base))
        return lax.all_to_all(send, "gy", 0, 0), near, over, base

    table = (SLOT_ROWS, LANES)
    outs = [
        f32(FIRST_SWAP, LANES),
        f32(FIRST_SWAP, LANES),
        f32(32, LANES),
        i32(*table),
        i32(*table),
        f32(*table),
        f32(*table),
    ]
    inputs = [depth, discharge, bank_cell, bank_site, bank_coeff, reach_state]
    inputs = [pltpu.with_memory_space_constraint(x, pltpu.HBM) for x in inputs]
    beside, across, mine, cell, site, coeff, slots = pl.pallas_call(
        first_kernel,
        out_shape=outs,
        in_specs=[pl.BlockSpec(memory_space=pltpu.HBM) for _ in inputs],
        out_specs=[pl.BlockSpec(memory_space=pltpu.VMEM) for _ in outs],
        scratch_shapes=[pltpu.VMEM(x.shape, x.dtype) for x in inputs]
        + [pltpu.SemaphoreType.DMA((len(inputs),))],
        compiler_params=None if INTERPRET else pltpu.CompilerParams(vmem_limit_bytes=16 << 20),
        interpret=pltpu.InterpretParams() if INTERPRET else False,
    )(*inputs)
    got, near, over, _ = exchange(first_pack, 32, beside, across, mine)
    got_first = got
    base = call(first_flow, [f32(3, ROWS, COLS)], [depth, discharge, roughness])[0]
    for step in range(STEPS - 1):
        first, tail = step == 0, step == STEPS - 2
        outs = [
            f32(3, ROWS, COLS),
            f32(FIELDS, LANES),
            f32(*table),
            f32(*table),
            f32(SWAP, LANES),
            f32(SWAP, LANES),
            f32(32, LANES),
        ]
        if first:
            outs += [i32(*table), f32(*table), f32(*table)]
            args = [depth, discharge, reach_state, site, celerity, base_inflow, upstream]
        else:
            args = [state, levels, owner_levels, owner_site, owner_coeff, own]
        args += [got, near, over, base, cell, coeff, slots]
        if tail:
            args += [total]
        result = call(functools.partial(step_kernel, first, tail), outs, args)
        state, levels, owner_levels, slots, beside, across, mine = result[:7]
        if first:
            owner_site, owner_coeff, own = result[7:10]
        if first:
            base, total = call(
                flow_and_total,
                [f32(3, ROWS, COLS), f32(FIELDS, LANES)],
                [state, roughness, owner_coeff, owner_site],
            )
        else:
            base = call(flow, [f32(3, ROWS, COLS)], [state, roughness])[0]
        got, near, over, base = exchange(
            last_pack if tail else pack, 40 if tail else BASINS, beside, across, mine, base
        )
    state, reach = call(
        last_kernel,
        [f32(3, ROWS, COLS), f32(BASINS, FIELDS * LANES)],
        [state, got, near, over, base, cell, coeff, slots, got_first, celerity, base_inflow, upstream],
    )
    return state, reach


def solution(mesh):
    return jax.shard_map(
        per_device,
        mesh=mesh,
        in_specs=(
            P("gx", "gy"),
            P(None, "gx", "gy"),
            P("gx", "gy"),
            P("gx", None),
            P("gx", None),
            P("gx", None),
            P("gx", None),
            P("gx", "gy"),
            P("gx", "gy"),
            P("gx", "gy"),
        ),
        out_specs=(P(None, "gx", "gy"), P("gx", None)),
        check_vma=False,
    )
```

```python
import functools

import jax
import jax.numpy as jnp
from jax import lax
from jax.experimental import pallas as pl
from jax.experimental.pallas import tpu as pltpu
from jax.sharding import PartitionSpec as P

STEPS = 4


GRAV = 9.81
DT = 0.5
DX = 10.0
NU = 0.1
RATIO = 0.25
FACTOR = DT / (2.0 * DX)

LANES = 128
ROWS = 32
QUADS = 4
COLS = QUADS * LANES
FIELDS = 8
BASINS = 8
SLOT_ROWS = 3 * BASINS
INTERPRET = False

FIRST_EDGE = 24
FIRST_LEVELS = 40
FIRST_SWAP = FIRST_LEVELS + FIELDS * BASINS
OUTLET = 16
EDGE = 24
SWAP = 40


def iota(shape, dim):
    return lax.broadcasted_iota(jnp.int32, shape, dim)


def lane_gather(rows, index):
    return jnp.take_along_axis(rows, index, axis=1, mode="promise_in_bounds")


def lane_to_column(row, count, offset):
    wide = jnp.broadcast_to(row, (count, LANES))
    hit = iota((count, LANES), 1) == iota((count, LANES), 0) + offset
    return jnp.sum(jnp.where(hit, wide, 0.0), axis=1, keepdims=True)


def column_to_lane(column, offset):
    count = column.shape[0]
    wide = jnp.broadcast_to(column, (count, LANES))
    hit = iota((count, LANES), 1) == iota((count, LANES), 0) + offset
    return jnp.sum(jnp.where(hit, wide, 0.0), axis=0, keepdims=True)


def own_row(block, y):
    return jnp.sum(jnp.where(iota(block.shape, 0) == y, block, 0.0), axis=0, keepdims=True)


def flux_terms(cells):
    h, p, q = cells
    inverse = 1.0 / h
    u = p * inverse
    v = q * inverse
    pressure = 0.5 * GRAV * h * h
    return (p, p * u + pressure, q * u), (q, p * v, q * v + pressure), u, v


def flood_base(cells, rough):
    flux_x, flux_y, u, v = flux_terms(cells)
    row = iota((ROWS, COLS), 0)
    col = iota((ROWS, COLS), 1)
    out = []
    for k in range(3):
        quarter = 0.25 * cells[k]
        from_top = jnp.where(row == 0, 0.0, pltpu.roll(quarter + FACTOR * flux_x[k], 1, 0))
        from_low = jnp.where(row == ROWS - 1, 0.0, pltpu.roll(quarter - FACTOR * flux_x[k], ROWS - 1, 0))
        from_left = jnp.where(col == 0, 0.0, pltpu.roll(quarter + FACTOR * flux_y[k], 1, 1))
        from_right = jnp.where(col == COLS - 1, 0.0, pltpu.roll(quarter - FACTOR * flux_y[k], COLS - 1, 1))
        out.append((from_top + from_low) + (from_left + from_right))
    h = cells[0]
    size = jnp.abs(h)
    root = jnp.exp(jnp.log(size) * (-1.0 / 3.0))
    root = root * (4.0 - size * (root * root * root)) * (1.0 / 3.0)
    root = jnp.where(h < 0.0, -root, root)
    drag = (GRAV * DT) * rough * rough * jnp.sqrt(u * u + v * v) * root
    return [out[0], out[1] - drag * u, out[2] - drag * v]


def flood_finish(base, edges, source):
    top, low, left, right = edges
    top_x = flux_terms(top)[0]
    low_x = flux_terms(low)[0]
    left_y = flux_terms(left)[1]
    right_y = flux_terms(right)[1]
    first_row = iota((8, COLS), 0) == 0
    last_row = iota((8, COLS), 0) == 7
    first_col = iota((ROWS, LANES), 1) == 0
    last_col = iota((ROWS, LANES), 1) == LANES - 1
    out = []
    for k in range(3):
        cells = base[k]
        upper = cells[0:8] + jnp.where(first_row, 0.25 * top[k] + FACTOR * top_x[k], 0.0)
        lower = cells[ROWS - 8 : ROWS] + jnp.where(last_row, 0.25 * low[k] - FACTOR * low_x[k], 0.0)
        cells = jnp.concatenate([upper, cells[8 : ROWS - 8], lower], axis=0)
        west = cells[:, :LANES] + jnp.where(first_col, 0.25 * left[k] + FACTOR * left_y[k], 0.0)
        east = cells[:, COLS - LANES :] + jnp.where(last_col, 0.25 * right[k] - FACTOR * right_y[k], 0.0)
        out.append(jnp.concatenate([west, cells[:, LANES : COLS - LANES], east], axis=1))
    out[0] = out[0] + DT * source
    return out


def halves(values):
    high = values.astype(jnp.bfloat16).astype(jnp.float32)
    return high, values - high


def spread(rates, major, minor, count):
    total = None
    rows = rates.shape[0]
    group = 4
    high, low = halves(rates)
    for start in range(0, rows, group):
        left, right = [], []
        for r in range(start, start + group):
            at = iota((count, LANES), 0) == major[r : r + 1]
            left.append(
                jnp.concatenate(
                    [
                        jnp.where(at, high[r : r + 1], 0.0),
                        jnp.where(at, low[r : r + 1], 0.0),
                    ],
                    axis=0,
                ).astype(jnp.bfloat16)
            )
            right.append(
                jnp.where(iota((LANES, LANES), 0) == minor[r : r + 1], 1.0, 0.0).astype(jnp.bfloat16)
            )
        part = lax.dot_general(
            jnp.concatenate(left, axis=1),
            jnp.concatenate(right, axis=1),
            (((1,), (1,)), ((), ())),
            preferred_element_type=jnp.float32,
        )
        total = part if total is None else total + part
    return total[:count] + total[count:]


def cell_parts(cell):
    col = cell & (COLS - 1)
    return (col >> 7) * ROWS + (cell >> 9), col & (LANES - 1)


def depth_at_slots(h_ref, index, cell):
    major, minor = cell_parts(cell)
    found = []
    for v in range(3):
        key = major[8 * v : 8 * v + 8]
        lane = minor[8 * v : 8 * v + 8]
        depth = jnp.zeros((8, LANES), jnp.float32)
        for quad in range(QUADS):
            for row in range(ROWS):
                values = h_ref[index + (slice(row, row + 1), slice(quad * LANES, (quad + 1) * LANES))]
                values = jnp.broadcast_to(values, (8, LANES))
                depth = jnp.where(key == quad * ROWS + row, lane_gather(values, lane), depth)
        found.append(depth)
    return jnp.concatenate(found, axis=0)


def level_at_sites(reach_rows, site):
    found = []
    for v in range(3):
        sites = site[8 * v : 8 * v + 8]
        field = sites >> 7
        station = sites & (LANES - 1)
        level = jnp.zeros((8, LANES), jnp.float32)
        for f in range(FIELDS):
            level = jnp.where(field == f, lane_gather(reach_rows(f, v), station), level)
        found.append(level)
    return jnp.concatenate(found, axis=0)


def edge_columns(cells):
    left = column_to_lane(cells[0][:, 0:1], 0)
    right = column_to_lane(cells[0][:, COLS - 1 : COLS], 0)
    for k in (1, 2):
        left = left + column_to_lane(cells[k][:, 0:1], k * ROWS)
        right = right + column_to_lane(cells[k][:, COLS - 1 : COLS], k * ROWS)
    return left, right


def put_edges(beside_ref, across_ref, cells, even, start):
    for k in range(3):
        first = cells[k][0:1]
        last = cells[k][ROWS - 1 : ROWS]
        inner = jnp.where(even, last, first)
        outer = jnp.where(even, first, last)
        for quad in range(QUADS):
            at = start + k * QUADS + quad
            lanes = slice(quad * LANES, (quad + 1) * LANES)
            beside_ref[at : at + 1, :] = inner[:, lanes]
            across_ref[at : at + 1, :] = outer[:, lanes]


def get_edges(got_ref, near_ref, over_ref, cells, spot, start, col_row):
    even, y, is_first, is_last = spot
    before = got_ref[jnp.maximum(y - 1, 0), col_row : col_row + 1, :]
    after = got_ref[jnp.minimum(y + 1, BASINS - 1), col_row : col_row + 1, :]

    def edge(ref, k):
        rows = [ref[start + k * QUADS + q : start + k * QUADS + q + 1, :] for q in range(QUADS)]
        return jnp.concatenate(rows, axis=1)

    top, low, left, right = [], [], [], []
    for k in range(3):
        inner = edge(near_ref, k)
        outer = edge(over_ref, k)
        top.append(jnp.where(is_first, cells[k][0:1], jnp.where(even, outer, inner)))
        low.append(jnp.where(is_last, cells[k][ROWS - 1 : ROWS], jnp.where(even, inner, outer)))
        left.append(jnp.where(y == 0, cells[k][:, 0:1], lane_to_column(before, ROWS, k * ROWS)))
        right.append(
            jnp.where(
                y == BASINS - 1, cells[k][:, COLS - 1 : COLS], lane_to_column(after, ROWS, k * ROWS)
            )
        )
    return top, low, left, right


def inflow_of(own, outlets):
    row = jnp.sum(own[16:24] * outlets, axis=0, keepdims=True)
    return own[8:16, 0:1] + lane_to_column(row, FIELDS, 0)


def river_update(current, inflow, rate, lateral):
    lane = iota((FIELDS, LANES), 1)
    sub = iota((FIELDS, LANES), 0)
    behind = jnp.where(lane == 0, inflow, pltpu.roll(current, 1, 1))
    above = jnp.where(sub == FIELDS - 1, current, pltpu.roll(current, FIELDS - 1, 0))
    below = jnp.where(sub == 0, current, pltpu.roll(current, 1, 0))
    mixing = above - 2.0 * current + below
    return current - rate * (current - behind) + NU * mixing - (DT * RATIO) * lateral


def owned_terms(celerity, base_inflow, upstream, y):
    square = iota((FIELDS, FIELDS), 0) == iota((FIELDS, FIELDS), 1)

    def by_field(ref):
        row = jnp.broadcast_to(own_row(ref[...], y), (FIELDS, FIELDS))
        return jnp.sum(jnp.where(square, row, 0.0), axis=1, keepdims=True)

    feeders = own_row(upstream[...].astype(jnp.float32), y)
    ids = ((lax.axis_index("gx") - 1) * BASINS + iota((BASINS, feeders.shape[1]), 0)).astype(jnp.float32)
    hits = jnp.where(jnp.broadcast_to(feeders, ids.shape) == ids, 1.0, 0.0)
    weight = jnp.sum(hits, axis=1, keepdims=True)
    return jnp.concatenate(
        [jnp.broadcast_to(column, (8, LANES)) for column in (by_field(celerity), by_field(base_inflow), weight)],
        axis=0,
    )


def place():
    gx = lax.axis_index("gx")
    return (gx & 1) == 0, lax.axis_index("gy"), gx == 0, gx == lax.axis_size("gx") - 1


def first_kernel(*refs):
    count = len(refs) - 1
    sources, held, arrived = refs[:6], refs[count - 6 : count], refs[count]
    copies = [
        pltpu.make_async_copy(source, target, arrived.at[i])
        for i, (source, target) in enumerate(zip(sources, held))
    ]
    for copy in copies:
        copy.start()
    for copy in copies:
        copy.wait()
    first_body(*held, *refs[6 : count - 6])


def first_body(
    depth,
    discharge,
    cell_in,
    site_in,
    coeff_in,
    reach,
    beside_ref,
    across_ref,
    mine_ref,
    cell_ref,
    site_ref,
    coeff_ref,
    slots_ref,
):
    even = place()[0]

    def arranged(ref):
        low, own, high = ref[0:8], ref[8:16], ref[16:24]
        return jnp.concatenate([own, jnp.where(even, high, low), jnp.where(even, low, high)], axis=0)

    cell = arranged(cell_in)
    site = arranged(site_in)
    coeff = jnp.where(cell >= 0, arranged(coeff_in), 0.0)
    cell = jnp.maximum(cell, 0)
    cell_ref[...] = cell
    site_ref[...] = site
    coeff_ref[...] = coeff
    slots = depth_at_slots(depth, (), cell)
    slots_ref[...] = slots
    for at, value in enumerate((slots, site.astype(jnp.float32), coeff)):
        for v, ref in enumerate((mine_ref, beside_ref, across_ref)):
            ref[8 * at : 8 * at + 8] = value[8 * v : 8 * v + 8]
    cells = [depth[...], discharge[0], discharge[1]]
    mine_ref[24:32] = jnp.zeros((8, LANES), jnp.float32)
    left, right = edge_columns(cells)
    mine_ref[24:25] = left
    mine_ref[25:26] = right
    for ref in (beside_ref, across_ref):
        ref[FIRST_EDGE:FIRST_LEVELS] = jnp.zeros((FIRST_LEVELS - FIRST_EDGE, LANES), jnp.float32)
        for f in range(FIELDS):
            at = FIRST_LEVELS + 8 * f
            ref[at : at + 8] = reach[:, f * LANES : (f + 1) * LANES]
    put_edges(beside_ref, across_ref, cells, even, FIRST_EDGE)


def column_for(mine, b, start):
    y = lax.axis_index("gy")
    left = mine[start : start + 1]
    right = mine[start + 1 : start + 2]
    return jnp.where(b == y - 1, left, jnp.where(b == y + 1, right, 0.0))


def first_pack(mine, near, over, send):
    refs = (mine, near, over)
    for b in range(BASINS):
        for v, ref in enumerate(refs):
            send[b, v : v + 1] = ref[b : b + 1]
            send[b, 3 + v : 4 + v] = ref[16 + b : 17 + b]
            send[b, 8 + 8 * v : 16 + 8 * v] = ref[8:16]
        send[b, 6:7] = column_for(mine, b, 24)
        send[b, 7:8] = jnp.zeros((1, LANES), jnp.float32)


def pack(mine, near, over, send):
    even = place()[0]
    outlet = jnp.where(even, over[OUTLET : OUTLET + 1], near[OUTLET : OUTLET + 1])
    refs = (mine, near, over)
    for b in range(BASINS):
        for v, ref in enumerate(refs):
            send[b, v : v + 1] = ref[b : b + 1]
            send[b, 3 + v : 4 + v] = ref[8 + b : 9 + b]
        send[b, 6:7] = column_for(mine, b, 16)
        send[b, 7:8] = outlet


def last_pack(mine, near, over, send):
    even = place()[0]
    outlet = jnp.where(even, over[OUTLET : OUTLET + 1], near[OUTLET : OUTLET + 1])
    refs = (mine, near, over)
    for b in range(BASINS):
        for v, ref in enumerate(refs):
            send[b, 3 + v : 4 + v] = ref[8 + b : 9 + b]
            send[b, 8 + 8 * v : 16 + 8 * v] = ref[0:8]
            send[b, v : v + 1] = jnp.zeros((1, LANES), jnp.float32)
        send[b, 6:7] = column_for(mine, b, 16)
        send[b, 7:8] = outlet
        send[b, 32:40] = mine[24:32]


def gathered(got, row):
    return jnp.concatenate([got[:, row + v, :] for v in range(3)], axis=0)


def advance_levels(current, outlets, own, site_owner, coeff_owner, segment_owner, slots_owner):
    rates = coeff_owner * (segment_owner - slots_owner)
    lateral = spread(rates, site_owner >> 7, site_owner & (LANES - 1), FIELDS)
    return river_update(current, inflow_of(own, outlets), own[0:8], lateral)


def advance_cells(base, edges, cell, coeff, segment, slots):
    major, minor = cell_parts(cell)
    rates = coeff * (segment - slots)
    blocks = spread(rates, major, minor, QUADS * ROWS)
    source = jnp.concatenate([blocks[q * ROWS : (q + 1) * ROWS] for q in range(QUADS)], axis=1)
    return flood_finish([base[0], base[1], base[2]], edges, source)


def first_flow(depth, discharge, rough, celerity, base_inflow, upstream, base, terms):
    new = flood_base([depth[...], discharge[0], discharge[1]], rough[...])
    for k in range(3):
        base[k] = new[k]
    for b in range(BASINS):
        terms[b] = owned_terms(celerity, base_inflow, upstream, b)


def flow(state, rough, base):
    new = flood_base([state[0], state[1], state[2]], rough[...])
    for k in range(3):
        base[k] = new[k]


def flow_and_total(state, rough, owner_coeff, owner_site, base, total):
    flow(state, rough, base)
    site = owner_site[...]
    total[...] = spread(owner_coeff[...], site >> 7, site & (LANES - 1), FIELDS)


def last_kernel(
    state, got, near, over, base, cell_ref, coeff_ref, slots_ref, got_first, terms, state_out, reach_out, held_state, sent
):
    cells = [state[0], state[1], state[2]]
    edges = get_edges(got, near, over, cells, place(), EDGE, 6)
    new = advance_cells(
        base, edges, cell_ref[...], coeff_ref[...], gathered(got, 3), slots_ref[...]
    )
    for k in range(3):
        held_state[k] = new[k]
    copy = pltpu.make_async_copy(held_state, state_out, sent)
    copy.start()
    outlets = got[:, 7, :]
    lane = iota((FIELDS, LANES), 1)
    for b in range(BASINS):
        own = terms[b]
        site = jnp.concatenate([got_first[:, 8 + 8 * v + b, :] for v in range(3)], axis=0)
        site = site.astype(jnp.int32)
        held = jnp.concatenate([got[:, 8 + 8 * v + b, :] for v in range(3)], axis=0)
        drawn = spread(held, site >> 7, site & (LANES - 1), FIELDS)
        entering = jnp.where(lane == 0, own[0:8] * inflow_of(own, outlets), 0.0)
        level = got[b, 32:40, :] + entering + (DT * RATIO) * drawn
        for f in range(FIELDS):
            reach_out[b : b + 1, f * LANES : (f + 1) * LANES] = level[f : f + 1]
    copy.wait()


def step_kernel(first, tail, *refs):
    refs = list(refs)

    def take(n):
        taken = refs[:n]
        del refs[:n]
        return taken

    if first:
        depth, discharge, reach, site_ref, terms = take(5)
    else:
        state, levels, owner_levels, owner_site, owner_coeff, own_ref = take(6)
    got, near, over, base, cell_ref, coeff_ref, slots_ref = take(7)
    if tail:
        (total,) = take(1)
    state_out, slots_out, beside_ref, across_ref, mine_ref = take(5)
    if not tail:
        levels_out, owner_levels_out = take(2)
    if first:
        owner_site_out, owner_coeff_out, own_out = take(3)
    spot = place()
    even, y = spot[0], spot[1]
    cell = cell_ref[...]

    slots_owner = gathered(got, 0)
    if first:
        cells = [depth[...], discharge[0], discharge[1]]
        current = jnp.concatenate(
            [own_row(reach[:, f * LANES : (f + 1) * LANES], y) for f in range(FIELDS)], axis=0
        )

        def tile_rows(f, v):
            if v == 0:
                return reach[:, f * LANES : (f + 1) * LANES]
            return (near if v == 1 else over)[FIRST_LEVELS + 8 * f : FIRST_LEVELS + 8 * f + 8, :]

        segment = level_at_sites(tile_rows, site_ref[...])
        site_owner = jnp.concatenate([got[:, 8 + 8 * v + y, :] for v in range(3)], axis=0)
        site_owner = site_owner.astype(jnp.int32)
        coeff_owner = gathered(got, 3)
        outlets = jnp.zeros((BASINS, LANES), jnp.float32)
        for f in range(FIELDS):
            source_rows = jnp.where(even, tile_rows(f, 2), tile_rows(f, 1))
            outlets = jnp.where(
                iota((BASINS, LANES), 1) == f, source_rows[:, LANES - 1 : LANES], outlets
            )
        segment_owner = level_at_sites(
            lambda f, v: jnp.broadcast_to(current[f : f + 1], (8, LANES)), site_owner
        )
        own = terms[y]
        owner_site_out[...] = site_owner
        owner_coeff_out[...] = coeff_owner
        own_out[...] = own
    else:
        cells = [state[0], state[1], state[2]]
        current = levels[...]
        segment = gathered(got, 3)
        site_owner = owner_site[...]
        coeff_owner = owner_coeff[...]
        segment_owner = owner_levels[...]
        outlets = got[:, 7, :]
        own = own_ref[...]

    levels_next = advance_levels(
        current, outlets, own, site_owner, coeff_owner, segment_owner, slots_owner
    )
    edges = get_edges(got, near, over, cells, spot, FIRST_EDGE if first else EDGE, 6)
    new = advance_cells(base, edges, cell, coeff_ref[...], segment, slots_ref[...])
    for k in range(3):
        state_out[k] = new[k]
    owned = level_at_sites(
        lambda f, v: jnp.broadcast_to(levels_next[f : f + 1], (8, LANES)), site_owner
    )
    if not tail:
        levels_out[...] = levels_next
        owner_levels_out[...] = owned
    slots = depth_at_slots(state_out, (0,), cell)
    slots_out[...] = slots
    if tail:
        slots = slots * coeff_ref[...]
    blank = jnp.zeros((8, LANES), jnp.float32)
    outlet_row = column_to_lane(levels_next[:, LANES - 1 : LANES], 0)
    for v, ref in enumerate((mine_ref, beside_ref, across_ref)):
        ref[0:8] = slots[8 * v : 8 * v + 8]
        ref[8:16] = owned[8 * v : 8 * v + 8]
        ref[16:24] = blank
        if v > 0:
            ref[OUTLET : OUTLET + 1] = outlet_row
            ref[EDGE : EDGE + 8] = blank
            ref[EDGE + 8 : EDGE + 16] = blank
    left, right = edge_columns(new)
    mine_ref[16:17] = left
    mine_ref[17:18] = right
    put_edges(beside_ref, across_ref, new, even, EDGE)
    if tail:
        none = jnp.zeros((FIELDS, 1), jnp.float32)
        mine_ref[24:32] = river_update(levels_next, none, own[0:8], total[...] * levels_next)
    else:
        mine_ref[24:32] = blank


def call(kernel, outs, args, limit=16 << 20):
    return pl.pallas_call(
        kernel,
        out_shape=outs,
        in_specs=[pl.BlockSpec(memory_space=pltpu.VMEM) for _ in args],
        out_specs=[pl.BlockSpec(memory_space=pltpu.VMEM) for _ in outs],
        compiler_params=None if INTERPRET else pltpu.CompilerParams(vmem_limit_bytes=limit),
        interpret=INTERPRET,
    )(*args)


def f32(*shape):
    return jax.ShapeDtypeStruct(shape, jnp.float32)


def i32(*shape):
    return jax.ShapeDtypeStruct(shape, jnp.int32)


def per_device(
    depth,
    discharge,
    roughness,
    reach_state,
    celerity,
    base_inflow,
    upstream,
    bank_cell,
    bank_site,
    bank_coeff,
):
    count_x = lax.axis_size("gx")
    chip = [(i, i ^ 1) for i in range(count_x)]
    border = [(i, i + 1) for i in range(1, count_x - 1, 2)]
    border = border + [(b, a) for a, b in border]

    def exchange(kernel, rows, beside, across, mine, ready):
        across, beside = lax.optimization_barrier((across, beside))
        near = lax.ppermute(beside, "gx", chip)
        over = lax.ppermute(across, "gx", border)
        over, near = lax.optimization_barrier((over, near))
        send = call(kernel, [f32(BASINS, rows, LANES)], [mine, near, over])[0]
        send, ready = lax.optimization_barrier((send, ready))
        return lax.all_to_all(send, "gy", 0, 0), near, over, ready

    table = (SLOT_ROWS, LANES)
    outs = [
        f32(FIRST_SWAP, LANES),
        f32(FIRST_SWAP, LANES),
        f32(32, LANES),
        i32(*table),
        i32(*table),
        f32(*table),
        f32(*table),
    ]
    inputs = [depth, discharge, bank_cell, bank_site, bank_coeff, reach_state]
    inputs = [pltpu.with_memory_space_constraint(x, pltpu.HBM) for x in inputs]
    beside, across, mine, cell, site, coeff, slots = pl.pallas_call(
        first_kernel,
        out_shape=outs,
        in_specs=[pl.BlockSpec(memory_space=pltpu.HBM) for _ in inputs],
        out_specs=[pl.BlockSpec(memory_space=pltpu.VMEM) for _ in outs],
        scratch_shapes=[pltpu.VMEM(x.shape, x.dtype) for x in inputs]
        + [pltpu.SemaphoreType.DMA((len(inputs),))],
        compiler_params=None if INTERPRET else pltpu.CompilerParams(vmem_limit_bytes=16 << 20),
        interpret=pltpu.InterpretParams() if INTERPRET else False,
    )(*inputs)
    base, terms = call(
        first_flow,
        [f32(3, ROWS, COLS), f32(BASINS, 24, LANES)],
        [depth, discharge, roughness, celerity, base_inflow, upstream],
    )
    got, near, over, (base, terms) = exchange(first_pack, 32, beside, across, mine, (base, terms))
    got_first = got
    for step in range(STEPS - 1):
        first, tail = step == 0, step == STEPS - 2
        outs = [
            f32(3, ROWS, COLS),
            f32(*table),
            f32(SWAP, LANES),
            f32(SWAP, LANES),
            f32(32, LANES),
        ]
        if not tail:
            outs += [f32(FIELDS, LANES), f32(*table)]
        if first:
            outs += [i32(*table), f32(*table), f32(*table)]
            args = [depth, discharge, reach_state, site, terms]
        else:
            args = [state, levels, owner_levels, owner_site, owner_coeff, own]
        args += [got, near, over, base, cell, coeff, slots]
        if tail:
            args += [total]
        result = call(functools.partial(step_kernel, first, tail), outs, args)
        state, slots, beside, across, mine = result[:5]
        if not tail:
            levels, owner_levels = result[5:7]
        if first:
            owner_site, owner_coeff, own = result[7:10]
        if first:
            base, total = call(
                flow_and_total,
                [f32(3, ROWS, COLS), f32(FIELDS, LANES)],
                [state, roughness, owner_coeff, owner_site],
            )
        else:
            base = call(flow, [f32(3, ROWS, COLS)], [state, roughness])[0]
        got, near, over, base = exchange(
            last_pack if tail else pack, 40 if tail else BASINS, beside, across, mine, base
        )
    inputs = [state, got, near, over, base, cell, coeff, slots, got_first, terms]
    state, reach = pl.pallas_call(
        last_kernel,
        out_shape=[f32(3, ROWS, COLS), f32(BASINS, FIELDS * LANES)],
        in_specs=[pl.BlockSpec(memory_space=pltpu.VMEM) for _ in inputs],
        out_specs=[pl.BlockSpec(memory_space=pl.ANY), pl.BlockSpec(memory_space=pltpu.VMEM)],
        scratch_shapes=[pltpu.VMEM((3, ROWS, COLS), jnp.float32), pltpu.SemaphoreType.DMA],
        compiler_params=None if INTERPRET else pltpu.CompilerParams(vmem_limit_bytes=16 << 20),
        interpret=pltpu.InterpretParams() if INTERPRET else False,
    )(*inputs)
    return state, reach


def solution(mesh):
    return jax.shard_map(
        per_device,
        mesh=mesh,
        in_specs=(
            P("gx", "gy"),
            P(None, "gx", "gy"),
            P("gx", "gy"),
            P("gx", None),
            P("gx", None),
            P("gx", None),
            P("gx", None),
            P("gx", "gy"),
            P("gx", "gy"),
            P("gx", "gy"),
        ),
        out_specs=(P(None, "gx", "gy"), P("gx", None)),
        check_vma=False,
    )
```

```python
import functools

import jax
import jax.numpy as jnp
from jax import lax
from jax.experimental import pallas as pl
from jax.experimental.pallas import tpu as pltpu
from jax.sharding import PartitionSpec as P

STEPS = 4


GRAV = 9.81
DT = 0.5
DX = 10.0
NU = 0.1
RATIO = 0.25
FACTOR = DT / (2.0 * DX)

LANES = 128
ROWS = 32
QUADS = 4
COLS = QUADS * LANES
FIELDS = 8
BASINS = 8
SLOT_ROWS = 3 * BASINS
INTERPRET = False

FIRST_EDGE = 24
FIRST_LEVELS = 40
FIRST_SWAP = FIRST_LEVELS + FIELDS * BASINS
OUTLET = 16
EDGE = 24
SWAP = 40


def iota(shape, dim):
    return lax.broadcasted_iota(jnp.int32, shape, dim)


def lane_gather(rows, index):
    return jnp.take_along_axis(rows, index, axis=1, mode="promise_in_bounds")


def lane_to_column(row, count, offset):
    wide = jnp.broadcast_to(row, (count, LANES))
    hit = iota((count, LANES), 1) == iota((count, LANES), 0) + offset
    return jnp.sum(jnp.where(hit, wide, 0.0), axis=1, keepdims=True)


def column_to_lane(column, offset):
    count = column.shape[0]
    wide = jnp.broadcast_to(column, (count, LANES))
    hit = iota((count, LANES), 1) == iota((count, LANES), 0) + offset
    return jnp.sum(jnp.where(hit, wide, 0.0), axis=0, keepdims=True)


def own_row(block, y):
    return jnp.sum(jnp.where(iota(block.shape, 0) == y, block, 0.0), axis=0, keepdims=True)


def flux_terms(cells):
    h, p, q = cells
    inverse = 1.0 / h
    u = p * inverse
    v = q * inverse
    pressure = 0.5 * GRAV * h * h
    return (p, p * u + pressure, q * u), (q, p * v, q * v + pressure), u, v


def flood_base(cells, rough):
    flux_x, flux_y, u, v = flux_terms(cells)
    row = iota((ROWS, COLS), 0)
    col = iota((ROWS, COLS), 1)
    out = []
    for k in range(3):
        quarter = 0.25 * cells[k]
        from_top = jnp.where(row == 0, 0.0, pltpu.roll(quarter + FACTOR * flux_x[k], 1, 0))
        from_low = jnp.where(row == ROWS - 1, 0.0, pltpu.roll(quarter - FACTOR * flux_x[k], ROWS - 1, 0))
        from_left = jnp.where(col == 0, 0.0, pltpu.roll(quarter + FACTOR * flux_y[k], 1, 1))
        from_right = jnp.where(col == COLS - 1, 0.0, pltpu.roll(quarter - FACTOR * flux_y[k], COLS - 1, 1))
        out.append((from_top + from_low) + (from_left + from_right))
    h = cells[0]
    size = jnp.abs(h)
    root = jnp.exp(jnp.log(size) * (-1.0 / 3.0))
    root = root * (4.0 - size * (root * root * root)) * (1.0 / 3.0)
    root = jnp.where(h < 0.0, -root, root)
    drag = (GRAV * DT) * rough * rough * jnp.sqrt(u * u + v * v) * root
    return [out[0], out[1] - drag * u, out[2] - drag * v]


def flood_finish(base, edges, source):
    top, low, left, right = edges
    top_x = flux_terms(top)[0]
    low_x = flux_terms(low)[0]
    left_y = flux_terms(left)[1]
    right_y = flux_terms(right)[1]
    first_row = iota((8, COLS), 0) == 0
    last_row = iota((8, COLS), 0) == 7
    first_col = iota((ROWS, LANES), 1) == 0
    last_col = iota((ROWS, LANES), 1) == LANES - 1
    out = []
    for k in range(3):
        cells = base[k]
        upper = cells[0:8] + jnp.where(first_row, 0.25 * top[k] + FACTOR * top_x[k], 0.0)
        lower = cells[ROWS - 8 : ROWS] + jnp.where(last_row, 0.25 * low[k] - FACTOR * low_x[k], 0.0)
        cells = jnp.concatenate([upper, cells[8 : ROWS - 8], lower], axis=0)
        west = cells[:, :LANES] + jnp.where(first_col, 0.25 * left[k] + FACTOR * left_y[k], 0.0)
        east = cells[:, COLS - LANES :] + jnp.where(last_col, 0.25 * right[k] - FACTOR * right_y[k], 0.0)
        out.append(jnp.concatenate([west, cells[:, LANES : COLS - LANES], east], axis=1))
    out[0] = out[0] + DT * source
    return out


def halves(values):
    high = values.astype(jnp.bfloat16).astype(jnp.float32)
    return high, values - high


def spread(rates, major, minor, count):
    total = None
    rows = rates.shape[0]
    group = 4
    high, low = halves(rates)
    for start in range(0, rows, group):
        left, right = [], []
        for r in range(start, start + group):
            at = iota((count, LANES), 0) == major[r : r + 1]
            left.append(
                jnp.concatenate(
                    [
                        jnp.where(at, high[r : r + 1], 0.0),
                        jnp.where(at, low[r : r + 1], 0.0),
                    ],
                    axis=0,
                ).astype(jnp.bfloat16)
            )
            right.append(
                jnp.where(iota((LANES, LANES), 0) == minor[r : r + 1], 1.0, 0.0).astype(jnp.bfloat16)
            )
        part = lax.dot_general(
            jnp.concatenate(left, axis=1),
            jnp.concatenate(right, axis=1),
            (((1,), (1,)), ((), ())),
            preferred_element_type=jnp.float32,
        )
        total = part if total is None else total + part
    return total[:count] + total[count:]


def repeated(row, count):
    tile = jnp.broadcast_to(row, (16, LANES)).astype(jnp.bfloat16)
    return jnp.concatenate([tile] * (count // 16), axis=0)


def spread_cells(rates, major, minor):
    high, low = halves(rates)
    major = major.astype(jnp.float32)
    minor = minor.astype(jnp.float32)
    row = iota((LANES, LANES), 0).astype(jnp.float32).astype(jnp.bfloat16)
    zero = jnp.zeros((), jnp.bfloat16)
    one = jnp.ones((), jnp.bfloat16)
    total = None
    group = 4
    for start in range(0, rates.shape[0], group):
        left, right = [], []
        for r in range(start, start + group):
            at = row == repeated(major[r : r + 1], LANES)
            left.append(
                jnp.concatenate(
                    [jnp.where(at, repeated(part[r : r + 1], LANES), zero) for part in (high, low)], axis=0
                )
            )
            right.append(jnp.where(row == repeated(minor[r : r + 1], LANES), one, zero))
        part = lax.dot_general(
            jnp.concatenate(left, axis=1),
            jnp.concatenate(right, axis=1),
            (((1,), (1,)), ((), ())),
            preferred_element_type=jnp.float32,
        )
        total = part if total is None else total + part
    return total[:LANES] + total[LANES:]


def cell_parts(cell):
    col = cell & (COLS - 1)
    return (col >> 7) * ROWS + (cell >> 9), col & (LANES - 1)


def depth_at_slots(h_ref, index, cell):
    major, minor = cell_parts(cell)
    found = []
    for v in range(3):
        key = major[8 * v : 8 * v + 8]
        lane = minor[8 * v : 8 * v + 8]
        depth = jnp.zeros((8, LANES), jnp.float32)
        for quad in range(QUADS):
            for row in range(ROWS):
                values = h_ref[index + (slice(row, row + 1), slice(quad * LANES, (quad + 1) * LANES))]
                values = jnp.broadcast_to(values, (8, LANES))
                depth = jnp.where(key == quad * ROWS + row, lane_gather(values, lane), depth)
        found.append(depth)
    return jnp.concatenate(found, axis=0)


def level_at_sites(reach_rows, site):
    found = []
    for v in range(3):
        sites = site[8 * v : 8 * v + 8]
        field = sites >> 7
        station = sites & (LANES - 1)
        level = jnp.zeros((8, LANES), jnp.float32)
        for f in range(FIELDS):
            level = jnp.where(field == f, lane_gather(reach_rows(f, v), station), level)
        found.append(level)
    return jnp.concatenate(found, axis=0)


def edge_columns(cells):
    left = column_to_lane(cells[0][:, 0:1], 0)
    right = column_to_lane(cells[0][:, COLS - 1 : COLS], 0)
    for k in (1, 2):
        left = left + column_to_lane(cells[k][:, 0:1], k * ROWS)
        right = right + column_to_lane(cells[k][:, COLS - 1 : COLS], k * ROWS)
    return left, right


def put_edges(beside_ref, across_ref, cells, even, start):
    for k in range(3):
        first = cells[k][0:1]
        last = cells[k][ROWS - 1 : ROWS]
        inner = jnp.where(even, last, first)
        outer = jnp.where(even, first, last)
        for quad in range(QUADS):
            at = start + k * QUADS + quad
            lanes = slice(quad * LANES, (quad + 1) * LANES)
            beside_ref[at : at + 1, :] = inner[:, lanes]
            across_ref[at : at + 1, :] = outer[:, lanes]


def get_edges(got_ref, near_ref, over_ref, cells, spot, start, col_row):
    even, y, is_first, is_last = spot
    before = got_ref[jnp.maximum(y - 1, 0), col_row : col_row + 1, :]
    after = got_ref[jnp.minimum(y + 1, BASINS - 1), col_row : col_row + 1, :]

    def edge(ref, k):
        rows = [ref[start + k * QUADS + q : start + k * QUADS + q + 1, :] for q in range(QUADS)]
        return jnp.concatenate(rows, axis=1)

    top, low, left, right = [], [], [], []
    for k in range(3):
        inner = edge(near_ref, k)
        outer = edge(over_ref, k)
        top.append(jnp.where(is_first, cells[k][0:1], jnp.where(even, outer, inner)))
        low.append(jnp.where(is_last, cells[k][ROWS - 1 : ROWS], jnp.where(even, inner, outer)))
        left.append(jnp.where(y == 0, cells[k][:, 0:1], lane_to_column(before, ROWS, k * ROWS)))
        right.append(
            jnp.where(
                y == BASINS - 1, cells[k][:, COLS - 1 : COLS], lane_to_column(after, ROWS, k * ROWS)
            )
        )
    return top, low, left, right


def inflow_of(own, outlets):
    row = jnp.sum(own[16:24] * outlets, axis=0, keepdims=True)
    return own[8:16, 0:1] + lane_to_column(row, FIELDS, 0)


def river_update(current, inflow, rate, lateral):
    lane = iota((FIELDS, LANES), 1)
    sub = iota((FIELDS, LANES), 0)
    behind = jnp.where(lane == 0, inflow, pltpu.roll(current, 1, 1))
    above = jnp.where(sub == FIELDS - 1, current, pltpu.roll(current, FIELDS - 1, 0))
    below = jnp.where(sub == 0, current, pltpu.roll(current, 1, 0))
    mixing = above - 2.0 * current + below
    return current - rate * (current - behind) + NU * mixing - (DT * RATIO) * lateral


def owned_terms(celerity, base_inflow, upstream, y):
    square = iota((FIELDS, FIELDS), 0) == iota((FIELDS, FIELDS), 1)

    def by_field(ref):
        row = jnp.broadcast_to(own_row(ref[...], y), (FIELDS, FIELDS))
        return jnp.sum(jnp.where(square, row, 0.0), axis=1, keepdims=True)

    feeders = own_row(upstream[...].astype(jnp.float32), y)
    ids = ((lax.axis_index("gx") - 1) * BASINS + iota((BASINS, feeders.shape[1]), 0)).astype(jnp.float32)
    hits = jnp.where(jnp.broadcast_to(feeders, ids.shape) == ids, 1.0, 0.0)
    weight = jnp.sum(hits, axis=1, keepdims=True)
    return jnp.concatenate(
        [jnp.broadcast_to(column, (8, LANES)) for column in (by_field(celerity), by_field(base_inflow), weight)],
        axis=0,
    )


def place():
    gx = lax.axis_index("gx")
    return (gx & 1) == 0, lax.axis_index("gy"), gx == 0, gx == lax.axis_size("gx") - 1


def first_kernel(*refs):
    count = len(refs) - 1
    sources, held, arrived = refs[:6], refs[count - 6 : count], refs[count]
    copies = [
        pltpu.make_async_copy(source, target, arrived.at[i])
        for i, (source, target) in enumerate(zip(sources, held))
    ]
    for copy in copies:
        copy.start()
    first_body(copies, *held, *refs[6 : count - 6])


def first_body(
    copies,
    depth,
    discharge,
    cell_in,
    site_in,
    coeff_in,
    reach,
    beside_ref,
    across_ref,
    mine_ref,
    cell_ref,
    site_ref,
    coeff_ref,
    slots_ref,
):
    even = place()[0]

    def arranged(ref):
        low, own, high = ref[0:8], ref[8:16], ref[16:24]
        return jnp.concatenate([own, jnp.where(even, high, low), jnp.where(even, low, high)], axis=0)

    copies[0].wait()
    copies[2].wait()
    bank = arranged(cell_in)
    cell = jnp.maximum(bank, 0)
    cell_ref[...] = cell
    slots = depth_at_slots(depth, (), cell)
    slots_ref[...] = slots
    for i in (1, 3, 4, 5):
        copies[i].wait()
    site = arranged(site_in)
    coeff = jnp.where(bank >= 0, arranged(coeff_in), 0.0)
    site_ref[...] = site
    coeff_ref[...] = coeff
    for at, value in enumerate((slots, site.astype(jnp.float32), coeff)):
        for v, ref in enumerate((mine_ref, beside_ref, across_ref)):
            ref[8 * at : 8 * at + 8] = value[8 * v : 8 * v + 8]
    cells = [depth[...], discharge[0], discharge[1]]
    mine_ref[24:32] = jnp.zeros((8, LANES), jnp.float32)
    left, right = edge_columns(cells)
    mine_ref[24:25] = left
    mine_ref[25:26] = right
    for ref in (beside_ref, across_ref):
        ref[FIRST_EDGE:FIRST_LEVELS] = jnp.zeros((FIRST_LEVELS - FIRST_EDGE, LANES), jnp.float32)
        for f in range(FIELDS):
            at = FIRST_LEVELS + 8 * f
            ref[at : at + 8] = reach[:, f * LANES : (f + 1) * LANES]
    put_edges(beside_ref, across_ref, cells, even, FIRST_EDGE)


def column_for(mine, b, start):
    y = lax.axis_index("gy")
    left = mine[start : start + 1]
    right = mine[start + 1 : start + 2]
    return jnp.where(b == y - 1, left, jnp.where(b == y + 1, right, 0.0))


def first_pack(mine, near, over, send):
    refs = (mine, near, over)
    for b in range(BASINS):
        for v, ref in enumerate(refs):
            send[b, v : v + 1] = ref[b : b + 1]
            send[b, 3 + v : 4 + v] = ref[16 + b : 17 + b]
            send[b, 8 + 8 * v : 16 + 8 * v] = ref[8:16]
        send[b, 6:7] = column_for(mine, b, 24)
        send[b, 7:8] = jnp.zeros((1, LANES), jnp.float32)


def pack(mine, near, over, send):
    even = place()[0]
    outlet = jnp.where(even, over[OUTLET : OUTLET + 1], near[OUTLET : OUTLET + 1])
    refs = (mine, near, over)
    for b in range(BASINS):
        for v, ref in enumerate(refs):
            send[b, v : v + 1] = ref[b : b + 1]
            send[b, 3 + v : 4 + v] = ref[8 + b : 9 + b]
        send[b, 6:7] = column_for(mine, b, 16)
        send[b, 7:8] = outlet


def last_pack(mine, near, over, send):
    even = place()[0]
    outlet = jnp.where(even, over[OUTLET : OUTLET + 1], near[OUTLET : OUTLET + 1])
    refs = (mine, near, over)
    for b in range(BASINS):
        for v, ref in enumerate(refs):
            send[b, 3 + v : 4 + v] = ref[8 + b : 9 + b]
            send[b, 8 + 8 * v : 16 + 8 * v] = ref[0:8]
            send[b, v : v + 1] = jnp.zeros((1, LANES), jnp.float32)
        send[b, 6:7] = column_for(mine, b, 16)
        send[b, 7:8] = outlet
        send[b, 32:40] = mine[24:32]


def gathered(got, row):
    return jnp.concatenate([got[:, row + v, :] for v in range(3)], axis=0)


def advance_levels(current, outlets, own, site_owner, coeff_owner, segment_owner, slots_owner):
    rates = coeff_owner * (segment_owner - slots_owner)
    lateral = spread(rates, site_owner >> 7, site_owner & (LANES - 1), FIELDS)
    return river_update(current, inflow_of(own, outlets), own[0:8], lateral)


def advance_cells(base, edges, cell, coeff, segment, slots):
    major, minor = cell_parts(cell)
    rates = coeff * (segment - slots)
    blocks = spread_cells(rates, major, minor)
    source = jnp.concatenate([blocks[q * ROWS : (q + 1) * ROWS] for q in range(QUADS)], axis=1)
    return flood_finish([base[0], base[1], base[2]], edges, source)


def first_flow(depth, discharge, rough, celerity, base_inflow, upstream, base, terms):
    new = flood_base([depth[...], discharge[0], discharge[1]], rough[...])
    for k in range(3):
        base[k] = new[k]
    for b in range(BASINS):
        terms[b] = owned_terms(celerity, base_inflow, upstream, b)


def flow(state, rough, base):
    new = flood_base([state[0], state[1], state[2]], rough[...])
    for k in range(3):
        base[k] = new[k]


def flow_and_total(state, rough, owner_coeff, owner_site, base, total):
    flow(state, rough, base)
    site = owner_site[...]
    total[...] = spread(owner_coeff[...], site >> 7, site & (LANES - 1), FIELDS)


def last_kernel(
    state, got, near, over, base, cell_ref, coeff_ref, slots_ref, got_first, terms, state_out, reach_out
):
    cells = [state[0], state[1], state[2]]
    edges = get_edges(got, near, over, cells, place(), EDGE, 6)
    new = advance_cells(
        base, edges, cell_ref[...], coeff_ref[...], gathered(got, 3), slots_ref[...]
    )
    for k in range(3):
        state_out[k] = new[k]
    outlets = got[:, 7, :]
    lane = iota((FIELDS, LANES), 1)
    for b in range(BASINS):
        own = terms[b]
        site = jnp.concatenate([got_first[:, 8 + 8 * v + b, :] for v in range(3)], axis=0)
        site = site.astype(jnp.int32)
        held = jnp.concatenate([got[:, 8 + 8 * v + b, :] for v in range(3)], axis=0)
        drawn = spread(held, site >> 7, site & (LANES - 1), FIELDS)
        entering = jnp.where(lane == 0, own[0:8] * inflow_of(own, outlets), 0.0)
        level = got[b, 32:40, :] + entering + (DT * RATIO) * drawn
        for f in range(FIELDS):
            reach_out[b : b + 1, f * LANES : (f + 1) * LANES] = level[f : f + 1]


def step_kernel(first, tail, *refs):
    refs = list(refs)

    def take(n):
        taken = refs[:n]
        del refs[:n]
        return taken

    if first:
        depth, discharge, reach, site_ref, terms = take(5)
    else:
        state, levels, owner_levels, owner_site, owner_coeff, own_ref = take(6)
    got, near, over, base, cell_ref, coeff_ref, slots_ref = take(7)
    if tail:
        (total,) = take(1)
    state_out, slots_out, beside_ref, across_ref, mine_ref = take(5)
    if not tail:
        levels_out, owner_levels_out = take(2)
    if first:
        owner_site_out, owner_coeff_out, own_out = take(3)
    spot = place()
    even, y = spot[0], spot[1]
    cell = cell_ref[...]

    slots_owner = gathered(got, 0)
    if first:
        cells = [depth[...], discharge[0], discharge[1]]
        current = jnp.concatenate(
            [own_row(reach[:, f * LANES : (f + 1) * LANES], y) for f in range(FIELDS)], axis=0
        )

        def tile_rows(f, v):
            if v == 0:
                return reach[:, f * LANES : (f + 1) * LANES]
            return (near if v == 1 else over)[FIRST_LEVELS + 8 * f : FIRST_LEVELS + 8 * f + 8, :]

        segment = level_at_sites(tile_rows, site_ref[...])
        site_owner = jnp.concatenate([got[:, 8 + 8 * v + y, :] for v in range(3)], axis=0)
        site_owner = site_owner.astype(jnp.int32)
        coeff_owner = gathered(got, 3)
        outlets = jnp.zeros((BASINS, LANES), jnp.float32)
        for f in range(FIELDS):
            source_rows = jnp.where(even, tile_rows(f, 2), tile_rows(f, 1))
            outlets = jnp.where(
                iota((BASINS, LANES), 1) == f, source_rows[:, LANES - 1 : LANES], outlets
            )
        segment_owner = level_at_sites(
            lambda f, v: jnp.broadcast_to(current[f : f + 1], (8, LANES)), site_owner
        )
        own = terms[y]
        owner_site_out[...] = site_owner
        owner_coeff_out[...] = coeff_owner
        own_out[...] = own
    else:
        cells = [state[0], state[1], state[2]]
        current = levels[...]
        segment = gathered(got, 3)
        site_owner = owner_site[...]
        coeff_owner = owner_coeff[...]
        segment_owner = owner_levels[...]
        outlets = got[:, 7, :]
        own = own_ref[...]

    levels_next = advance_levels(
        current, outlets, own, site_owner, coeff_owner, segment_owner, slots_owner
    )
    edges = get_edges(got, near, over, cells, spot, FIRST_EDGE if first else EDGE, 6)
    new = advance_cells(base, edges, cell, coeff_ref[...], segment, slots_ref[...])
    for k in range(3):
        state_out[k] = new[k]
    owned = level_at_sites(
        lambda f, v: jnp.broadcast_to(levels_next[f : f + 1], (8, LANES)), site_owner
    )
    if not tail:
        levels_out[...] = levels_next
        owner_levels_out[...] = owned
    slots = depth_at_slots(state_out, (0,), cell)
    slots_out[...] = slots
    if tail:
        slots = slots * coeff_ref[...]
    blank = jnp.zeros((8, LANES), jnp.float32)
    outlet_row = column_to_lane(levels_next[:, LANES - 1 : LANES], 0)
    for v, ref in enumerate((mine_ref, beside_ref, across_ref)):
        ref[0:8] = slots[8 * v : 8 * v + 8]
        ref[8:16] = owned[8 * v : 8 * v + 8]
        ref[16:24] = blank
        if v > 0:
            ref[OUTLET : OUTLET + 1] = outlet_row
            ref[EDGE : EDGE + 8] = blank
            ref[EDGE + 8 : EDGE + 16] = blank
    left, right = edge_columns(new)
    mine_ref[16:17] = left
    mine_ref[17:18] = right
    put_edges(beside_ref, across_ref, new, even, EDGE)
    if tail:
        none = jnp.zeros((FIELDS, 1), jnp.float32)
        mine_ref[24:32] = river_update(levels_next, none, own[0:8], total[...] * levels_next)
    else:
        mine_ref[24:32] = blank


def call(kernel, outs, args, limit=16 << 20):
    return pl.pallas_call(
        kernel,
        out_shape=outs,
        in_specs=[pl.BlockSpec(memory_space=pltpu.VMEM) for _ in args],
        out_specs=[pl.BlockSpec(memory_space=pltpu.VMEM) for _ in outs],
        compiler_params=None if INTERPRET else pltpu.CompilerParams(vmem_limit_bytes=limit),
        interpret=INTERPRET,
    )(*args)


def f32(*shape):
    return jax.ShapeDtypeStruct(shape, jnp.float32)


def i32(*shape):
    return jax.ShapeDtypeStruct(shape, jnp.int32)


def per_device(
    depth,
    discharge,
    roughness,
    reach_state,
    celerity,
    base_inflow,
    upstream,
    bank_cell,
    bank_site,
    bank_coeff,
):
    count_x = lax.axis_size("gx")
    chip = [(i, i ^ 1) for i in range(count_x)]
    border = [(i, i + 1) for i in range(1, count_x - 1, 2)]
    border = border + [(b, a) for a, b in border]

    def exchange(kernel, rows, beside, across, mine, ready):
        across, beside = lax.optimization_barrier((across, beside))
        near = lax.ppermute(beside, "gx", chip)
        over = lax.ppermute(across, "gx", border)
        over, near = lax.optimization_barrier((over, near))
        send = call(kernel, [f32(BASINS, rows, LANES)], [mine, near, over])[0]
        send, ready = lax.optimization_barrier((send, ready))
        return lax.all_to_all(send, "gy", 0, 0), near, over, ready

    table = (SLOT_ROWS, LANES)
    outs = [
        f32(FIRST_SWAP, LANES),
        f32(FIRST_SWAP, LANES),
        f32(32, LANES),
        i32(*table),
        i32(*table),
        f32(*table),
        f32(*table),
    ]
    inputs = [depth, discharge, bank_cell, bank_site, bank_coeff, reach_state]
    inputs = [pltpu.with_memory_space_constraint(x, pltpu.HBM) for x in inputs]
    beside, across, mine, cell, site, coeff, slots = pl.pallas_call(
        first_kernel,
        out_shape=outs,
        in_specs=[pl.BlockSpec(memory_space=pltpu.HBM) for _ in inputs],
        out_specs=[pl.BlockSpec(memory_space=pltpu.VMEM) for _ in outs],
        scratch_shapes=[pltpu.VMEM(x.shape, x.dtype) for x in inputs]
        + [pltpu.SemaphoreType.DMA((len(inputs),))],
        compiler_params=None if INTERPRET else pltpu.CompilerParams(vmem_limit_bytes=16 << 20),
        interpret=pltpu.InterpretParams() if INTERPRET else False,
    )(*inputs)
    base, terms = call(
        first_flow,
        [f32(3, ROWS, COLS), f32(BASINS, 24, LANES)],
        [depth, discharge, roughness, celerity, base_inflow, upstream],
    )
    got, near, over, (base, terms) = exchange(first_pack, 32, beside, across, mine, (base, terms))
    got_first = got
    for step in range(STEPS - 1):
        first, tail = step == 0, step == STEPS - 2
        outs = [
            f32(3, ROWS, COLS),
            f32(*table),
            f32(SWAP, LANES),
            f32(SWAP, LANES),
            f32(32, LANES),
        ]
        if not tail:
            outs += [f32(FIELDS, LANES), f32(*table)]
        if first:
            outs += [i32(*table), f32(*table), f32(*table)]
            args = [depth, discharge, reach_state, site, terms]
        else:
            args = [state, levels, owner_levels, owner_site, owner_coeff, own]
        args += [got, near, over, base, cell, coeff, slots]
        if tail:
            args += [total]
        result = call(functools.partial(step_kernel, first, tail), outs, args)
        state, slots, beside, across, mine = result[:5]
        if not tail:
            levels, owner_levels = result[5:7]
        if first:
            owner_site, owner_coeff, own = result[7:10]
        if first:
            base, total = call(
                flow_and_total,
                [f32(3, ROWS, COLS), f32(FIELDS, LANES)],
                [state, roughness, owner_coeff, owner_site],
            )
        else:
            base = call(flow, [f32(3, ROWS, COLS)], [state, roughness])[0]
        got, near, over, base = exchange(
            last_pack if tail else pack, 40 if tail else BASINS, beside, across, mine, base
        )
    state, reach = call(
        last_kernel,
        [f32(3, ROWS, COLS), f32(BASINS, FIELDS * LANES)],
        [state, got, near, over, base, cell, coeff, slots, got_first, terms],
    )
    return state, reach


def solution(mesh):
    return jax.shard_map(
        per_device,
        mesh=mesh,
        in_specs=(
            P("gx", "gy"),
            P(None, "gx", "gy"),
            P("gx", "gy"),
            P("gx", None),
            P("gx", None),
            P("gx", None),
            P("gx", None),
            P("gx", "gy"),
            P("gx", "gy"),
            P("gx", "gy"),
        ),
        out_specs=(P(None, "gx", "gy"), P("gx", None)),
        check_vma=False,
    )
```

```python
import functools

import jax
import jax.numpy as jnp
from jax import lax
from jax.experimental import pallas as pl
from jax.experimental.pallas import tpu as pltpu
from jax.sharding import PartitionSpec as P

STEPS = 4


GRAV = 9.81
DT = 0.5
DX = 10.0
NU = 0.1
RATIO = 0.25
FACTOR = DT / (2.0 * DX)

LANES = 128
ROWS = 32
QUADS = 4
COLS = QUADS * LANES
FIELDS = 8
BASINS = 8
SLOT_ROWS = 3 * BASINS
INTERPRET = False

FIRST_EDGE = 24
FIRST_LEVELS = 40
FIRST_SWAP = FIRST_LEVELS + FIELDS * BASINS
OUTLET = 16
EDGE = 24
SWAP = 40


def iota(shape, dim):
    return lax.broadcasted_iota(jnp.int32, shape, dim)


def lane_gather(rows, index):
    return jnp.take_along_axis(rows, index, axis=1, mode="promise_in_bounds")


def lane_to_column(row, count, offset):
    wide = jnp.broadcast_to(row, (count, LANES))
    hit = iota((count, LANES), 1) == iota((count, LANES), 0) + offset
    return jnp.sum(jnp.where(hit, wide, 0.0), axis=1, keepdims=True)


def column_to_lane(column, offset):
    count = column.shape[0]
    wide = jnp.broadcast_to(column, (count, LANES))
    hit = iota((count, LANES), 1) == iota((count, LANES), 0) + offset
    return jnp.sum(jnp.where(hit, wide, 0.0), axis=0, keepdims=True)


def own_row(block, y):
    return jnp.sum(jnp.where(iota(block.shape, 0) == y, block, 0.0), axis=0, keepdims=True)


def flux_terms(cells):
    h, p, q = cells
    inverse = 1.0 / h
    u = p * inverse
    v = q * inverse
    pressure = 0.5 * GRAV * h * h
    return (p, p * u + pressure, q * u), (q, p * v, q * v + pressure), u, v


def flood_base(cells, rough):
    flux_x, flux_y, u, v = flux_terms(cells)
    row = iota((ROWS, COLS), 0)
    col = iota((ROWS, COLS), 1)
    out = []
    for k in range(3):
        quarter = 0.25 * cells[k]
        from_top = jnp.where(row == 0, 0.0, pltpu.roll(quarter + FACTOR * flux_x[k], 1, 0))
        from_low = jnp.where(row == ROWS - 1, 0.0, pltpu.roll(quarter - FACTOR * flux_x[k], ROWS - 1, 0))
        from_left = jnp.where(col == 0, 0.0, pltpu.roll(quarter + FACTOR * flux_y[k], 1, 1))
        from_right = jnp.where(col == COLS - 1, 0.0, pltpu.roll(quarter - FACTOR * flux_y[k], COLS - 1, 1))
        out.append((from_top + from_low) + (from_left + from_right))
    h = cells[0]
    size = jnp.abs(h)
    root = jnp.exp(jnp.log(size) * (-1.0 / 3.0))
    root = root * (4.0 - size * (root * root * root)) * (1.0 / 3.0)
    root = jnp.where(h < 0.0, -root, root)
    drag = (GRAV * DT) * rough * rough * jnp.sqrt(u * u + v * v) * root
    return [out[0], out[1] - drag * u, out[2] - drag * v]


def flood_finish(base, edges, source):
    top, low, left, right = edges
    top_x = flux_terms(top)[0]
    low_x = flux_terms(low)[0]
    left_y = flux_terms(left)[1]
    right_y = flux_terms(right)[1]
    first_row = iota((8, COLS), 0) == 0
    last_row = iota((8, COLS), 0) == 7
    first_col = iota((ROWS, LANES), 1) == 0
    last_col = iota((ROWS, LANES), 1) == LANES - 1
    out = []
    for k in range(3):
        cells = base[k]
        upper = cells[0:8] + jnp.where(first_row, 0.25 * top[k] + FACTOR * top_x[k], 0.0)
        lower = cells[ROWS - 8 : ROWS] + jnp.where(last_row, 0.25 * low[k] - FACTOR * low_x[k], 0.0)
        cells = jnp.concatenate([upper, cells[8 : ROWS - 8], lower], axis=0)
        west = cells[:, :LANES] + jnp.where(first_col, 0.25 * left[k] + FACTOR * left_y[k], 0.0)
        east = cells[:, COLS - LANES :] + jnp.where(last_col, 0.25 * right[k] - FACTOR * right_y[k], 0.0)
        out.append(jnp.concatenate([west, cells[:, LANES : COLS - LANES], east], axis=1))
    out[0] = out[0] + DT * source
    return out


def halves(values):
    high = values.astype(jnp.bfloat16).astype(jnp.float32)
    return high, values - high


def spread(rates, major, minor, count):
    total = None
    rows = rates.shape[0]
    group = 4
    high, low = halves(rates)
    for start in range(0, rows, group):
        left, right = [], []
        for r in range(start, start + group):
            at = iota((count, LANES), 0) == major[r : r + 1]
            left.append(
                jnp.concatenate(
                    [
                        jnp.where(at, high[r : r + 1], 0.0),
                        jnp.where(at, low[r : r + 1], 0.0),
                    ],
                    axis=0,
                ).astype(jnp.bfloat16)
            )
            right.append(
                jnp.where(iota((LANES, LANES), 0) == minor[r : r + 1], 1.0, 0.0).astype(jnp.bfloat16)
            )
        part = lax.dot_general(
            jnp.concatenate(left, axis=1),
            jnp.concatenate(right, axis=1),
            (((1,), (1,)), ((), ())),
            preferred_element_type=jnp.float32,
        )
        total = part if total is None else total + part
    return total[:count] + total[count:]


def repeated(row, count):
    tile = jnp.broadcast_to(row, (16, LANES)).astype(jnp.bfloat16)
    return jnp.concatenate([tile] * (count // 16), axis=0)


def spread_cells(rates, major, minor):
    high, low = halves(rates)
    major = major.astype(jnp.float32)
    minor = minor.astype(jnp.float32)
    row = iota((LANES, LANES), 0).astype(jnp.float32).astype(jnp.bfloat16)
    zero = jnp.zeros((), jnp.bfloat16)
    one = jnp.ones((), jnp.bfloat16)
    total = None
    group = 4
    for start in range(0, rates.shape[0], group):
        left, right = [], []
        for r in range(start, start + group):
            at = row == repeated(major[r : r + 1], LANES)
            left.append(
                jnp.concatenate(
                    [jnp.where(at, repeated(part[r : r + 1], LANES), zero) for part in (high, low)], axis=0
                )
            )
            right.append(jnp.where(row == repeated(minor[r : r + 1], LANES), one, zero))
        part = lax.dot_general(
            jnp.concatenate(left, axis=1),
            jnp.concatenate(right, axis=1),
            (((1,), (1,)), ((), ())),
            preferred_element_type=jnp.float32,
        )
        total = part if total is None else total + part
    return total[:LANES] + total[LANES:]


def cell_parts(cell):
    col = cell & (COLS - 1)
    return (col >> 7) * ROWS + (cell >> 9), col & (LANES - 1)


def depth_at_slots(h_ref, index, cell):
    major, minor = cell_parts(cell)
    found = []
    for v in range(3):
        key = major[8 * v : 8 * v + 8]
        lane = minor[8 * v : 8 * v + 8]
        depth = jnp.zeros((8, LANES), jnp.float32)
        for quad in range(QUADS):
            for row in range(ROWS):
                values = h_ref[index + (slice(row, row + 1), slice(quad * LANES, (quad + 1) * LANES))]
                values = jnp.broadcast_to(values, (8, LANES))
                depth = jnp.where(key == quad * ROWS + row, lane_gather(values, lane), depth)
        found.append(depth)
    return jnp.concatenate(found, axis=0)


def level_at_sites(reach_rows, site):
    found = []
    for v in range(3):
        sites = site[8 * v : 8 * v + 8]
        field = sites >> 7
        station = sites & (LANES - 1)
        level = jnp.zeros((8, LANES), jnp.float32)
        for f in range(FIELDS):
            level = jnp.where(field == f, lane_gather(reach_rows(f, v), station), level)
        found.append(level)
    return jnp.concatenate(found, axis=0)


def edge_columns(cells):
    left = column_to_lane(cells[0][:, 0:1], 0)
    right = column_to_lane(cells[0][:, COLS - 1 : COLS], 0)
    for k in (1, 2):
        left = left + column_to_lane(cells[k][:, 0:1], k * ROWS)
        right = right + column_to_lane(cells[k][:, COLS - 1 : COLS], k * ROWS)
    return left, right


def put_edges(beside_ref, across_ref, cells, even, start):
    for k in range(3):
        first = cells[k][0:1]
        last = cells[k][ROWS - 1 : ROWS]
        inner = jnp.where(even, last, first)
        outer = jnp.where(even, first, last)
        for quad in range(QUADS):
            at = start + k * QUADS + quad
            lanes = slice(quad * LANES, (quad + 1) * LANES)
            beside_ref[at : at + 1, :] = inner[:, lanes]
            across_ref[at : at + 1, :] = outer[:, lanes]


def get_edges(got_ref, near_ref, over_ref, cells, spot, start, col_row):
    even, y, is_first, is_last = spot
    before = got_ref[jnp.maximum(y - 1, 0), col_row : col_row + 1, :]
    after = got_ref[jnp.minimum(y + 1, BASINS - 1), col_row : col_row + 1, :]

    def edge(ref, k):
        rows = [ref[start + k * QUADS + q : start + k * QUADS + q + 1, :] for q in range(QUADS)]
        return jnp.concatenate(rows, axis=1)

    top, low, left, right = [], [], [], []
    for k in range(3):
        inner = edge(near_ref, k)
        outer = edge(over_ref, k)
        top.append(jnp.where(is_first, cells[k][0:1], jnp.where(even, outer, inner)))
        low.append(jnp.where(is_last, cells[k][ROWS - 1 : ROWS], jnp.where(even, inner, outer)))
        left.append(jnp.where(y == 0, cells[k][:, 0:1], lane_to_column(before, ROWS, k * ROWS)))
        right.append(
            jnp.where(
                y == BASINS - 1, cells[k][:, COLS - 1 : COLS], lane_to_column(after, ROWS, k * ROWS)
            )
        )
    return top, low, left, right


def inflow_of(own, outlets):
    row = jnp.sum(own[16:24] * outlets, axis=0, keepdims=True)
    return own[8:16, 0:1] + lane_to_column(row, FIELDS, 0)


def river_update(current, inflow, rate, lateral):
    lane = iota((FIELDS, LANES), 1)
    sub = iota((FIELDS, LANES), 0)
    behind = jnp.where(lane == 0, inflow, pltpu.roll(current, 1, 1))
    above = jnp.where(sub == FIELDS - 1, current, pltpu.roll(current, FIELDS - 1, 0))
    below = jnp.where(sub == 0, current, pltpu.roll(current, 1, 0))
    mixing = above - 2.0 * current + below
    return current - rate * (current - behind) + NU * mixing - (DT * RATIO) * lateral


def owned_terms(celerity, base_inflow, upstream, y):
    square = iota((FIELDS, FIELDS), 0) == iota((FIELDS, FIELDS), 1)

    def by_field(ref):
        row = jnp.broadcast_to(own_row(ref[...], y), (FIELDS, FIELDS))
        return jnp.sum(jnp.where(square, row, 0.0), axis=1, keepdims=True)

    feeders = own_row(upstream[...].astype(jnp.float32), y)
    ids = ((lax.axis_index("gx") - 1) * BASINS + iota((BASINS, feeders.shape[1]), 0)).astype(jnp.float32)
    hits = jnp.where(jnp.broadcast_to(feeders, ids.shape) == ids, 1.0, 0.0)
    weight = jnp.sum(hits, axis=1, keepdims=True)
    return jnp.concatenate(
        [jnp.broadcast_to(column, (8, LANES)) for column in (by_field(celerity), by_field(base_inflow), weight)],
        axis=0,
    )


def place():
    gx = lax.axis_index("gx")
    return (gx & 1) == 0, lax.axis_index("gy"), gx == 0, gx == lax.axis_size("gx") - 1


def first_kernel(*refs):
    count = len(refs) - 1
    sources, held, arrived = refs[:6], refs[count - 6 : count], refs[count]
    copies = [
        pltpu.make_async_copy(source, target, arrived.at[i])
        for i, (source, target) in enumerate(zip(sources, held))
    ]
    for copy in copies:
        copy.start()
    first_body(copies, *held, *refs[6 : count - 6])


def first_body(
    copies,
    depth,
    discharge,
    cell_in,
    site_in,
    coeff_in,
    reach,
    beside_ref,
    across_ref,
    mine_ref,
    cell_ref,
    site_ref,
    coeff_ref,
    slots_ref,
):
    even = place()[0]

    def arranged(ref):
        low, own, high = ref[0:8], ref[8:16], ref[16:24]
        return jnp.concatenate([own, jnp.where(even, high, low), jnp.where(even, low, high)], axis=0)

    copies[0].wait()
    copies[2].wait()
    bank = arranged(cell_in)
    cell = jnp.maximum(bank, 0)
    cell_ref[...] = cell
    slots = depth_at_slots(depth, (), cell)
    slots_ref[...] = slots
    for i in (1, 3, 4, 5):
        copies[i].wait()
    site = arranged(site_in)
    coeff = jnp.where(bank >= 0, arranged(coeff_in), 0.0)
    site_ref[...] = site
    coeff_ref[...] = coeff
    for at, value in enumerate((slots, site.astype(jnp.float32), coeff)):
        for v, ref in enumerate((mine_ref, beside_ref, across_ref)):
            ref[8 * at : 8 * at + 8] = value[8 * v : 8 * v + 8]
    cells = [depth[...], discharge[0], discharge[1]]
    mine_ref[24:32] = jnp.zeros((8, LANES), jnp.float32)
    left, right = edge_columns(cells)
    mine_ref[24:25] = left
    mine_ref[25:26] = right
    for ref in (beside_ref, across_ref):
        ref[FIRST_EDGE:FIRST_LEVELS] = jnp.zeros((FIRST_LEVELS - FIRST_EDGE, LANES), jnp.float32)
        for f in range(FIELDS):
            at = FIRST_LEVELS + 8 * f
            ref[at : at + 8] = reach[:, f * LANES : (f + 1) * LANES]
    put_edges(beside_ref, across_ref, cells, even, FIRST_EDGE)


def column_for(mine, b, start):
    y = lax.axis_index("gy")
    left = mine[start : start + 1]
    right = mine[start + 1 : start + 2]
    return jnp.where(b == y - 1, left, jnp.where(b == y + 1, right, 0.0))


def first_pack(mine, near, over, send):
    refs = (mine, near, over)
    for b in range(BASINS):
        for v, ref in enumerate(refs):
            send[b, v : v + 1] = ref[b : b + 1]
            send[b, 3 + v : 4 + v] = ref[16 + b : 17 + b]
            send[b, 8 + 8 * v : 16 + 8 * v] = ref[8:16]
        send[b, 6:7] = column_for(mine, b, 24)
        send[b, 7:8] = jnp.zeros((1, LANES), jnp.float32)


def pack(mine, near, over, send):
    even = place()[0]
    outlet = jnp.where(even, over[OUTLET : OUTLET + 1], near[OUTLET : OUTLET + 1])
    refs = (mine, near, over)
    for b in range(BASINS):
        for v, ref in enumerate(refs):
            send[b, v : v + 1] = ref[b : b + 1]
            send[b, 3 + v : 4 + v] = ref[8 + b : 9 + b]
        send[b, 6:7] = column_for(mine, b, 16)
        send[b, 7:8] = outlet


def last_pack(mine, near, over, send):
    even = place()[0]
    outlet = jnp.where(even, over[OUTLET : OUTLET + 1], near[OUTLET : OUTLET + 1])
    refs = (mine, near, over)
    for b in range(BASINS):
        for v, ref in enumerate(refs):
            send[b, 3 + v : 4 + v] = ref[8 + b : 9 + b]
            send[b, 8 + 8 * v : 16 + 8 * v] = ref[0:8]
            send[b, v : v + 1] = jnp.zeros((1, LANES), jnp.float32)
        send[b, 6:7] = column_for(mine, b, 16)
        send[b, 7:8] = outlet
        send[b, 32:40] = mine[24:32]


def gathered(got, row):
    return jnp.concatenate([got[:, row + v, :] for v in range(3)], axis=0)


def advance_levels(current, outlets, own, site_owner, coeff_owner, segment_owner, slots_owner):
    rates = coeff_owner * (segment_owner - slots_owner)
    lateral = spread(rates, site_owner >> 7, site_owner & (LANES - 1), FIELDS)
    return river_update(current, inflow_of(own, outlets), own[0:8], lateral)


def advance_cells(base, edges, cell, coeff, segment, slots):
    major, minor = cell_parts(cell)
    rates = coeff * (segment - slots)
    blocks = spread_cells(rates, major, minor)
    source = jnp.concatenate([blocks[q * ROWS : (q + 1) * ROWS] for q in range(QUADS)], axis=1)
    return flood_finish([base[0], base[1], base[2]], edges, source)


def first_flow(depth, discharge, rough, celerity, base_inflow, upstream, base, terms):
    new = flood_base([depth[...], discharge[0], discharge[1]], rough[...])
    for k in range(3):
        base[k] = new[k]
    for b in range(BASINS):
        terms[b] = owned_terms(celerity, base_inflow, upstream, b)


def flow(state, rough, base):
    new = flood_base([state[0], state[1], state[2]], rough[...])
    for k in range(3):
        base[k] = new[k]


def flow_and_total(state, rough, owner_coeff, owner_site, base, total):
    flow(state, rough, base)
    site = owner_site[...]
    total[...] = spread(owner_coeff[...], site >> 7, site & (LANES - 1), FIELDS)


def last_kernel(
    state, got, near, over, base, cell_ref, coeff_ref, slots_ref, got_first, terms, state_out, reach_out
):
    cells = [state[0], state[1], state[2]]
    edges = get_edges(got, near, over, cells, place(), EDGE, 6)
    new = advance_cells(
        base, edges, cell_ref[...], coeff_ref[...], gathered(got, 3), slots_ref[...]
    )
    for k in range(3):
        state_out[k] = new[k]
    outlets = got[:, 7, :]
    lane = iota((FIELDS, LANES), 1)
    for b in range(BASINS):
        own = terms[b]
        site = jnp.concatenate([got_first[:, 8 + 8 * v + b, :] for v in range(3)], axis=0)
        site = site.astype(jnp.int32)
        held = jnp.concatenate([got[:, 8 + 8 * v + b, :] for v in range(3)], axis=0)
        drawn = spread(held, site >> 7, site & (LANES - 1), FIELDS)
        entering = jnp.where(lane == 0, own[0:8] * inflow_of(own, outlets), 0.0)
        level = got[b, 32:40, :] + entering + (DT * RATIO) * drawn
        for f in range(FIELDS):
            reach_out[b : b + 1, f * LANES : (f + 1) * LANES] = level[f : f + 1]


def step_kernel(first, tail, *refs):
    refs = list(refs)

    def take(n):
        taken = refs[:n]
        del refs[:n]
        return taken

    if first:
        depth, discharge, reach, site_ref, terms = take(5)
    else:
        state, levels, owner_levels, owner_site, owner_coeff, own_ref = take(6)
    got, near, over, base, cell_ref, coeff_ref, slots_ref = take(7)
    if tail:
        (total,) = take(1)
    state_out, slots_out, beside_ref, across_ref, mine_ref = take(5)
    if not tail:
        levels_out, owner_levels_out = take(2)
    if first:
        owner_site_out, owner_coeff_out, own_out = take(3)
    spot = place()
    even, y = spot[0], spot[1]
    cell = cell_ref[...]

    slots_owner = gathered(got, 0)
    if first:
        cells = [depth[...], discharge[0], discharge[1]]
        current = jnp.concatenate(
            [own_row(reach[:, f * LANES : (f + 1) * LANES], y) for f in range(FIELDS)], axis=0
        )

        def tile_rows(f, v):
            if v == 0:
                return reach[:, f * LANES : (f + 1) * LANES]
            return (near if v == 1 else over)[FIRST_LEVELS + 8 * f : FIRST_LEVELS + 8 * f + 8, :]

        segment = level_at_sites(tile_rows, site_ref[...])
        site_owner = jnp.concatenate([got[:, 8 + 8 * v + y, :] for v in range(3)], axis=0)
        site_owner = site_owner.astype(jnp.int32)
        coeff_owner = gathered(got, 3)
        outlets = jnp.zeros((BASINS, LANES), jnp.float32)
        for f in range(FIELDS):
            source_rows = jnp.where(even, tile_rows(f, 2), tile_rows(f, 1))
            outlets = jnp.where(
                iota((BASINS, LANES), 1) == f, source_rows[:, LANES - 1 : LANES], outlets
            )
        segment_owner = level_at_sites(
            lambda f, v: jnp.broadcast_to(current[f : f + 1], (8, LANES)), site_owner
        )
        own = terms[y]
        owner_site_out[...] = site_owner
        owner_coeff_out[...] = coeff_owner
        own_out[...] = own
    else:
        cells = [state[0], state[1], state[2]]
        current = levels[...]
        segment = gathered(got, 3)
        site_owner = owner_site[...]
        coeff_owner = owner_coeff[...]
        segment_owner = owner_levels[...]
        outlets = got[:, 7, :]
        own = own_ref[...]

    levels_next = advance_levels(
        current, outlets, own, site_owner, coeff_owner, segment_owner, slots_owner
    )
    edges = get_edges(got, near, over, cells, spot, FIRST_EDGE if first else EDGE, 6)
    new = advance_cells(base, edges, cell, coeff_ref[...], segment, slots_ref[...])
    for k in range(3):
        state_out[k] = new[k]
    owned = level_at_sites(
        lambda f, v: jnp.broadcast_to(levels_next[f : f + 1], (8, LANES)), site_owner
    )
    if not tail:
        levels_out[...] = levels_next
        owner_levels_out[...] = owned
    slots = depth_at_slots(state_out, (0,), cell)
    slots_out[...] = slots
    if tail:
        slots = slots * coeff_ref[...]
    blank = jnp.zeros((8, LANES), jnp.float32)
    outlet_row = column_to_lane(levels_next[:, LANES - 1 : LANES], 0)
    for v, ref in enumerate((mine_ref, beside_ref, across_ref)):
        ref[0:8] = slots[8 * v : 8 * v + 8]
        ref[8:16] = owned[8 * v : 8 * v + 8]
        ref[16:24] = blank
        if v > 0:
            ref[OUTLET : OUTLET + 1] = outlet_row
            ref[EDGE : EDGE + 8] = blank
            ref[EDGE + 8 : EDGE + 16] = blank
    left, right = edge_columns(new)
    mine_ref[16:17] = left
    mine_ref[17:18] = right
    put_edges(beside_ref, across_ref, new, even, EDGE)
    if tail:
        none = jnp.zeros((FIELDS, 1), jnp.float32)
        mine_ref[24:32] = river_update(levels_next, none, own[0:8], total[...] * levels_next)
    else:
        mine_ref[24:32] = blank


def call(kernel, outs, args, limit=16 << 20):
    return pl.pallas_call(
        kernel,
        out_shape=outs,
        in_specs=[pl.BlockSpec(memory_space=pltpu.VMEM) for _ in args],
        out_specs=[pl.BlockSpec(memory_space=pltpu.VMEM) for _ in outs],
        compiler_params=None if INTERPRET else pltpu.CompilerParams(vmem_limit_bytes=limit),
        interpret=INTERPRET,
    )(*args)


def f32(*shape):
    return jax.ShapeDtypeStruct(shape, jnp.float32)


def i32(*shape):
    return jax.ShapeDtypeStruct(shape, jnp.int32)


def per_device(
    depth,
    discharge,
    roughness,
    reach_state,
    celerity,
    base_inflow,
    upstream,
    bank_cell,
    bank_site,
    bank_coeff,
):
    count_x = lax.axis_size("gx")
    chip = [(i, i ^ 1) for i in range(count_x)]
    border = [(i, i + 1) for i in range(1, count_x - 1, 2)]
    border = border + [(b, a) for a, b in border]

    def exchange(kernel, rows, beside, across, mine, ready):
        across, beside = lax.optimization_barrier((across, beside))
        over = lax.ppermute(across, "gx", border)
        near = lax.ppermute(beside, "gx", chip)
        near, over = lax.optimization_barrier((near, over))
        send = call(kernel, [f32(BASINS, rows, LANES)], [mine, near, over])[0]
        send, ready = lax.optimization_barrier((send, ready))
        return lax.all_to_all(send, "gy", 0, 0), near, over, ready

    table = (SLOT_ROWS, LANES)
    outs = [
        f32(FIRST_SWAP, LANES),
        f32(FIRST_SWAP, LANES),
        f32(32, LANES),
        i32(*table),
        i32(*table),
        f32(*table),
        f32(*table),
    ]
    inputs = [depth, discharge, bank_cell, bank_site, bank_coeff, reach_state]
    inputs = [pltpu.with_memory_space_constraint(x, pltpu.HBM) for x in inputs]
    beside, across, mine, cell, site, coeff, slots = pl.pallas_call(
        first_kernel,
        out_shape=outs,
        in_specs=[pl.BlockSpec(memory_space=pltpu.HBM) for _ in inputs],
        out_specs=[pl.BlockSpec(memory_space=pltpu.VMEM) for _ in outs],
        scratch_shapes=[pltpu.VMEM(x.shape, x.dtype) for x in inputs]
        + [pltpu.SemaphoreType.DMA((len(inputs),))],
        compiler_params=None if INTERPRET else pltpu.CompilerParams(vmem_limit_bytes=16 << 20),
        interpret=pltpu.InterpretParams() if INTERPRET else False,
    )(*inputs)
    base, terms = call(
        first_flow,
        [f32(3, ROWS, COLS), f32(BASINS, 24, LANES)],
        [depth, discharge, roughness, celerity, base_inflow, upstream],
    )
    got, near, over, (base, terms) = exchange(first_pack, 32, beside, across, mine, (base, terms))
    got_first = got
    for step in range(STEPS - 1):
        first, tail = step == 0, step == STEPS - 2
        outs = [
            f32(3, ROWS, COLS),
            f32(*table),
            f32(SWAP, LANES),
            f32(SWAP, LANES),
            f32(32, LANES),
        ]
        if not tail:
            outs += [f32(FIELDS, LANES), f32(*table)]
        if first:
            outs += [i32(*table), f32(*table), f32(*table)]
            args = [depth, discharge, reach_state, site, terms]
        else:
            args = [state, levels, owner_levels, owner_site, owner_coeff, own]
        args += [got, near, over, base, cell, coeff, slots]
        if tail:
            args += [total]
        result = call(functools.partial(step_kernel, first, tail), outs, args)
        state, slots, beside, across, mine = result[:5]
        if not tail:
            levels, owner_levels = result[5:7]
        if first:
            owner_site, owner_coeff, own = result[7:10]
        if first:
            base, total = call(
                flow_and_total,
                [f32(3, ROWS, COLS), f32(FIELDS, LANES)],
                [state, roughness, owner_coeff, owner_site],
            )
        else:
            base = call(flow, [f32(3, ROWS, COLS)], [state, roughness])[0]
        got, near, over, base = exchange(
            last_pack if tail else pack, 40 if tail else BASINS, beside, across, mine, base
        )
    state, reach = call(
        last_kernel,
        [f32(3, ROWS, COLS), f32(BASINS, FIELDS * LANES)],
        [state, got, near, over, base, cell, coeff, slots, got_first, terms],
    )
    return state, reach


def solution(mesh):
    return jax.shard_map(
        per_device,
        mesh=mesh,
        in_specs=(
            P("gx", "gy"),
            P(None, "gx", "gy"),
            P("gx", "gy"),
            P("gx", None),
            P("gx", None),
            P("gx", None),
            P("gx", None),
            P("gx", "gy"),
            P("gx", "gy"),
            P("gx", "gy"),
        ),
        out_specs=(P(None, "gx", "gy"), P("gx", None)),
        check_vma=False,
    )
```

```python
import functools

import jax
import jax.numpy as jnp
from jax import lax
from jax.experimental import pallas as pl
from jax.experimental.pallas import tpu as pltpu
from jax.sharding import PartitionSpec as P

STEPS = 4


GRAV = 9.81
DT = 0.5
DX = 10.0
NU = 0.1
RATIO = 0.25
FACTOR = DT / (2.0 * DX)

LANES = 128
ROWS = 32
QUADS = 4
COLS = QUADS * LANES
FIELDS = 8
BASINS = 8
SLOT_ROWS = 3 * BASINS
INTERPRET = False

FIRST_EDGE = 24
FIRST_LEVELS = 40
FIRST_SWAP = FIRST_LEVELS + FIELDS * BASINS
OUTLET = 16
EDGE = 24
SWAP = 40


def iota(shape, dim):
    return lax.broadcasted_iota(jnp.int32, shape, dim)


def lane_gather(rows, index):
    return jnp.take_along_axis(rows, index, axis=1, mode="promise_in_bounds")


def lane_to_column(row, count, offset):
    wide = jnp.broadcast_to(row, (count, LANES))
    hit = iota((count, LANES), 1) == iota((count, LANES), 0) + offset
    return jnp.sum(jnp.where(hit, wide, 0.0), axis=1, keepdims=True)


def column_to_lane(column, offset):
    count = column.shape[0]
    wide = jnp.broadcast_to(column, (count, LANES))
    hit = iota((count, LANES), 1) == iota((count, LANES), 0) + offset
    return jnp.sum(jnp.where(hit, wide, 0.0), axis=0, keepdims=True)


def own_row(block, y):
    return jnp.sum(jnp.where(iota(block.shape, 0) == y, block, 0.0), axis=0, keepdims=True)


def flux_terms(cells):
    h, p, q = cells
    inverse = 1.0 / h
    u = p * inverse
    v = q * inverse
    pressure = 0.5 * GRAV * h * h
    return (p, p * u + pressure, q * u), (q, p * v, q * v + pressure), u, v


def flood_base(cells, rough):
    flux_x, flux_y, u, v = flux_terms(cells)
    row = iota((ROWS, COLS), 0)
    col = iota((ROWS, COLS), 1)
    out = []
    for k in range(3):
        quarter = 0.25 * cells[k]
        from_top = jnp.where(row == 0, 0.0, pltpu.roll(quarter + FACTOR * flux_x[k], 1, 0))
        from_low = jnp.where(row == ROWS - 1, 0.0, pltpu.roll(quarter - FACTOR * flux_x[k], ROWS - 1, 0))
        from_left = jnp.where(col == 0, 0.0, pltpu.roll(quarter + FACTOR * flux_y[k], 1, 1))
        from_right = jnp.where(col == COLS - 1, 0.0, pltpu.roll(quarter - FACTOR * flux_y[k], COLS - 1, 1))
        out.append((from_top + from_low) + (from_left + from_right))
    h = cells[0]
    size = jnp.abs(h)
    root = jnp.exp(jnp.log(size) * (-1.0 / 3.0))
    root = root * (4.0 - size * (root * root * root)) * (1.0 / 3.0)
    root = jnp.where(h < 0.0, -root, root)
    drag = (GRAV * DT) * rough * rough * jnp.sqrt(u * u + v * v) * root
    return [out[0], out[1] - drag * u, out[2] - drag * v]


def flood_finish(base, edges, source):
    top, low, left, right = edges
    top_x = flux_terms(top)[0]
    low_x = flux_terms(low)[0]
    left_y = flux_terms(left)[1]
    right_y = flux_terms(right)[1]
    first_row = iota((8, COLS), 0) == 0
    last_row = iota((8, COLS), 0) == 7
    first_col = iota((ROWS, LANES), 1) == 0
    last_col = iota((ROWS, LANES), 1) == LANES - 1
    out = []
    for k in range(3):
        cells = base[k]
        upper = cells[0:8] + jnp.where(first_row, 0.25 * top[k] + FACTOR * top_x[k], 0.0)
        lower = cells[ROWS - 8 : ROWS] + jnp.where(last_row, 0.25 * low[k] - FACTOR * low_x[k], 0.0)
        cells = jnp.concatenate([upper, cells[8 : ROWS - 8], lower], axis=0)
        west = cells[:, :LANES] + jnp.where(first_col, 0.25 * left[k] + FACTOR * left_y[k], 0.0)
        east = cells[:, COLS - LANES :] + jnp.where(last_col, 0.25 * right[k] - FACTOR * right_y[k], 0.0)
        out.append(jnp.concatenate([west, cells[:, LANES : COLS - LANES], east], axis=1))
    out[0] = out[0] + DT * source
    return out


def halves(values):
    high = values.astype(jnp.bfloat16).astype(jnp.float32)
    return high, values - high


def spread(rates, major, minor, count):
    total = None
    rows = rates.shape[0]
    group = 4
    high, low = halves(rates)
    for start in range(0, rows, group):
        left, right = [], []
        for r in range(start, start + group):
            at = iota((count, LANES), 0) == major[r : r + 1]
            left.append(
                jnp.concatenate(
                    [
                        jnp.where(at, high[r : r + 1], 0.0),
                        jnp.where(at, low[r : r + 1], 0.0),
                    ],
                    axis=0,
                ).astype(jnp.bfloat16)
            )
            right.append(
                jnp.where(iota((LANES, LANES), 0) == minor[r : r + 1], 1.0, 0.0).astype(jnp.bfloat16)
            )
        part = lax.dot_general(
            jnp.concatenate(left, axis=1),
            jnp.concatenate(right, axis=1),
            (((1,), (1,)), ((), ())),
            preferred_element_type=jnp.float32,
        )
        total = part if total is None else total + part
    return total[:count] + total[count:]


def repeated(row, count):
    tile = jnp.broadcast_to(row, (16, LANES)).astype(jnp.bfloat16)
    return jnp.concatenate([tile] * (count // 16), axis=0)


def spread_cells(rates, major, minor):
    high, low = halves(rates)
    major = major.astype(jnp.float32)
    minor = minor.astype(jnp.float32)
    row = iota((LANES, LANES), 0).astype(jnp.float32).astype(jnp.bfloat16)
    zero = jnp.zeros((), jnp.bfloat16)
    one = jnp.ones((), jnp.bfloat16)
    total = None
    group = 4
    for start in range(0, rates.shape[0], group):
        left, right = [], []
        for r in range(start, start + group):
            at = row == repeated(major[r : r + 1], LANES)
            left.append(
                jnp.concatenate(
                    [jnp.where(at, repeated(part[r : r + 1], LANES), zero) for part in (high, low)], axis=0
                )
            )
            right.append(jnp.where(row == repeated(minor[r : r + 1], LANES), one, zero))
        part = lax.dot_general(
            jnp.concatenate(left, axis=1),
            jnp.concatenate(right, axis=1),
            (((1,), (1,)), ((), ())),
            preferred_element_type=jnp.float32,
        )
        total = part if total is None else total + part
    return total[:LANES] + total[LANES:]


def cell_parts(cell):
    col = cell & (COLS - 1)
    return (col >> 7) * ROWS + (cell >> 9), col & (LANES - 1)


def depth_at_slots(h_ref, index, cell):
    major, minor = cell_parts(cell)
    found = []
    for v in range(3):
        key = major[8 * v : 8 * v + 8]
        lane = minor[8 * v : 8 * v + 8]
        depth = jnp.zeros((8, LANES), jnp.float32)
        for quad in range(QUADS):
            for row in range(ROWS):
                values = h_ref[index + (slice(row, row + 1), slice(quad * LANES, (quad + 1) * LANES))]
                values = jnp.broadcast_to(values, (8, LANES))
                depth = jnp.where(key == quad * ROWS + row, lane_gather(values, lane), depth)
        found.append(depth)
    return jnp.concatenate(found, axis=0)


def level_at_sites(reach_rows, site):
    found = []
    for v in range(3):
        sites = site[8 * v : 8 * v + 8]
        field = sites >> 7
        station = sites & (LANES - 1)
        level = jnp.zeros((8, LANES), jnp.float32)
        for f in range(FIELDS):
            level = jnp.where(field == f, lane_gather(reach_rows(f, v), station), level)
        found.append(level)
    return jnp.concatenate(found, axis=0)


def edge_columns(cells):
    left = column_to_lane(cells[0][:, 0:1], 0)
    right = column_to_lane(cells[0][:, COLS - 1 : COLS], 0)
    for k in (1, 2):
        left = left + column_to_lane(cells[k][:, 0:1], k * ROWS)
        right = right + column_to_lane(cells[k][:, COLS - 1 : COLS], k * ROWS)
    return left, right


def put_edges(beside_ref, across_ref, cells, even, start):
    for k in range(3):
        first = cells[k][0:1]
        last = cells[k][ROWS - 1 : ROWS]
        inner = jnp.where(even, last, first)
        outer = jnp.where(even, first, last)
        for quad in range(QUADS):
            at = start + k * QUADS + quad
            lanes = slice(quad * LANES, (quad + 1) * LANES)
            beside_ref[at : at + 1, :] = inner[:, lanes]
            across_ref[at : at + 1, :] = outer[:, lanes]


def get_edges(got_ref, near_ref, over_ref, cells, spot, start, col_row):
    even, y, is_first, is_last = spot
    before = got_ref[jnp.maximum(y - 1, 0), col_row : col_row + 1, :]
    after = got_ref[jnp.minimum(y + 1, BASINS - 1), col_row : col_row + 1, :]

    def edge(ref, k):
        rows = [ref[start + k * QUADS + q : start + k * QUADS + q + 1, :] for q in range(QUADS)]
        return jnp.concatenate(rows, axis=1)

    top, low, left, right = [], [], [], []
    for k in range(3):
        inner = edge(near_ref, k)
        outer = edge(over_ref, k)
        top.append(jnp.where(is_first, cells[k][0:1], jnp.where(even, outer, inner)))
        low.append(jnp.where(is_last, cells[k][ROWS - 1 : ROWS], jnp.where(even, inner, outer)))
        left.append(jnp.where(y == 0, cells[k][:, 0:1], lane_to_column(before, ROWS, k * ROWS)))
        right.append(
            jnp.where(
                y == BASINS - 1, cells[k][:, COLS - 1 : COLS], lane_to_column(after, ROWS, k * ROWS)
            )
        )
    return top, low, left, right


def inflow_of(own, outlets):
    row = jnp.sum(own[16:24] * outlets, axis=0, keepdims=True)
    return own[8:16, 0:1] + lane_to_column(row, FIELDS, 0)


def river_update(current, inflow, rate, lateral):
    lane = iota((FIELDS, LANES), 1)
    sub = iota((FIELDS, LANES), 0)
    behind = jnp.where(lane == 0, inflow, pltpu.roll(current, 1, 1))
    above = jnp.where(sub == FIELDS - 1, current, pltpu.roll(current, FIELDS - 1, 0))
    below = jnp.where(sub == 0, current, pltpu.roll(current, 1, 0))
    mixing = above - 2.0 * current + below
    return current - rate * (current - behind) + NU * mixing - (DT * RATIO) * lateral


def owned_terms(celerity, base_inflow, upstream, y):
    square = iota((FIELDS, FIELDS), 0) == iota((FIELDS, FIELDS), 1)

    def by_field(ref):
        row = jnp.broadcast_to(own_row(ref[...], y), (FIELDS, FIELDS))
        return jnp.sum(jnp.where(square, row, 0.0), axis=1, keepdims=True)

    feeders = own_row(upstream[...].astype(jnp.float32), y)
    ids = ((lax.axis_index("gx") - 1) * BASINS + iota((BASINS, feeders.shape[1]), 0)).astype(jnp.float32)
    hits = jnp.where(jnp.broadcast_to(feeders, ids.shape) == ids, 1.0, 0.0)
    weight = jnp.sum(hits, axis=1, keepdims=True)
    return jnp.concatenate(
        [jnp.broadcast_to(column, (8, LANES)) for column in (by_field(celerity), by_field(base_inflow), weight)],
        axis=0,
    )


def place():
    gx = lax.axis_index("gx")
    return (gx & 1) == 0, lax.axis_index("gy"), gx == 0, gx == lax.axis_size("gx") - 1


def first_kernel(*refs):
    count = len(refs) - 1
    sources, held, arrived = refs[:6], refs[count - 6 : count], refs[count]
    copies = [
        pltpu.make_async_copy(source, target, arrived.at[i])
        for i, (source, target) in enumerate(zip(sources, held))
    ]
    for copy in copies:
        copy.start()
    first_body(copies, *held, *refs[6 : count - 6])


def first_body(
    copies,
    depth,
    discharge,
    cell_in,
    site_in,
    coeff_in,
    reach,
    beside_ref,
    across_ref,
    mine_ref,
    cell_ref,
    site_ref,
    coeff_ref,
    slots_ref,
):
    even = place()[0]

    def arranged(ref):
        low, own, high = ref[0:8], ref[8:16], ref[16:24]
        return jnp.concatenate([own, jnp.where(even, high, low), jnp.where(even, low, high)], axis=0)

    copies[0].wait()
    copies[2].wait()
    bank = arranged(cell_in)
    cell = jnp.maximum(bank, 0)
    cell_ref[...] = cell
    slots = depth_at_slots(depth, (), cell)
    slots_ref[...] = slots
    for i in (1, 3, 4, 5):
        copies[i].wait()
    site = arranged(site_in)
    coeff = jnp.where(bank >= 0, arranged(coeff_in), 0.0)
    site_ref[...] = site
    coeff_ref[...] = coeff
    for at, value in enumerate((slots, site.astype(jnp.float32), coeff)):
        for v, ref in enumerate((mine_ref, beside_ref, across_ref)):
            ref[8 * at : 8 * at + 8] = value[8 * v : 8 * v + 8]
    cells = [depth[...], discharge[0], discharge[1]]
    mine_ref[24:32] = jnp.zeros((8, LANES), jnp.float32)
    left, right = edge_columns(cells)
    mine_ref[24:25] = left
    mine_ref[25:26] = right
    for ref in (beside_ref, across_ref):
        ref[FIRST_EDGE:FIRST_LEVELS] = jnp.zeros((FIRST_LEVELS - FIRST_EDGE, LANES), jnp.float32)
        for f in range(FIELDS):
            at = FIRST_LEVELS + 8 * f
            ref[at : at + 8] = reach[:, f * LANES : (f + 1) * LANES]
    put_edges(beside_ref, across_ref, cells, even, FIRST_EDGE)


def column_for(mine, b, start):
    y = lax.axis_index("gy")
    left = mine[start : start + 1]
    right = mine[start + 1 : start + 2]
    return jnp.where(b == y - 1, left, jnp.where(b == y + 1, right, 0.0))


def first_pack(mine, near, over, send):
    refs = (mine, near, over)
    for b in range(BASINS):
        for v, ref in enumerate(refs):
            send[b, v : v + 1] = ref[b : b + 1]
            send[b, 3 + v : 4 + v] = ref[16 + b : 17 + b]
            send[b, 8 + 8 * v : 16 + 8 * v] = ref[8:16]
        send[b, 6:7] = column_for(mine, b, 24)
        send[b, 7:8] = jnp.zeros((1, LANES), jnp.float32)


def pack(mine, near, over, send):
    even = place()[0]
    outlet = jnp.where(even, over[OUTLET : OUTLET + 1], near[OUTLET : OUTLET + 1])
    refs = (mine, near, over)
    for b in range(BASINS):
        for v, ref in enumerate(refs):
            send[b, v : v + 1] = ref[b : b + 1]
            send[b, 3 + v : 4 + v] = ref[8 + b : 9 + b]
        send[b, 6:7] = column_for(mine, b, 16)
        send[b, 7:8] = outlet


def last_pack(mine, near, over, send):
    even = place()[0]
    outlet = jnp.where(even, over[OUTLET : OUTLET + 1], near[OUTLET : OUTLET + 1])
    refs = (mine, near, over)
    for b in range(BASINS):
        for v, ref in enumerate(refs):
            send[b, 3 + v : 4 + v] = ref[8 + b : 9 + b]
            send[b, 8 + 8 * v : 16 + 8 * v] = ref[0:8]
            send[b, v : v + 1] = jnp.zeros((1, LANES), jnp.float32)
        send[b, 6:7] = column_for(mine, b, 16)
        send[b, 7:8] = outlet
        send[b, 32:40] = mine[24:32]


def gathered(got, row):
    return jnp.concatenate([got[:, row + v, :] for v in range(3)], axis=0)


def advance_levels(current, outlets, own, site_owner, coeff_owner, segment_owner, slots_owner):
    rates = coeff_owner * (segment_owner - slots_owner)
    lateral = spread(rates, site_owner >> 7, site_owner & (LANES - 1), FIELDS)
    return river_update(current, inflow_of(own, outlets), own[0:8], lateral)


def advance_cells(base, edges, cell, coeff, segment, slots):
    major, minor = cell_parts(cell)
    rates = coeff * (segment - slots)
    blocks = spread_cells(rates, major, minor)
    source = jnp.concatenate([blocks[q * ROWS : (q + 1) * ROWS] for q in range(QUADS)], axis=1)
    return flood_finish([base[0], base[1], base[2]], edges, source)


def first_flow(depth, discharge, rough, celerity, base_inflow, upstream, base, terms):
    new = flood_base([depth[...], discharge[0], discharge[1]], rough[...])
    for k in range(3):
        base[k] = new[k]
    for b in range(BASINS):
        terms[b] = owned_terms(celerity, base_inflow, upstream, b)


def flow(state, rough, base):
    new = flood_base([state[0], state[1], state[2]], rough[...])
    for k in range(3):
        base[k] = new[k]


def flow_and_total(state, rough, owner_coeff, owner_site, base, total):
    flow(state, rough, base)
    site = owner_site[...]
    total[...] = spread(owner_coeff[...], site >> 7, site & (LANES - 1), FIELDS)


def last_kernel(
    state, got, near, over, base, cell_ref, coeff_ref, slots_ref, got_first, terms, state_out, reach_out
):
    cells = [state[0], state[1], state[2]]
    edges = get_edges(got, near, over, cells, place(), EDGE, 6)
    new = advance_cells(
        base, edges, cell_ref[...], coeff_ref[...], gathered(got, 3), slots_ref[...]
    )
    for k in range(3):
        state_out[k] = new[k]
    outlets = got[:, 7, :]
    lane = iota((FIELDS, LANES), 1)
    for b in range(BASINS):
        own = terms[b]
        site = jnp.concatenate([got_first[:, 8 + 8 * v + b, :] for v in range(3)], axis=0)
        site = site.astype(jnp.int32)
        held = jnp.concatenate([got[:, 8 + 8 * v + b, :] for v in range(3)], axis=0)
        drawn = spread(held, site >> 7, site & (LANES - 1), FIELDS)
        entering = jnp.where(lane == 0, own[0:8] * inflow_of(own, outlets), 0.0)
        level = got[b, 32:40, :] + entering + (DT * RATIO) * drawn
        for f in range(FIELDS):
            reach_out[b : b + 1, f * LANES : (f + 1) * LANES] = level[f : f + 1]


def step_kernel(first, tail, *refs):
    refs = list(refs)

    def take(n):
        taken = refs[:n]
        del refs[:n]
        return taken

    if first:
        depth, discharge, reach, site_ref, terms = take(5)
    else:
        state, levels, owner_levels, owner_site, owner_coeff, own_ref = take(6)
    got, near, over, base, cell_ref, coeff_ref, slots_ref = take(7)
    if tail:
        (total,) = take(1)
    state_out, slots_out, beside_ref, across_ref, mine_ref = take(5)
    if not tail:
        levels_out, owner_levels_out = take(2)
    if first:
        owner_site_out, owner_coeff_out, own_out = take(3)
    spot = place()
    even, y = spot[0], spot[1]
    cell = cell_ref[...]

    slots_owner = gathered(got, 0)
    if first:
        cells = [depth[...], discharge[0], discharge[1]]
        current = jnp.concatenate(
            [own_row(reach[:, f * LANES : (f + 1) * LANES], y) for f in range(FIELDS)], axis=0
        )

        def tile_rows(f, v):
            if v == 0:
                return reach[:, f * LANES : (f + 1) * LANES]
            return (near if v == 1 else over)[FIRST_LEVELS + 8 * f : FIRST_LEVELS + 8 * f + 8, :]

        segment = level_at_sites(tile_rows, site_ref[...])
        site_owner = jnp.concatenate([got[:, 8 + 8 * v + y, :] for v in range(3)], axis=0)
        site_owner = site_owner.astype(jnp.int32)
        coeff_owner = gathered(got, 3)
        outlets = jnp.zeros((BASINS, LANES), jnp.float32)
        for f in range(FIELDS):
            source_rows = jnp.where(even, tile_rows(f, 2), tile_rows(f, 1))
            outlets = jnp.where(
                iota((BASINS, LANES), 1) == f, source_rows[:, LANES - 1 : LANES], outlets
            )
        segment_owner = level_at_sites(
            lambda f, v: jnp.broadcast_to(current[f : f + 1], (8, LANES)), site_owner
        )
        own = terms[y]
        owner_site_out[...] = site_owner
        owner_coeff_out[...] = coeff_owner
        own_out[...] = own
    else:
        cells = [state[0], state[1], state[2]]
        current = levels[...]
        segment = gathered(got, 3)
        site_owner = owner_site[...]
        coeff_owner = owner_coeff[...]
        segment_owner = owner_levels[...]
        outlets = got[:, 7, :]
        own = own_ref[...]

    levels_next = advance_levels(
        current, outlets, own, site_owner, coeff_owner, segment_owner, slots_owner
    )
    edges = get_edges(got, near, over, cells, spot, FIRST_EDGE if first else EDGE, 6)
    new = advance_cells(base, edges, cell, coeff_ref[...], segment, slots_ref[...])
    for k in range(3):
        state_out[k] = new[k]
    owned = level_at_sites(
        lambda f, v: jnp.broadcast_to(levels_next[f : f + 1], (8, LANES)), site_owner
    )
    if not tail:
        levels_out[...] = levels_next
        owner_levels_out[...] = owned
    slots = depth_at_slots(state_out, (0,), cell)
    slots_out[...] = slots
    if tail:
        slots = slots * coeff_ref[...]
    blank = jnp.zeros((8, LANES), jnp.float32)
    outlet_row = column_to_lane(levels_next[:, LANES - 1 : LANES], 0)
    for v, ref in enumerate((mine_ref, beside_ref, across_ref)):
        ref[0:8] = slots[8 * v : 8 * v + 8]
        ref[8:16] = owned[8 * v : 8 * v + 8]
        ref[16:24] = blank
        if v > 0:
            ref[OUTLET : OUTLET + 1] = outlet_row
            ref[EDGE : EDGE + 8] = blank
            ref[EDGE + 8 : EDGE + 16] = blank
    left, right = edge_columns(new)
    mine_ref[16:17] = left
    mine_ref[17:18] = right
    put_edges(beside_ref, across_ref, new, even, EDGE)
    if tail:
        none = jnp.zeros((FIELDS, 1), jnp.float32)
        mine_ref[24:32] = river_update(levels_next, none, own[0:8], total[...] * levels_next)
    else:
        mine_ref[24:32] = blank


def call(kernel, outs, args, limit=16 << 20):
    return pl.pallas_call(
        kernel,
        out_shape=outs,
        in_specs=[pl.BlockSpec(memory_space=pltpu.VMEM) for _ in args],
        out_specs=[pl.BlockSpec(memory_space=pltpu.VMEM) for _ in outs],
        compiler_params=None if INTERPRET else pltpu.CompilerParams(vmem_limit_bytes=limit),
        interpret=INTERPRET,
    )(*args)


def f32(*shape):
    return jax.ShapeDtypeStruct(shape, jnp.float32)


def i32(*shape):
    return jax.ShapeDtypeStruct(shape, jnp.int32)


def per_device(
    depth,
    discharge,
    roughness,
    reach_state,
    celerity,
    base_inflow,
    upstream,
    bank_cell,
    bank_site,
    bank_coeff,
):
    count_x = lax.axis_size("gx")
    chip = [(i, i ^ 1) for i in range(count_x)]
    border = [(i, i + 1) for i in range(1, count_x - 1, 2)]
    border = border + [(b, a) for a, b in border]

    def exchange(kernel, rows, beside, across, mine, ready):
        across, beside = lax.optimization_barrier((across, beside))
        beside, ready = lax.optimization_barrier((beside, ready))
        near = lax.ppermute(beside, "gx", chip)
        over = lax.ppermute(across, "gx", border)
        over, near = lax.optimization_barrier((over, near))
        send = call(kernel, [f32(BASINS, rows, LANES)], [mine, near, over])[0]
        send, ready = lax.optimization_barrier((send, ready))
        return lax.all_to_all(send, "gy", 0, 0), near, over, ready

    table = (SLOT_ROWS, LANES)
    outs = [
        f32(FIRST_SWAP, LANES),
        f32(FIRST_SWAP, LANES),
        f32(32, LANES),
        i32(*table),
        i32(*table),
        f32(*table),
        f32(*table),
    ]
    inputs = [depth, discharge, bank_cell, bank_site, bank_coeff, reach_state]
    inputs = [pltpu.with_memory_space_constraint(x, pltpu.HBM) for x in inputs]
    beside, across, mine, cell, site, coeff, slots = pl.pallas_call(
        first_kernel,
        out_shape=outs,
        in_specs=[pl.BlockSpec(memory_space=pltpu.HBM) for _ in inputs],
        out_specs=[pl.BlockSpec(memory_space=pltpu.VMEM) for _ in outs],
        scratch_shapes=[pltpu.VMEM(x.shape, x.dtype) for x in inputs]
        + [pltpu.SemaphoreType.DMA((len(inputs),))],
        compiler_params=None if INTERPRET else pltpu.CompilerParams(vmem_limit_bytes=16 << 20),
        interpret=pltpu.InterpretParams() if INTERPRET else False,
    )(*inputs)
    base, terms = call(
        first_flow,
        [f32(3, ROWS, COLS), f32(BASINS, 24, LANES)],
        [depth, discharge, roughness, celerity, base_inflow, upstream],
    )
    got, near, over, (base, terms) = exchange(first_pack, 32, beside, across, mine, (base, terms))
    got_first = got
    for step in range(STEPS - 1):
        first, tail = step == 0, step == STEPS - 2
        outs = [
            f32(3, ROWS, COLS),
            f32(*table),
            f32(SWAP, LANES),
            f32(SWAP, LANES),
            f32(32, LANES),
        ]
        if not tail:
            outs += [f32(FIELDS, LANES), f32(*table)]
        if first:
            outs += [i32(*table), f32(*table), f32(*table)]
            args = [depth, discharge, reach_state, site, terms]
        else:
            args = [state, levels, owner_levels, owner_site, owner_coeff, own]
        args += [got, near, over, base, cell, coeff, slots]
        if tail:
            args += [total]
        result = call(functools.partial(step_kernel, first, tail), outs, args)
        state, slots, beside, across, mine = result[:5]
        if not tail:
            levels, owner_levels = result[5:7]
        if first:
            owner_site, owner_coeff, own = result[7:10]
        if first:
            base, total = call(
                flow_and_total,
                [f32(3, ROWS, COLS), f32(FIELDS, LANES)],
                [state, roughness, owner_coeff, owner_site],
            )
        else:
            base = call(flow, [f32(3, ROWS, COLS)], [state, roughness])[0]
        got, near, over, base = exchange(
            last_pack if tail else pack, 40 if tail else BASINS, beside, across, mine, base
        )
    state, reach = call(
        last_kernel,
        [f32(3, ROWS, COLS), f32(BASINS, FIELDS * LANES)],
        [state, got, near, over, base, cell, coeff, slots, got_first, terms],
    )
    return state, reach


def solution(mesh):
    return jax.shard_map(
        per_device,
        mesh=mesh,
        in_specs=(
            P("gx", "gy"),
            P(None, "gx", "gy"),
            P("gx", "gy"),
            P("gx", None),
            P("gx", None),
            P("gx", None),
            P("gx", None),
            P("gx", "gy"),
            P("gx", "gy"),
            P("gx", "gy"),
        ),
        out_specs=(P(None, "gx", "gy"), P("gx", None)),
        check_vma=False,
    )
```

```python
import functools

import jax
import jax.numpy as jnp
from jax import lax
from jax.experimental import pallas as pl
from jax.experimental.pallas import tpu as pltpu
from jax.sharding import PartitionSpec as P

STEPS = 4


GRAV = 9.81
DT = 0.5
DX = 10.0
NU = 0.1
RATIO = 0.25
FACTOR = DT / (2.0 * DX)

LANES = 128
ROWS = 32
QUADS = 4
COLS = QUADS * LANES
FIELDS = 8
BASINS = 8
SLOT_ROWS = 3 * BASINS
INTERPRET = False

FIRST_EDGE = 24
FIRST_LEVELS = 40
FIRST_SWAP = FIRST_LEVELS + FIELDS * BASINS
OUTLET = 16
EDGE = 24
SWAP = 40


def iota(shape, dim):
    return lax.broadcasted_iota(jnp.int32, shape, dim)


def lane_gather(rows, index):
    return jnp.take_along_axis(rows, index, axis=1, mode="promise_in_bounds")


def lane_to_column(row, count, offset):
    wide = jnp.broadcast_to(row, (count, LANES))
    hit = iota((count, LANES), 1) == iota((count, LANES), 0) + offset
    return jnp.sum(jnp.where(hit, wide, 0.0), axis=1, keepdims=True)


def column_to_lane(column, offset):
    count = column.shape[0]
    wide = jnp.broadcast_to(column, (count, LANES))
    hit = iota((count, LANES), 1) == iota((count, LANES), 0) + offset
    return jnp.sum(jnp.where(hit, wide, 0.0), axis=0, keepdims=True)


def own_row(block, y):
    return jnp.sum(jnp.where(iota(block.shape, 0) == y, block, 0.0), axis=0, keepdims=True)


def flux_terms(cells):
    h, p, q = cells
    inverse = 1.0 / h
    u = p * inverse
    v = q * inverse
    pressure = 0.5 * GRAV * h * h
    return (p, p * u + pressure, q * u), (q, p * v, q * v + pressure), u, v


def flood_base(cells, rough):
    flux_x, flux_y, u, v = flux_terms(cells)
    row = iota((ROWS, COLS), 0)
    col = iota((ROWS, COLS), 1)
    out = []
    for k in range(3):
        quarter = 0.25 * cells[k]
        from_top = jnp.where(row == 0, 0.0, pltpu.roll(quarter + FACTOR * flux_x[k], 1, 0))
        from_low = jnp.where(row == ROWS - 1, 0.0, pltpu.roll(quarter - FACTOR * flux_x[k], ROWS - 1, 0))
        from_left = jnp.where(col == 0, 0.0, pltpu.roll(quarter + FACTOR * flux_y[k], 1, 1))
        from_right = jnp.where(col == COLS - 1, 0.0, pltpu.roll(quarter - FACTOR * flux_y[k], COLS - 1, 1))
        out.append((from_top + from_low) + (from_left + from_right))
    h = cells[0]
    size = jnp.abs(h)
    root = jnp.exp(jnp.log(size) * (-1.0 / 3.0))
    root = root * (4.0 - size * (root * root * root)) * (1.0 / 3.0)
    root = jnp.where(h < 0.0, -root, root)
    drag = (GRAV * DT) * rough * rough * jnp.sqrt(u * u + v * v) * root
    return [out[0], out[1] - drag * u, out[2] - drag * v]


def flood_finish(base, edges, source):
    top, low, left, right = edges
    top_x = flux_terms(top)[0]
    low_x = flux_terms(low)[0]
    left_y = flux_terms(left)[1]
    right_y = flux_terms(right)[1]
    first_row = iota((8, COLS), 0) == 0
    last_row = iota((8, COLS), 0) == 7
    first_col = iota((ROWS, LANES), 1) == 0
    last_col = iota((ROWS, LANES), 1) == LANES - 1
    out = []
    for k in range(3):
        cells = base[k]
        upper = cells[0:8] + jnp.where(first_row, 0.25 * top[k] + FACTOR * top_x[k], 0.0)
        lower = cells[ROWS - 8 : ROWS] + jnp.where(last_row, 0.25 * low[k] - FACTOR * low_x[k], 0.0)
        cells = jnp.concatenate([upper, cells[8 : ROWS - 8], lower], axis=0)
        west = cells[:, :LANES] + jnp.where(first_col, 0.25 * left[k] + FACTOR * left_y[k], 0.0)
        east = cells[:, COLS - LANES :] + jnp.where(last_col, 0.25 * right[k] - FACTOR * right_y[k], 0.0)
        out.append(jnp.concatenate([west, cells[:, LANES : COLS - LANES], east], axis=1))
    out[0] = out[0] + DT * source
    return out


def halves(values):
    high = values.astype(jnp.bfloat16).astype(jnp.float32)
    return high, values - high


def spread(rates, major, minor, count):
    total = None
    rows = rates.shape[0]
    group = 4
    high, low = halves(rates)
    for start in range(0, rows, group):
        left, right = [], []
        for r in range(start, start + group):
            at = iota((count, LANES), 0) == major[r : r + 1]
            left.append(
                jnp.concatenate(
                    [
                        jnp.where(at, high[r : r + 1], 0.0),
                        jnp.where(at, low[r : r + 1], 0.0),
                    ],
                    axis=0,
                ).astype(jnp.bfloat16)
            )
            right.append(
                jnp.where(iota((LANES, LANES), 0) == minor[r : r + 1], 1.0, 0.0).astype(jnp.bfloat16)
            )
        part = lax.dot_general(
            jnp.concatenate(left, axis=1),
            jnp.concatenate(right, axis=1),
            (((1,), (1,)), ((), ())),
            preferred_element_type=jnp.float32,
        )
        total = part if total is None else total + part
    return total[:count] + total[count:]


def repeated(row, count):
    tile = jnp.broadcast_to(row, (16, LANES)).astype(jnp.bfloat16)
    return jnp.concatenate([tile] * (count // 16), axis=0)


def spread_cells(rates, major, minor):
    high, low = halves(rates)
    major = major.astype(jnp.float32)
    minor = minor.astype(jnp.float32)
    row = iota((LANES, LANES), 0).astype(jnp.float32).astype(jnp.bfloat16)
    zero = jnp.zeros((), jnp.bfloat16)
    one = jnp.ones((), jnp.bfloat16)
    total = None
    group = 4
    for start in range(0, rates.shape[0], group):
        left, right = [], []
        for r in range(start, start + group):
            at = row == repeated(major[r : r + 1], LANES)
            left.append(
                jnp.concatenate(
                    [jnp.where(at, repeated(part[r : r + 1], LANES), zero) for part in (high, low)], axis=0
                )
            )
            right.append(jnp.where(row == repeated(minor[r : r + 1], LANES), one, zero))
        part = lax.dot_general(
            jnp.concatenate(left, axis=1),
            jnp.concatenate(right, axis=1),
            (((1,), (1,)), ((), ())),
            preferred_element_type=jnp.float32,
        )
        total = part if total is None else total + part
    return total[:LANES] + total[LANES:]


def cell_parts(cell):
    col = cell & (COLS - 1)
    return (col >> 7) * ROWS + (cell >> 9), col & (LANES - 1)


def depth_at_slots(h_ref, index, cell):
    major, minor = cell_parts(cell)
    found = []
    for v in range(3):
        key = major[8 * v : 8 * v + 8]
        lane = minor[8 * v : 8 * v + 8]
        depth = jnp.zeros((8, LANES), jnp.float32)
        for quad in range(QUADS):
            for row in range(ROWS):
                values = h_ref[index + (slice(row, row + 1), slice(quad * LANES, (quad + 1) * LANES))]
                values = jnp.broadcast_to(values, (8, LANES))
                depth = jnp.where(key == quad * ROWS + row, lane_gather(values, lane), depth)
        found.append(depth)
    return jnp.concatenate(found, axis=0)


def level_at_sites(reach_rows, site):
    found = []
    for v in range(3):
        sites = site[8 * v : 8 * v + 8]
        field = sites >> 7
        station = sites & (LANES - 1)
        level = jnp.zeros((8, LANES), jnp.float32)
        for f in range(FIELDS):
            level = jnp.where(field == f, lane_gather(reach_rows(f, v), station), level)
        found.append(level)
    return jnp.concatenate(found, axis=0)


def edge_columns(cells):
    left = column_to_lane(cells[0][:, 0:1], 0)
    right = column_to_lane(cells[0][:, COLS - 1 : COLS], 0)
    for k in (1, 2):
        left = left + column_to_lane(cells[k][:, 0:1], k * ROWS)
        right = right + column_to_lane(cells[k][:, COLS - 1 : COLS], k * ROWS)
    return left, right


def put_edges(beside_ref, across_ref, cells, even, start):
    for k in range(3):
        first = cells[k][0:1]
        last = cells[k][ROWS - 1 : ROWS]
        inner = jnp.where(even, last, first)
        outer = jnp.where(even, first, last)
        for quad in range(QUADS):
            at = start + k * QUADS + quad
            lanes = slice(quad * LANES, (quad + 1) * LANES)
            beside_ref[at : at + 1, :] = inner[:, lanes]
            across_ref[at : at + 1, :] = outer[:, lanes]


def get_edges(got_ref, near_ref, over_ref, cells, spot, start, col_row):
    even, y, is_first, is_last = spot
    before = got_ref[jnp.maximum(y - 1, 0), col_row : col_row + 1, :]
    after = got_ref[jnp.minimum(y + 1, BASINS - 1), col_row : col_row + 1, :]

    def edge(ref, k):
        rows = [ref[start + k * QUADS + q : start + k * QUADS + q + 1, :] for q in range(QUADS)]
        return jnp.concatenate(rows, axis=1)

    top, low, left, right = [], [], [], []
    for k in range(3):
        inner = edge(near_ref, k)
        outer = edge(over_ref, k)
        top.append(jnp.where(is_first, cells[k][0:1], jnp.where(even, outer, inner)))
        low.append(jnp.where(is_last, cells[k][ROWS - 1 : ROWS], jnp.where(even, inner, outer)))
        left.append(jnp.where(y == 0, cells[k][:, 0:1], lane_to_column(before, ROWS, k * ROWS)))
        right.append(
            jnp.where(
                y == BASINS - 1, cells[k][:, COLS - 1 : COLS], lane_to_column(after, ROWS, k * ROWS)
            )
        )
    return top, low, left, right


def inflow_of(own, outlets):
    row = jnp.sum(own[16:24] * outlets, axis=0, keepdims=True)
    return own[8:16, 0:1] + lane_to_column(row, FIELDS, 0)


def river_update(current, inflow, rate, lateral):
    lane = iota((FIELDS, LANES), 1)
    sub = iota((FIELDS, LANES), 0)
    behind = jnp.where(lane == 0, inflow, pltpu.roll(current, 1, 1))
    above = jnp.where(sub == FIELDS - 1, current, pltpu.roll(current, FIELDS - 1, 0))
    below = jnp.where(sub == 0, current, pltpu.roll(current, 1, 0))
    mixing = above - 2.0 * current + below
    return current - rate * (current - behind) + NU * mixing - (DT * RATIO) * lateral


def owned_terms(celerity, base_inflow, upstream, y):
    square = iota((FIELDS, FIELDS), 0) == iota((FIELDS, FIELDS), 1)

    def by_field(ref):
        row = jnp.broadcast_to(own_row(ref[...], y), (FIELDS, FIELDS))
        return jnp.sum(jnp.where(square, row, 0.0), axis=1, keepdims=True)

    feeders = own_row(upstream[...].astype(jnp.float32), y)
    ids = ((lax.axis_index("gx") - 1) * BASINS + iota((BASINS, feeders.shape[1]), 0)).astype(jnp.float32)
    hits = jnp.where(jnp.broadcast_to(feeders, ids.shape) == ids, 1.0, 0.0)
    weight = jnp.sum(hits, axis=1, keepdims=True)
    return jnp.concatenate(
        [jnp.broadcast_to(column, (8, LANES)) for column in (by_field(celerity), by_field(base_inflow), weight)],
        axis=0,
    )


def place():
    gx = lax.axis_index("gx")
    return (gx & 1) == 0, lax.axis_index("gy"), gx == 0, gx == lax.axis_size("gx") - 1


def first_kernel(*refs):
    count = len(refs) - 1
    sources, held, arrived = refs[:6], refs[count - 6 : count], refs[count]
    copies = [
        pltpu.make_async_copy(source, target, arrived.at[i])
        for i, (source, target) in enumerate(zip(sources, held))
    ]
    for copy in copies:
        copy.start()
    first_body(copies, *held, *refs[6 : count - 6])


def first_body(
    copies,
    depth,
    discharge,
    cell_in,
    site_in,
    coeff_in,
    reach,
    beside_ref,
    across_ref,
    mine_ref,
    cell_ref,
    site_ref,
    coeff_ref,
    slots_ref,
):
    even = place()[0]

    def arranged(ref):
        low, own, high = ref[0:8], ref[8:16], ref[16:24]
        return jnp.concatenate([own, jnp.where(even, high, low), jnp.where(even, low, high)], axis=0)

    copies[0].wait()
    copies[2].wait()
    bank = arranged(cell_in)
    cell = jnp.maximum(bank, 0)
    cell_ref[...] = cell
    slots = depth_at_slots(depth, (), cell)
    slots_ref[...] = slots
    for i in (1, 3, 4, 5):
        copies[i].wait()
    site = arranged(site_in)
    coeff = jnp.where(bank >= 0, arranged(coeff_in), 0.0)
    site_ref[...] = site
    coeff_ref[...] = coeff
    for at, value in enumerate((slots, site.astype(jnp.float32), coeff)):
        for v, ref in enumerate((mine_ref, beside_ref, across_ref)):
            ref[8 * at : 8 * at + 8] = value[8 * v : 8 * v + 8]
    cells = [depth[...], discharge[0], discharge[1]]
    mine_ref[24:32] = jnp.zeros((8, LANES), jnp.float32)
    left, right = edge_columns(cells)
    mine_ref[24:25] = left
    mine_ref[25:26] = right
    for ref in (beside_ref, across_ref):
        ref[FIRST_EDGE:FIRST_LEVELS] = jnp.zeros((FIRST_LEVELS - FIRST_EDGE, LANES), jnp.float32)
        for f in range(FIELDS):
            at = FIRST_LEVELS + 8 * f
            ref[at : at + 8] = reach[:, f * LANES : (f + 1) * LANES]
    put_edges(beside_ref, across_ref, cells, even, FIRST_EDGE)


def column_for(mine, b, start):
    y = lax.axis_index("gy")
    left = mine[start : start + 1]
    right = mine[start + 1 : start + 2]
    return jnp.where(b == y - 1, left, jnp.where(b == y + 1, right, 0.0))


def first_pack(mine, near, over, send):
    refs = (mine, near, over)
    for b in range(BASINS):
        for v, ref in enumerate(refs):
            send[b, v : v + 1] = ref[b : b + 1]
            send[b, 3 + v : 4 + v] = ref[16 + b : 17 + b]
            send[b, 8 + 8 * v : 16 + 8 * v] = ref[8:16]
        send[b, 6:7] = column_for(mine, b, 24)
        send[b, 7:8] = jnp.zeros((1, LANES), jnp.float32)


def pack(mine, near, over, send):
    even = place()[0]
    outlet = jnp.where(even, over[OUTLET : OUTLET + 1], near[OUTLET : OUTLET + 1])
    refs = (mine, near, over)
    for b in range(BASINS):
        for v, ref in enumerate(refs):
            send[b, v : v + 1] = ref[b : b + 1]
            send[b, 3 + v : 4 + v] = ref[8 + b : 9 + b]
        send[b, 6:7] = column_for(mine, b, 16)
        send[b, 7:8] = outlet


def last_pack(mine, near, over, send):
    even = place()[0]
    outlet = jnp.where(even, over[OUTLET : OUTLET + 1], near[OUTLET : OUTLET + 1])
    refs = (mine, near, over)
    for b in range(BASINS):
        for v, ref in enumerate(refs):
            send[b, 3 + v : 4 + v] = ref[8 + b : 9 + b]
            send[b, 8 + 8 * v : 16 + 8 * v] = ref[0:8]
            send[b, v : v + 1] = jnp.zeros((1, LANES), jnp.float32)
        send[b, 6:7] = column_for(mine, b, 16)
        send[b, 7:8] = outlet
        send[b, 32:40] = mine[24:32]


def gathered(got, row):
    return jnp.concatenate([got[:, row + v, :] for v in range(3)], axis=0)


def advance_levels(current, outlets, own, site_owner, coeff_owner, segment_owner, slots_owner):
    rates = coeff_owner * (segment_owner - slots_owner)
    lateral = spread(rates, site_owner >> 7, site_owner & (LANES - 1), FIELDS)
    return river_update(current, inflow_of(own, outlets), own[0:8], lateral)


def advance_cells(base, edges, cell, coeff, segment, slots):
    major, minor = cell_parts(cell)
    rates = coeff * (segment - slots)
    blocks = spread_cells(rates, major, minor)
    source = jnp.concatenate([blocks[q * ROWS : (q + 1) * ROWS] for q in range(QUADS)], axis=1)
    return flood_finish([base[0], base[1], base[2]], edges, source)


def first_flow(depth, discharge, rough, celerity, base_inflow, upstream, base, terms):
    new = flood_base([depth[...], discharge[0], discharge[1]], rough[...])
    for k in range(3):
        base[k] = new[k]
    for b in range(BASINS):
        terms[b] = owned_terms(celerity, base_inflow, upstream, b)


def flow(state, rough, base):
    new = flood_base([state[0], state[1], state[2]], rough[...])
    for k in range(3):
        base[k] = new[k]


def flow_and_total(state, rough, owner_coeff, owner_site, base, total):
    flow(state, rough, base)
    site = owner_site[...]
    total[...] = spread(owner_coeff[...], site >> 7, site & (LANES - 1), FIELDS)


def flow_and_sites(state, rough, got_first, base, sites):
    flow(state, rough, base)
    for b in range(BASINS):
        site = jnp.concatenate([got_first[:, 8 + 8 * v + b, :] for v in range(3)], axis=0)
        sites[b] = site.astype(jnp.int32)


def last_kernel(
    state, got, near, over, base, cell_ref, coeff_ref, slots_ref, sites, terms, state_out, reach_out
):
    cells = [state[0], state[1], state[2]]
    edges = get_edges(got, near, over, cells, place(), EDGE, 6)
    new = advance_cells(
        base, edges, cell_ref[...], coeff_ref[...], gathered(got, 3), slots_ref[...]
    )
    for k in range(3):
        state_out[k] = new[k]
    outlets = got[:, 7, :]
    lane = iota((FIELDS, LANES), 1)
    for b in range(BASINS):
        own = terms[b]
        site = sites[b]
        held = jnp.concatenate([got[:, 8 + 8 * v + b, :] for v in range(3)], axis=0)
        drawn = spread(held, site >> 7, site & (LANES - 1), FIELDS)
        entering = jnp.where(lane == 0, own[0:8] * inflow_of(own, outlets), 0.0)
        level = got[b, 32:40, :] + entering + (DT * RATIO) * drawn
        for f in range(FIELDS):
            reach_out[b : b + 1, f * LANES : (f + 1) * LANES] = level[f : f + 1]


def step_kernel(first, tail, *refs):
    refs = list(refs)

    def take(n):
        taken = refs[:n]
        del refs[:n]
        return taken

    if first:
        depth, discharge, reach, site_ref, terms = take(5)
    else:
        state, levels, owner_levels, owner_site, owner_coeff, own_ref = take(6)
    got, near, over, base, cell_ref, coeff_ref, slots_ref = take(7)
    if tail:
        (total,) = take(1)
    state_out, slots_out, beside_ref, across_ref, mine_ref = take(5)
    if not tail:
        levels_out, owner_levels_out = take(2)
    if first:
        owner_site_out, owner_coeff_out, own_out = take(3)
    spot = place()
    even, y = spot[0], spot[1]
    cell = cell_ref[...]

    slots_owner = gathered(got, 0)
    if first:
        cells = [depth[...], discharge[0], discharge[1]]
        current = jnp.concatenate(
            [own_row(reach[:, f * LANES : (f + 1) * LANES], y) for f in range(FIELDS)], axis=0
        )

        def tile_rows(f, v):
            if v == 0:
                return reach[:, f * LANES : (f + 1) * LANES]
            return (near if v == 1 else over)[FIRST_LEVELS + 8 * f : FIRST_LEVELS + 8 * f + 8, :]

        segment = level_at_sites(tile_rows, site_ref[...])
        site_owner = jnp.concatenate([got[:, 8 + 8 * v + y, :] for v in range(3)], axis=0)
        site_owner = site_owner.astype(jnp.int32)
        coeff_owner = gathered(got, 3)
        outlets = jnp.zeros((BASINS, LANES), jnp.float32)
        for f in range(FIELDS):
            source_rows = jnp.where(even, tile_rows(f, 2), tile_rows(f, 1))
            outlets = jnp.where(
                iota((BASINS, LANES), 1) == f, source_rows[:, LANES - 1 : LANES], outlets
            )
        segment_owner = level_at_sites(
            lambda f, v: jnp.broadcast_to(current[f : f + 1], (8, LANES)), site_owner
        )
        own = terms[y]
        owner_site_out[...] = site_owner
        owner_coeff_out[...] = coeff_owner
        own_out[...] = own
    else:
        cells = [state[0], state[1], state[2]]
        current = levels[...]
        segment = gathered(got, 3)
        site_owner = owner_site[...]
        coeff_owner = owner_coeff[...]
        segment_owner = owner_levels[...]
        outlets = got[:, 7, :]
        own = own_ref[...]

    levels_next = advance_levels(
        current, outlets, own, site_owner, coeff_owner, segment_owner, slots_owner
    )
    edges = get_edges(got, near, over, cells, spot, FIRST_EDGE if first else EDGE, 6)
    new = advance_cells(base, edges, cell, coeff_ref[...], segment, slots_ref[...])
    for k in range(3):
        state_out[k] = new[k]
    owned = level_at_sites(
        lambda f, v: jnp.broadcast_to(levels_next[f : f + 1], (8, LANES)), site_owner
    )
    if not tail:
        levels_out[...] = levels_next
        owner_levels_out[...] = owned
    slots = depth_at_slots(state_out, (0,), cell)
    slots_out[...] = slots
    if tail:
        slots = slots * coeff_ref[...]
    blank = jnp.zeros((8, LANES), jnp.float32)
    outlet_row = column_to_lane(levels_next[:, LANES - 1 : LANES], 0)
    for v, ref in enumerate((mine_ref, beside_ref, across_ref)):
        ref[0:8] = slots[8 * v : 8 * v + 8]
        ref[8:16] = owned[8 * v : 8 * v + 8]
        ref[16:24] = blank
        if v > 0:
            ref[OUTLET : OUTLET + 1] = outlet_row
            ref[EDGE : EDGE + 8] = blank
            ref[EDGE + 8 : EDGE + 16] = blank
    left, right = edge_columns(new)
    mine_ref[16:17] = left
    mine_ref[17:18] = right
    put_edges(beside_ref, across_ref, new, even, EDGE)
    if tail:
        none = jnp.zeros((FIELDS, 1), jnp.float32)
        mine_ref[24:32] = river_update(levels_next, none, own[0:8], total[...] * levels_next)
    else:
        mine_ref[24:32] = blank


def call(kernel, outs, args, limit=16 << 20):
    return pl.pallas_call(
        kernel,
        out_shape=outs,
        in_specs=[pl.BlockSpec(memory_space=pltpu.VMEM) for _ in args],
        out_specs=[pl.BlockSpec(memory_space=pltpu.VMEM) for _ in outs],
        compiler_params=None if INTERPRET else pltpu.CompilerParams(vmem_limit_bytes=limit),
        interpret=INTERPRET,
    )(*args)


def f32(*shape):
    return jax.ShapeDtypeStruct(shape, jnp.float32)


def i32(*shape):
    return jax.ShapeDtypeStruct(shape, jnp.int32)


def per_device(
    depth,
    discharge,
    roughness,
    reach_state,
    celerity,
    base_inflow,
    upstream,
    bank_cell,
    bank_site,
    bank_coeff,
):
    count_x = lax.axis_size("gx")
    chip = [(i, i ^ 1) for i in range(count_x)]
    border = [(i, i + 1) for i in range(1, count_x - 1, 2)]
    border = border + [(b, a) for a, b in border]

    def exchange(kernel, rows, beside, across, mine, ready):
        across, beside = lax.optimization_barrier((across, beside))
        near = lax.ppermute(beside, "gx", chip)
        over = lax.ppermute(across, "gx", border)
        over, near = lax.optimization_barrier((over, near))
        send = call(kernel, [f32(BASINS, rows, LANES)], [mine, near, over])[0]
        send, ready = lax.optimization_barrier((send, ready))
        return lax.all_to_all(send, "gy", 0, 0), near, over, ready

    table = (SLOT_ROWS, LANES)
    outs = [
        f32(FIRST_SWAP, LANES),
        f32(FIRST_SWAP, LANES),
        f32(32, LANES),
        i32(*table),
        i32(*table),
        f32(*table),
        f32(*table),
    ]
    inputs = [depth, discharge, bank_cell, bank_site, bank_coeff, reach_state]
    inputs = [pltpu.with_memory_space_constraint(x, pltpu.HBM) for x in inputs]
    beside, across, mine, cell, site, coeff, slots = pl.pallas_call(
        first_kernel,
        out_shape=outs,
        in_specs=[pl.BlockSpec(memory_space=pltpu.HBM) for _ in inputs],
        out_specs=[pl.BlockSpec(memory_space=pltpu.VMEM) for _ in outs],
        scratch_shapes=[pltpu.VMEM(x.shape, x.dtype) for x in inputs]
        + [pltpu.SemaphoreType.DMA((len(inputs),))],
        compiler_params=None if INTERPRET else pltpu.CompilerParams(vmem_limit_bytes=16 << 20),
        interpret=pltpu.InterpretParams() if INTERPRET else False,
    )(*inputs)
    base, terms = call(
        first_flow,
        [f32(3, ROWS, COLS), f32(BASINS, 24, LANES)],
        [depth, discharge, roughness, celerity, base_inflow, upstream],
    )
    got, near, over, (base, terms) = exchange(first_pack, 32, beside, across, mine, (base, terms))
    got_first = got
    for step in range(STEPS - 1):
        first, tail = step == 0, step == STEPS - 2
        outs = [
            f32(3, ROWS, COLS),
            f32(*table),
            f32(SWAP, LANES),
            f32(SWAP, LANES),
            f32(32, LANES),
        ]
        if not tail:
            outs += [f32(FIELDS, LANES), f32(*table)]
        if first:
            outs += [i32(*table), f32(*table), f32(*table)]
            args = [depth, discharge, reach_state, site, terms]
        else:
            args = [state, levels, owner_levels, owner_site, owner_coeff, own]
        args += [got, near, over, base, cell, coeff, slots]
        if tail:
            args += [total]
        result = call(functools.partial(step_kernel, first, tail), outs, args)
        state, slots, beside, across, mine = result[:5]
        if not tail:
            levels, owner_levels = result[5:7]
        if first:
            owner_site, owner_coeff, own = result[7:10]
        if first:
            base, total = call(
                flow_and_total,
                [f32(3, ROWS, COLS), f32(FIELDS, LANES)],
                [state, roughness, owner_coeff, owner_site],
            )
        elif tail:
            base, sites = call(
                flow_and_sites,
                [f32(3, ROWS, COLS), i32(BASINS, SLOT_ROWS, LANES)],
                [state, roughness, got_first],
            )
        else:
            base = call(flow, [f32(3, ROWS, COLS)], [state, roughness])[0]
        ready = (base, sites) if tail else (base,)
        got, near, over, ready = exchange(
            last_pack if tail else pack, 40 if tail else BASINS, beside, across, mine, ready
        )
        base = ready[0]
        if tail:
            sites = ready[1]
    state, reach = call(
        last_kernel,
        [f32(3, ROWS, COLS), f32(BASINS, FIELDS * LANES)],
        [state, got, near, over, base, cell, coeff, slots, sites, terms],
    )
    return state, reach


def solution(mesh):
    return jax.shard_map(
        per_device,
        mesh=mesh,
        in_specs=(
            P("gx", "gy"),
            P(None, "gx", "gy"),
            P("gx", "gy"),
            P("gx", None),
            P("gx", None),
            P("gx", None),
            P("gx", None),
            P("gx", "gy"),
            P("gx", "gy"),
            P("gx", "gy"),
        ),
        out_specs=(P(None, "gx", "gy"), P("gx", None)),
        check_vma=False,
    )
```
